32 devices in a mesh: expert: 8 (over z, y), shard: 4 (over x, core).
Axes of the slice: x: 2, y: 2, z: 4, core: 2. Of those that a mesh axis runs over, the one named last changes fastest.
Arguments:
- tokens: bfloat16 [4096, 2048], P(('expert', 'shard')), may hold values from -6 to 6
- cotangent: bfloat16 [4096, 2048], P(('expert', 'shard')), may hold values from -6 to 6
- norm1_gain: bfloat16 [2048], P(('expert', 'shard')), may hold values from 0.5 to 1.5
- q_weight: bfloat16 [2048, 3072], P(('expert', 'shard')), may hold values from -0.125 to 0.125
- kva_weight: bfloat16 [2048, 576], P(('expert', 'shard')), may hold values from -0.125 to 0.125
- kv_gain: bfloat16 [512], P(('expert', 'shard')), may hold values from 0.5 to 1.5
- kvb_weight: bfloat16 [512, 4096], P(('expert', 'shard')), may hold values from -0.25 to 0.25
- o_weight: bfloat16 [2048, 2048], P(('expert', 'shard')), may hold values from -0.75 to 0.75
- norm2_gain: bfloat16 [2048], P(('expert', 'shard')), may hold values from 0.5 to 1.5
- router_weight: bfloat16 [2048, 16], P(('expert', 'shard')), may hold values from -0.0625 to 0.0625
- shared_gate: bfloat16 [2048, 2816], P(('expert', 'shard')), may hold values from -0.125 to 0.125
- shared_up: bfloat16 [2048, 2816], P(('expert', 'shard')), may hold values from -0.125 to 0.125
- shared_down: bfloat16 [2816, 2048], P(('expert', 'shard')), may hold values from -0.15625 to 0.15625
- expert_gate: bfloat16 [16, 2048, 1408], P('expert', None, 'shard'), may hold values from -0.125 to 0.125
- expert_up: bfloat16 [16, 2048, 1408], P('expert', None, 'shard'), may hold values from -0.125 to 0.125
- expert_down: bfloat16 [16, 1408, 2048], P('expert', 'shard'), may hold values from -0.4375 to 0.4375
- expert_ids: int32 [4096, 6], P(('expert', 'shard')), may hold values from 0 to 15, all different within a row
- token_rank: int32 [4096], P(('expert', 'shard')), may hold values from 0 to 127, as said below
- seq_ids: int32 [4096], P('expert'), may hold values from 0 to 2, as said below
Outputs:
- output: bfloat16 [4096, 2048], P(('expert', 'shard'))
- tokens_grad: float32 [4096, 2048], P(('expert', 'shard'))
- norm1_gain_grad: float32 [2048], P(('expert', 'shard'))
- q_weight_grad: float32 [2048, 3072], P(('expert', 'shard'))
- kva_weight_grad: float32 [2048, 576], P(('expert', 'shard'))
- kv_gain_grad: float32 [512], P(('expert', 'shard'))
- kvb_weight_grad: float32 [512, 4096], P(('expert', 'shard'))
- o_weight_grad: float32 [2048, 2048], P(('expert', 'shard'))
- norm2_gain_grad: float32 [2048], P(('expert', 'shard'))
- router_weight_grad: float32 [2048, 16], P(('expert', 'shard'))
- shared_gate_grad: float32 [2048, 2816], P(('expert', 'shard'))
- shared_up_grad: float32 [2048, 2816], P(('expert', 'shard'))
- shared_down_grad: float32 [2816, 2048], P(('expert', 'shard'))
- expert_gate_grad: float32 [16, 2048, 1408], P('expert', None, 'shard')
- expert_up_grad: float32 [16, 2048, 1408], P('expert', None, 'shard')
- expert_down_grad: float32 [16, 1408, 2048], P('expert', 'shard')
The draws below stay inside these ranges and needn't reach their ends.
Inputs may be any that keep to these rules, and one draw needn't show every extreme that they name: `token_rank`: within each aligned block of 128 tokens (the rows of one device) every value of 0 to 127 appears once. `seq_ids`: in each group of 512 tokens the ids never fall; the first 256 are 0 and the others belong to continuations 1 to 2, each of one token or more.
All inputs are finite; a program needn't handle non-finite values.
Results may differ from the reference program's by a relative error of at most 0.02.
Values may be sent and summed in bfloat16 or wider, within the bound.
A program may use at most 448 MiB of HBM per device.

```python
import jax
import jax.numpy as jnp
from jax import lax

D = 2048
HEADS = 16
NOPE = 128
ROPE = 64
VDIM = 128
KV_RANK = 512
FFE = 1408
SHARED_FF = 2816
TOP = 6
CONT = 128
CONTS = 2
PROMPT = 256
EXPERTS = 16
GLEN = 512
TOK_DEV = 128
TOKENS = 4096
CAP = 48
N_SHARD = 4


def draw_token_rank(key, part):
    key = jax.random.fold_in(key, 11)
    block_count = TOKENS // TOK_DEV
    block_keys = jax.random.split(key, block_count)
    rank_rows = jax.vmap(lambda single_key: jax.random.permutation(single_key, TOK_DEV))(block_keys)
    return rank_rows.reshape(TOKENS).astype(jnp.int32)


def draw_seq_ids(key, part):
    key = jax.random.fold_in(key, 23)
    group_count = TOKENS // GLEN
    cont_tokens = CONTS * CONT
    cut_points = jnp.sort(jax.random.randint(key, (group_count, CONTS - 1), 1, cont_tokens), axis=1)
    places = jnp.arange(cont_tokens, dtype=jnp.int32)
    labels = 1 + jnp.sum((places[None, :, None] >= cut_points[:, None, :]).astype(jnp.int32), axis=2)
    prompt_ids = jnp.zeros((group_count, PROMPT), jnp.int32)
    return jnp.concatenate([prompt_ids, labels.astype(jnp.int32)], axis=1).reshape(TOKENS).astype(jnp.int32)


def spiked(result, own_key, source, target, parts, factor):
    def block_of(axis_at):
        return (jnp.arange(result.shape[axis_at]) // (result.shape[axis_at] // parts)).reshape((-1,) + (1,) * (result.ndim - 1 - axis_at))

    first = jax.random.permutation(own_key, parts)[block_of(target)]
    far = (block_of(target) + parts // 2) % parts
    return jnp.where((block_of(source) == first) | (block_of(source) == far), factor * result, result)


def block_scale(own_key, extent, shards, smallest, largest):
    factor_of, own = 1.0, jax.random.fold_in(own_key, 6)
    for dim, shards_of in shards:
        steps = jnp.exp(jax.random.uniform(jax.random.fold_in(own, dim), (shards_of,), jnp.float32, smallest / len(shards), largest / len(shards)))
        factor_of = factor_of * jnp.repeat(steps, extent[dim] // shards_of).reshape([-1 if axis == dim else 1 for axis in range(len(extent))])
    return factor_of


def different_ones(own_key, rows, number_of, top, lift):
    order = jax.random.permutation(jax.random.fold_in(own_key, 1), number_of)
    pull = order
    for power in range(3):
        pull = pull * pull // number_of
    pull = pull * lift // number_of
    chance = jax.random.randint(jax.random.fold_in(own_key, 2), (rows, number_of), 0, 4096) + pull
    holders = jax.random.permutation(jax.random.fold_in(own_key, 3), rows)[jnp.arange(number_of) % rows]
    chance = jnp.where(jnp.arange(rows)[:, None] == holders[None, :], 1 << 14, chance)
    priority = chance * number_of + jnp.arange(number_of)
    return lax.top_k(priority.astype(jnp.int32), top)[1].astype(jnp.int32)


def bell_draw(rng, dims, deviation, limit, cuts=(), kind=jnp.bfloat16):
    result = deviation * jax.random.normal(rng, dims, jnp.float32)
    if cuts:
        result = result * block_scale(rng, dims, cuts, -0.22, 0.18)
    return jnp.clip(result, -limit, limit).astype(kind)


def gaussian_with(stream_key, shape, scale, reach, cuts, heavy, kind=jnp.bfloat16):
    array = scale * jax.random.normal(stream_key, shape, jnp.float32)
    if cuts:
        array = array * block_scale(stream_key, shape, cuts, -0.22, 0.18)
    return jnp.clip(spiked(array, jax.random.fold_in(stream_key, 3), *heavy), -reach, reach).astype(kind)


def setup_inputs(seed: int = 0) -> dict:
    splits = jax.random.split(jax.random.key(seed), 20)
    return {
        "tokens": gaussian_with(splits[0], (TOKENS, D), 1.0, 6.0, ((0, 32),), (0, 1, 32, 2.75)),
        "cotangent": bell_draw(splits[1], (TOKENS, D), 1.0, 6.0, ((0, 32),)),
        "norm1_gain": jnp.clip(1.0 + 0.1 * jax.random.normal(splits[2], (D,), jnp.float32), 0.5, 1.5).astype(jnp.bfloat16),
        "q_weight": bell_draw(splits[3], (D, HEADS * (NOPE + ROPE)), D ** -0.5, 0.125, ((0, 32),)),
        "kva_weight": bell_draw(splits[4], (D, KV_RANK + ROPE), D ** -0.5, 0.125, ((0, 32),)),
        "kv_gain": jnp.clip(1.0 + 0.1 * jax.random.normal(splits[5], (KV_RANK,), jnp.float32), 0.5, 1.5).astype(jnp.bfloat16),
        "kvb_weight": bell_draw(splits[6], (KV_RANK, HEADS * (NOPE + VDIM)), KV_RANK ** -0.5, 0.25, ((0, 32),)),
        "o_weight": bell_draw(splits[7], (HEADS * VDIM, D), (HEADS * VDIM // 32) ** -0.5, 0.75, ((0, 32),)),
        "norm2_gain": jnp.clip(1.0 + 0.1 * jax.random.normal(splits[8], (D,), jnp.float32), 0.5, 1.5).astype(jnp.bfloat16),
        "router_weight": bell_draw(splits[9], (D, EXPERTS), (4 * D) ** -0.5, 0.0625, ((0, 32),)),
        "shared_gate": bell_draw(splits[10], (D, SHARED_FF), D ** -0.5, 0.125, ((0, 32),)),
        "shared_up": bell_draw(splits[11], (D, SHARED_FF), D ** -0.5, 0.125, ((0, 32),)),
        "shared_down": bell_draw(splits[12], (SHARED_FF, D), (SHARED_FF // 2) ** -0.5, 0.15625, ((0, 32),)),
        "expert_gate": bell_draw(splits[13], (EXPERTS, D, FFE), D ** -0.5, 0.125, ((0, 8), (2, 4))),
        "expert_up": bell_draw(splits[14], (EXPERTS, D, FFE), D ** -0.5, 0.125, ((0, 8), (2, 4))),
        "expert_down": bell_draw(splits[15], (EXPERTS, FFE, D), (FFE // 8) ** -0.5, 0.4375, ((0, 8), (1, 4))),
        "expert_ids": different_ones(splits[16], TOKENS, EXPERTS, TOP, 3072),
        "token_rank": draw_token_rank(jax.random.fold_in(splits[19], 71), 0),
        "seq_ids": draw_seq_ids(jax.random.fold_in(splits[19], 71), 0),
    }


EPSILON = 1e-06
THETA = 10000.0
NEGATIVE = -1e+30
HIGHEST = lax.Precision.HIGHEST

@jax.custom_vjp
def low(v):
    return lax.optimization_barrier(v.astype(jnp.bfloat16)).astype(jnp.float32)

@jax.custom_vjp
def low_back(v):
    return v

def low_keep(v):
    return (low(v), None)

def low_pass(kept, grad):
    return (grad,)

def back_keep(v):
    return (v, None)

def back_low(kept, grad):
    return (low(grad),)
low.defvjp(low_keep, low_pass)
low_back.defvjp(back_keep, back_low)

def rms_norm(values, gain_row):
    return values * lax.rsqrt(lax.optimization_barrier(jnp.mean(values * values, axis=-1, keepdims=True)) + EPSILON) * gain_row

def rope_tables(positions, width):
    half_width = width // 2
    frequency = THETA ** (-2.0 * jnp.arange(half_width, dtype=jnp.float32) / width)
    angles = positions.astype(jnp.float32)[:, None] * frequency[None, :]
    return (jnp.cos(angles), jnp.sin(angles))

def rotate(values, cosine_table, sine_table):
    half_width = values.shape[-1] // 2
    first_half = values[..., :half_width]
    second = values[..., half_width:]
    return jnp.concatenate([first_half * cosine_table - second * sine_table, second * cosine_table + first_half * sine_table], axis=-1)

def positions_of(group_ids):
    length = group_ids.shape[0]
    token_index = jnp.arange(length, dtype=jnp.int32)
    labels = jnp.arange(CONTS + 1, dtype=jnp.int32)
    member = (group_ids[:, None] == labels[None, :]).astype(jnp.int32)
    counts = lax.optimization_barrier(jnp.sum(member, axis=0))
    starts = jnp.cumsum(counts) - counts
    start_of = lax.optimization_barrier(jnp.sum(member * starts[None, :], axis=1))
    return token_index - start_of + jnp.where(group_ids > 0, counts[0], 0)

def route_slots(choice_ids, rank_row, expert_total, capacity):
    row_count, top_count = choice_ids.shape
    pair_count = row_count * top_count
    order_key = (jnp.arange(top_count, dtype=jnp.int32)[None, :] * row_count + rank_row[:, None]).reshape(pair_count)
    flat_ids = choice_ids.reshape(pair_count)
    pair_range = jnp.arange(pair_count, dtype=jnp.int32)
    in_order = jnp.zeros((pair_count,), jnp.int32).at[order_key].set(pair_range)
    sorted_ids = flat_ids[in_order]
    member = (sorted_ids[:, None] == jnp.arange(expert_total, dtype=jnp.int32)[None, :]).astype(jnp.int32)
    earlier = jnp.cumsum(member, axis=0) - member
    place_sorted = lax.optimization_barrier(jnp.sum(earlier * member, axis=1))
    pair_place = place_sorted[order_key]
    pair_dest = jnp.where(pair_place < capacity, flat_ids * capacity + pair_place, expert_total * capacity)
    slot_pair = jnp.full((expert_total * capacity + 1,), pair_count, jnp.int32).at[pair_dest].set(pair_range)
    return (pair_dest.reshape(row_count, top_count), slot_pair[:expert_total * capacity])

def attention_group(group_rows, group_ids, first_norm_scale, query_weight, compress_weight, latent_norm_scale, expand_weight, output_weight):
    length = group_rows.shape[0]
    cosine_table, sine_table = rope_tables(positions_of(group_ids), ROPE)
    hidden_one = low(rms_norm(group_rows, first_norm_scale))
    query_raw = low_back(jnp.dot(hidden_one, query_weight, precision=HIGHEST)).reshape(length, HEADS, NOPE + ROPE)
    q_nope = low(query_raw[:, :, :NOPE])
    q_rope = low(rotate(query_raw[:, :, NOPE:], cosine_table[:, None, :], sine_table[:, None, :]))
    compressed = low_back(jnp.dot(hidden_one, compress_weight, precision=HIGHEST))
    latent = low(rms_norm(compressed[:, :KV_RANK], latent_norm_scale))
    k_rope = low(rotate(compressed[:, KV_RANK:], cosine_table, sine_table))
    keyval = low_back(low(jnp.dot(latent, expand_weight, precision=HIGHEST))).reshape(length, HEADS, NOPE + VDIM)
    k_nope = keyval[:, :, :NOPE]
    values = keyval[:, :, NOPE:]
    raw_scores = jnp.einsum('qhd,khd->hqk', q_nope, k_nope, precision=HIGHEST) + jnp.einsum('qhd,kd->hqk', q_rope, k_rope, precision=HIGHEST)
    scores = low_back(raw_scores * (NOPE + ROPE) ** (-0.5))
    token_index = jnp.arange(length, dtype=jnp.int32)
    allowed = (token_index[None, :] <= token_index[:, None]) & ((group_ids[None, :] == 0) | (group_ids[None, :] == group_ids[:, None]))
    scores = jnp.where(allowed[None], scores, NEGATIVE)
    top_score = lax.optimization_barrier(jnp.max(scores, axis=-1, keepdims=True))
    log_total = top_score + jnp.log(lax.optimization_barrier(jnp.sum(jnp.exp(scores - top_score), axis=-1, keepdims=True)))
    prob_low = low(jnp.exp(scores - log_total))
    attended = low_back(low(jnp.einsum('hqk,khd->qhd', prob_low, values, precision=HIGHEST))).reshape(length, HEADS * VDIM)
    return group_rows + low_back(jnp.dot(attended, output_weight, precision=HIGHEST))

def shared_block(row_vals, shared_gate_weight, shared_up_weight, shared_down_weight):
    gate_val = low_back(jnp.dot(row_vals, shared_gate_weight, precision=HIGHEST))
    up_val = low_back(jnp.dot(row_vals, shared_up_weight, precision=HIGHEST))
    return jnp.dot(low(jax.nn.silu(gate_val) * up_val), shared_down_weight, precision=HIGHEST)

def expert_layer_block(padded_tokens, expert_entry):
    row_index, w_gate, w_up, w_down = expert_entry
    row_vals = low_back(jnp.take(padded_tokens, row_index, axis=0))
    quarter_width = FFE // N_SHARD
    running = jnp.zeros((row_index.shape[0], D), jnp.float32)
    for quarter in range(N_SHARD):
        col_start = quarter * quarter_width
        copy_rows = low_back(row_vals)
        gate_val = low_back(jnp.dot(copy_rows, w_gate[:, col_start:col_start + quarter_width], precision=HIGHEST))
        up_val = low_back(jnp.dot(copy_rows, w_up[:, col_start:col_start + quarter_width], precision=HIGHEST))
        hidden_val = low(jax.nn.silu(gate_val) * up_val)
        running = running + low(jnp.dot(hidden_val, w_down[col_start:col_start + quarter_width, :], precision=HIGHEST))
    return low_back(low(running))

def reference(tokens, cotangent, norm1_gain, q_weight, kva_weight, kv_gain, kvb_weight, o_weight, norm2_gain, router_weight, shared_gate, shared_up, shared_down, expert_gate, expert_up, expert_down, expert_ids, token_rank, seq_ids):
    block_count = TOKENS // TOK_DEV
    group_count = TOKENS // GLEN
    route = jax.vmap(lambda ids_row, rank_row: route_slots(ids_row, rank_row, EXPERTS, CAP))
    pair_dest, slot_pair = route(expert_ids.reshape(block_count, TOK_DEV, TOP), token_rank.reshape(block_count, TOK_DEV))
    block_base = jnp.arange(block_count, dtype=jnp.int32)[:, None]
    slot_token = slot_pair // TOP
    global_token = jnp.where(slot_token < TOK_DEV, slot_token + block_base * TOK_DEV, TOKENS).astype(jnp.int32)
    expert_token_rows = global_token.reshape(block_count, EXPERTS, CAP).transpose(1, 0, 2).reshape(EXPERTS, block_count * CAP)
    dest_flat = pair_dest.reshape(block_count, TOK_DEV * TOP)
    pair_index = jnp.where(dest_flat < EXPERTS * CAP, dest_flat // CAP * (block_count * CAP) + block_base * CAP + dest_flat % CAP, EXPERTS * block_count * CAP).astype(jnp.int32).reshape(TOKENS * TOP)

    def forward_pass(input_rows, first_norm_scale, query_weight, compress_weight, latent_norm_scale, expand_weight, output_weight, second_norm_scale, router_matrix, shared_gate_weight, shared_up_weight, shared_down_weight, expert_gate_weight, expert_up_weight, expert_down_weight):
        attend = jax.checkpoint(lambda group_item: attention_group(group_item[0], group_item[1], first_norm_scale, query_weight, compress_weight, latent_norm_scale, expand_weight, output_weight))
        mixed = lax.map(attend, (input_rows.reshape(group_count, GLEN, D), seq_ids.reshape(group_count, GLEN))).reshape(TOKENS, D)
        hidden_two = low(rms_norm(mixed, second_norm_scale))
        logits = low_back(jnp.dot(hidden_two, router_matrix, precision=HIGHEST))
        gate_probs = jax.nn.softmax(jnp.take_along_axis(logits, expert_ids, axis=1), axis=-1)
        shared = lax.map(jax.checkpoint(lambda row_vals: shared_block(row_vals, shared_gate_weight, shared_up_weight, shared_down_weight)), hidden_two.reshape(group_count, GLEN, D)).reshape(TOKENS, D)
        padded_tokens = jnp.concatenate([hidden_two, jnp.zeros((1, D), jnp.float32)], axis=0)
        expert_output = lax.map(jax.checkpoint(lambda expert_entry: expert_layer_block(padded_tokens, expert_entry)), (expert_token_rows, expert_gate_weight, expert_up_weight, expert_down_weight))
        flat_out = jnp.concatenate([expert_output.reshape(EXPERTS * block_count * CAP, D), jnp.zeros((1, D), jnp.float32)], axis=0)
        pair_out = jnp.take(flat_out, pair_index, axis=0).reshape(TOKENS, TOP, D)
        routed = lax.optimization_barrier(jnp.sum(gate_probs[:, :, None] * pair_out, axis=1))
        return mixed + routed + shared
    floats = [weight_arg.astype(jnp.float32) for weight_arg in (tokens, norm1_gain, q_weight, kva_weight, kv_gain, kvb_weight, o_weight, norm2_gain, router_weight, shared_gate, shared_up, shared_down, expert_gate, expert_up, expert_down)]
    output, pullback = jax.vjp(forward_pass, *floats)
    grads = pullback(cotangent.astype(jnp.float32))
    return (output.astype(jnp.bfloat16), grads[0], grads[1], grads[2], grads[3], grads[4], grads[5], grads[6], grads[7], grads[8], grads[9], grads[10], grads[11], grads[12], grads[13], grads[14])
```

```python
import jax
import jax.numpy as jnp
from jax import lax
from jax.sharding import PartitionSpec as P

HEADS = 16
NOPE = 128
ROPE = 64
VDIM = 128
KV_RANK = 512
CONTS = 2


EPSILON = 1e-06
THETA = 10000.0
NEGATIVE = -1e30
BOTH = ("expert", "shard")
BF = jnp.bfloat16
F32 = jnp.float32


def rms_forward(values, gain_row):
    inverse = lax.rsqrt(jnp.mean(values * values, axis=-1, keepdims=True) + EPSILON)
    return (values * inverse * gain_row, inverse)


def rms_backward(values, inverse, gain_row, upstream):
    normed = values * inverse
    scaled = upstream * gain_row
    value_grad = inverse * (scaled - normed * jnp.mean(scaled * normed, axis=-1, keepdims=True))
    return (value_grad, jnp.sum(upstream * normed, axis=0))


def rope_tables(positions, width):
    half_width = width // 2
    frequency = THETA ** (-2.0 * jnp.arange(half_width, dtype=jnp.float32) / width)
    angles = positions.astype(jnp.float32)[:, None] * frequency[None, :]
    return (jnp.cos(angles), jnp.sin(angles))


def rotate(values, cosine_table, sine_table):
    half_width = values.shape[-1] // 2
    first_half = values[..., :half_width]
    second = values[..., half_width:]
    return jnp.concatenate(
        [
            first_half * cosine_table - second * sine_table,
            second * cosine_table + first_half * sine_table,
        ],
        axis=-1,
    )


def positions_of(group_ids):
    length = group_ids.shape[0]
    token_index = jnp.arange(length, dtype=jnp.int32)
    labels = jnp.arange(CONTS + 1, dtype=jnp.int32)
    member = (group_ids[:, None] == labels[None, :]).astype(jnp.int32)
    counts = jnp.sum(member, axis=0)
    starts = jnp.cumsum(counts) - counts
    start_of = jnp.sum(member * starts[None, :], axis=1)
    return token_index - start_of + jnp.where(group_ids > 0, counts[0], 0)


def kept_pairs(choice_ids, rank_row, choice_hot, capacity):
    row_count, top_count, expert_total = choice_hot.shape
    per_k = jnp.sum(choice_hot, axis=0)
    before_k = jnp.cumsum(per_k, axis=0) - per_k
    lower = (rank_row[None, :] < rank_row[:, None]).astype(F32)
    same_k = jnp.dot(
        lower.astype(BF),
        choice_hot.reshape(row_count, top_count * expert_total).astype(BF),
        preferred_element_type=F32,
    ).reshape(row_count, top_count, expert_total)
    place = jnp.sum((same_k + before_k[None]) * choice_hot, axis=-1)
    return (place < capacity).astype(F32)


def mm(a, b):
    return jnp.dot(a, b, preferred_element_type=F32)


def mm_nt(a, b):
    return lax.dot_general(a, b, (((1,), (1,)), ((), ())), preferred_element_type=F32)


def mm_tn(a, b):
    return lax.dot_general(a, b, (((0,), (0,)), ((), ())), preferred_element_type=F32)


def gather(value, axes):
    return lax.all_gather(value, axes, axis=0, tiled=True)


def scatter_sum(value, axes):
    return lax.psum_scatter(value, axes, scatter_dimension=0, tiled=True)


def columns_out(value):
    count = lax.axis_size("shard")
    rows, width = value.shape
    parts = value.reshape(rows, count, width // count).transpose(1, 0, 2)
    return lax.all_to_all(parts, "shard", split_axis=0, concat_axis=0).reshape(
        count * rows, width // count
    )


def columns_back(value):
    count = lax.axis_size("shard")
    rows, width = value.shape
    parts = lax.all_to_all(
        value.reshape(count, rows // count, width), "shard", split_axis=0, concat_axis=0
    )
    return parts.transpose(1, 0, 2).reshape(rows // count, count * width)


def ffn_chunk(rows, cots, gates, w_gate, w_up, w_down, widths):
    tokens = rows.shape[0]
    spread = jnp.concatenate(
        [
            jnp.broadcast_to(gates[:, i : i + 1], (tokens, width))
            for i, width in enumerate(widths[:-1])
        ]
        + [jnp.ones((tokens, widths[-1]), F32)],
        axis=1,
    )
    gate_val = mm(rows, w_gate)
    up_val = mm(rows, w_up)
    down_grad = mm_nt(cots, w_down)
    sigmoid = jax.nn.sigmoid(gate_val)
    act = gate_val * sigmoid
    slope = sigmoid * (1.0 + gate_val * (1.0 - sigmoid))
    hidden = (act * up_val).astype(BF).astype(F32)
    scaled_hidden = (hidden * spread).astype(BF)
    part = mm(scaled_hidden, w_down).astype(BF)
    weighted = hidden * down_grad
    starts = [sum(widths[:i]) for i in range(len(widths) - 1)]
    gate_grads = jnp.stack(
        [jnp.sum(weighted[:, b : b + w], axis=1) for b, w in zip(starts, widths)], axis=1
    )
    down_grad = down_grad * spread
    gate_d = (down_grad * up_val * slope).astype(BF)
    up_d = (down_grad * act).astype(BF)
    back = (mm_nt(gate_d, w_gate) + mm_nt(up_d, w_up)).astype(BF)
    return (
        part,
        back,
        gate_grads,
        mm_tn(rows, gate_d),
        mm_tn(rows, up_d),
        mm_tn(scaled_hidden, cots),
    )


def on_device(
    tokens,
    cotangent,
    norm1_gain,
    q_weight,
    kva_weight,
    kv_gain,
    kvb_weight,
    o_weight,
    norm2_gain,
    router_weight,
    shared_gate,
    shared_up,
    shared_down,
    expert_gate,
    expert_up,
    expert_down,
    expert_ids,
    token_rank,
    seq_ids,
):
    expert_count = lax.axis_size("expert")
    shard_count = lax.axis_size("shard")
    device_count = expert_count * shard_count
    expert_at = lax.axis_index("expert")
    shard_at = lax.axis_index("shard")
    tok_rows, width = tokens.shape
    group_len = seq_ids.shape[0]
    local_experts = expert_gate.shape[0]
    all_experts = local_experts * expert_count
    top_count = expert_ids.shape[1]
    capacity = max(2, tok_rows * top_count // all_experts)
    score_scale = (NOPE + ROPE) ** (-0.5)
    own_heads = HEADS // shard_count
    latent_width = kva_weight.shape[1]

    q_mine = gather(columns_out(q_weight), "expert")
    kvb_mine = gather(columns_out(kvb_weight), "expert")
    kva_all = gather(kva_weight, BOTH)
    o_all = gather(o_weight, BOTH)
    o_mine = lax.dynamic_slice_in_dim(o_all, shard_at * own_heads * VDIM, own_heads * VDIM)
    norm1_scale = gather(norm1_gain, BOTH).astype(F32)
    latent_scale = gather(kv_gain, BOTH).astype(F32)
    norm2_scale = gather(norm2_gain, BOTH).astype(F32)
    router = gather(router_weight, BOTH)

    positions = positions_of(seq_ids)
    cosine_table, sine_table = rope_tables(positions, ROPE)
    token_index = jnp.arange(group_len, dtype=jnp.int32)
    allowed = (token_index[None, :] <= token_index[:, None]) & (
        (seq_ids[None, :] == 0) | (seq_ids[None, :] == seq_ids[:, None])
    )
    input_rows = tokens.astype(F32)
    group_rows = gather(tokens, "shard").astype(F32)
    normed_group, _ = rms_forward(group_rows, norm1_scale)
    hidden_one = normed_group.astype(BF)
    query_raw = mm(hidden_one, q_mine).reshape(group_len, own_heads, NOPE + ROPE)
    q_nope = query_raw[:, :, :NOPE].astype(BF)
    q_rope = rotate(
        query_raw[:, :, NOPE:], cosine_table[:, None, :], sine_table[:, None, :]
    ).astype(BF)
    compressed = mm(hidden_one, kva_all)
    latent_norm, inverse_latent = rms_forward(compressed[:, :KV_RANK], latent_scale)
    latent = latent_norm.astype(BF)
    k_rope = rotate(compressed[:, KV_RANK:], cosine_table, sine_table).astype(BF)
    keyval = mm(latent, kvb_mine).astype(BF).reshape(group_len, own_heads, NOPE + VDIM)
    keys = keyval[:, :, :NOPE]
    values = keyval[:, :, NOPE:]
    scores = jnp.einsum("qhd,khd->hqk", q_nope, keys, preferred_element_type=F32)
    scores = scores + jnp.einsum("qhd,kd->hqk", q_rope, k_rope, preferred_element_type=F32)
    scores = jnp.where(allowed[None], scores * score_scale, NEGATIVE)
    top_score = jnp.max(scores, axis=-1, keepdims=True)
    log_total = top_score + jnp.log(jnp.sum(jnp.exp(scores - top_score), axis=-1, keepdims=True))
    soft_probs = jnp.exp(scores - log_total)
    prob_low = soft_probs.astype(BF)
    attended = (
        jnp.einsum("hqk,khd->qhd", prob_low, values, preferred_element_type=F32)
        .astype(BF)
        .reshape(group_len, own_heads * VDIM)
    )
    projected = scatter_sum(mm(attended, o_mine).astype(BF), "shard").astype(F32)
    mixed = input_rows + projected

    normed_two, inverse_two = rms_forward(mixed, norm2_scale)
    hidden_two = normed_two.astype(BF)
    logits = mm(hidden_two, router)
    choice_hot = (
        expert_ids[:, :, None] == jnp.arange(all_experts, dtype=jnp.int32)[None, None, :]
    ).astype(F32)
    chosen = jnp.sum(choice_hot * logits[:, None, :], axis=-1)
    gate_probs = jax.nn.softmax(chosen, axis=-1)
    kept = kept_pairs(expert_ids, token_rank, choice_hot, capacity)
    gate_table = jnp.sum(choice_hot * (gate_probs * kept)[:, :, None], axis=1)

    shared_width = shared_down.shape[0]
    both_shared = jnp.stack([shared_gate, shared_up]).reshape(
        2, shared_gate.shape[0], device_count, shared_width
    )
    both_shared = lax.all_to_all(
        both_shared.transpose(2, 0, 1, 3), BOTH, split_axis=0, concat_axis=0
    )
    both_shared = both_shared.transpose(1, 0, 2, 3).reshape(2, width, shared_width)
    own_width = expert_gate.shape[2]
    widths = [own_width] * local_experts + [shared_width]
    w_gate = jnp.concatenate([expert_gate[i] for i in range(local_experts)] + [both_shared[0]], 1)
    w_up = jnp.concatenate([expert_up[i] for i in range(local_experts)] + [both_shared[1]], 1)
    w_down = jnp.concatenate([expert_down[i] for i in range(local_experts)] + [shared_down], 0)
    def ffn(rows, cots, table):
        rows_all = gather(rows, BOTH)
        cots_all = gather(cots, BOTH)
        gates_all = gather(table, BOTH)
        gates_mine = lax.dynamic_slice_in_dim(
            gates_all, expert_at * local_experts, local_experts, 1
        )
        out_part, back_part, gate_grads, *weight_grads = ffn_chunk(
            rows_all, cots_all, gates_mine, w_gate, w_up, w_down, widths
        )
        gate_grad_table = jnp.where(
            (jnp.arange(128) // local_experts == expert_at)[None, :],
            jnp.tile(gate_grads, (1, 128 // local_experts)),
            0.0,
        ).astype(BF)
        back_sum = scatter_sum(jnp.concatenate([back_part, gate_grad_table], axis=1), BOTH)
        return scatter_sum(out_part, BOTH), back_sum, weight_grads

    rounds = max(1, tok_rows * device_count // 4096)
    if rounds == 1:
        out_sum, back_sum, weight_grads = ffn(hidden_two, cotangent, gate_table)
    else:

        def one_round(total, part):
            out_rows, back_rows, grads = ffn(*part)
            return [t + g for t, g in zip(total, grads)], (out_rows, back_rows)

        in_rounds = lambda value: value.reshape((rounds, -1) + value.shape[1:])
        zeros = [jnp.zeros(w.shape, F32) for w in (w_gate, w_up, w_down)]
        weight_grads, (out_sum, back_sum) = lax.scan(
            one_round, zeros, (in_rounds(hidden_two), in_rounds(cotangent), in_rounds(gate_table))
        )
        out_sum = out_sum.reshape((tok_rows,) + out_sum.shape[2:])
        back_sum = back_sum.reshape((tok_rows,) + back_sum.shape[2:])
    out_sum, back_sum = out_sum.astype(F32), back_sum.astype(F32)
    w_gate_grad, w_up_grad, w_down_grad = weight_grads
    output = (mixed + out_sum).astype(BF)

    def split_experts(grad, axis):
        pieces = [
            lax.slice_in_dim(grad, i * own_width, (i + 1) * own_width, axis=axis)
            for i in range(local_experts)
        ]
        shared = lax.slice_in_dim(grad, local_experts * own_width, None, axis=axis)
        return jnp.stack(pieces), shared

    egate_grad, sgate_mine = split_experts(w_gate_grad, 1)
    eup_grad, sup_mine = split_experts(w_up_grad, 1)
    edown_grad, sdown_grad = split_experts(w_down_grad, 0)
    shared_grads = (
        jnp.stack([sgate_mine, sup_mine])
        .reshape(2, device_count, width // device_count, shared_width)
        .transpose(1, 0, 2, 3)
    )
    shared_grads = lax.all_to_all(shared_grads, BOTH, split_axis=0, concat_axis=0)
    shared_grads = shared_grads.transpose(1, 2, 0, 3).reshape(
        2, width // device_count, device_count * shared_width
    )

    upstream = cotangent.astype(F32)
    gate_grad = jnp.sum(
        choice_hot * back_sum[:, None, width : width + all_experts], axis=-1
    ) * kept
    chosen_grad = gate_probs * (gate_grad - jnp.sum(gate_probs * gate_grad, axis=-1, keepdims=True))
    logit_grad = jnp.sum(choice_hot * chosen_grad[:, :, None], axis=1).astype(BF)
    router_part = mm_tn(hidden_two, logit_grad)
    hidden_two_grad = back_sum[:, :width] + mm_nt(logit_grad, router)
    mixed_norm_grad, norm2_part = rms_backward(mixed, inverse_two, norm2_scale, hidden_two_grad)
    mixed_grad = upstream + mixed_norm_grad

    mixed_grad_group = gather(mixed_grad.astype(BF), "shard")
    o_part = mm_tn(attended, mixed_grad_group)
    attended_grad = (
        mm_nt(mixed_grad_group, o_mine).astype(BF).reshape(group_len, own_heads, VDIM)
    )
    prob_grad = jnp.einsum("qhd,khd->hqk", attended_grad, values, preferred_element_type=F32)
    values_grad = jnp.einsum("hqk,qhd->khd", prob_low, attended_grad, preferred_element_type=F32)
    score_grad = (
        soft_probs * (prob_grad - jnp.sum(soft_probs * prob_grad, axis=-1, keepdims=True))
    ).astype(BF)
    q_nope_grad = (
        jnp.einsum("hqk,khd->qhd", score_grad, keys, preferred_element_type=F32) * score_scale
    )
    q_rope_grad = (
        jnp.einsum("hqk,kd->qhd", score_grad, k_rope, preferred_element_type=F32) * score_scale
    )
    keys_grad = (
        jnp.einsum("hqk,qhd->khd", score_grad, q_nope, preferred_element_type=F32) * score_scale
    )
    rope_grad = (
        jnp.einsum("hqk,qhd->kd", score_grad, q_rope, preferred_element_type=F32) * score_scale
    )
    keyval_grad = (
        jnp.concatenate([keys_grad, values_grad], axis=-1)
        .reshape(group_len, own_heads * (NOPE + VDIM))
        .astype(BF)
    )
    kvb_part = mm_tn(latent, keyval_grad)
    latent_part = jnp.concatenate([mm_nt(keyval_grad, kvb_mine), rope_grad], axis=1).astype(BF)
    latent_sum = scatter_sum(latent_part, "shard").astype(F32)
    own_start = shard_at * tok_rows
    own_rows = lambda value: lax.dynamic_slice_in_dim(value, own_start, tok_rows)
    latent_raw_grad, kv_gain_part = rms_backward(
        own_rows(compressed[:, :KV_RANK]),
        own_rows(inverse_latent),
        latent_scale,
        latent_sum[:, :KV_RANK],
    )
    compressed_grad = jnp.concatenate(
        [
            latent_raw_grad,
            rotate(latent_sum[:, KV_RANK:], own_rows(cosine_table), -own_rows(sine_table)),
        ],
        axis=1,
    ).astype(BF)
    compressed_grad_group = gather(compressed_grad, "shard")
    kva_columns = latent_width // shard_count
    compressed_mine = lax.dynamic_slice_in_dim(
        compressed_grad_group, shard_at * kva_columns, kva_columns, 1
    )
    kva_mine = lax.dynamic_slice_in_dim(kva_all, shard_at * kva_columns, kva_columns, 1)
    query_grad = jnp.concatenate(
        [q_nope_grad, rotate(q_rope_grad, cosine_table[:, None, :], -sine_table[:, None, :])],
        axis=-1,
    )
    query_grad = query_grad.reshape(group_len, own_heads * (NOPE + ROPE)).astype(BF)
    q_part = mm_tn(hidden_one, query_grad)
    kva_part = mm_tn(hidden_one, compressed_mine)
    hidden_one_part = mm_nt(query_grad, q_mine) + mm_nt(compressed_mine, kva_mine)
    hidden_one_grad = scatter_sum(hidden_one_part.astype(BF), "shard").astype(F32)
    _, inverse_one = rms_forward(input_rows, norm1_scale)
    input_norm_grad, norm1_part = rms_backward(
        input_rows, inverse_one, norm1_scale, hidden_one_grad
    )
    tokens_grad = mixed_grad + input_norm_grad

    q_grad = columns_back(scatter_sum(q_part.astype(BF), "expert")).astype(F32)
    kva_grad = columns_back(scatter_sum(kva_part.astype(BF), "expert")).astype(F32)
    kvb_grad = columns_back(scatter_sum(kvb_part.astype(BF), "expert")).astype(F32)
    o_wide = lax.dynamic_update_slice_in_dim(
        jnp.zeros(o_all.shape, BF), o_part.astype(BF), shard_at * own_heads * VDIM, 0
    )
    o_grad = scatter_sum(o_wide, BOTH).astype(F32)
    router_grad = scatter_sum(router_part, BOTH)
    norm1_grad = scatter_sum(norm1_part, BOTH)
    norm2_grad = scatter_sum(norm2_part, BOTH)
    kv_gain_grad = scatter_sum(kv_gain_part, BOTH)
    return (
        output,
        tokens_grad,
        norm1_grad,
        q_grad,
        kva_grad,
        kv_gain_grad,
        kvb_grad,
        o_grad,
        norm2_grad,
        router_grad,
        shared_grads[0],
        shared_grads[1],
        sdown_grad,
        egate_grad,
        eup_grad,
        edown_grad,
    )


def solution(mesh):
    rows = P(BOTH, None)
    flat = P(BOTH)
    columns = P("expert", None, "shard")
    depth = P("expert", "shard", None)
    return jax.shard_map(
        on_device,
        mesh=mesh,
        in_specs=(
            rows,
            rows,
            flat,
            rows,
            rows,
            flat,
            rows,
            rows,
            flat,
            rows,
            rows,
            rows,
            rows,
            columns,
            columns,
            depth,
            rows,
            flat,
            P("expert"),
        ),
        out_specs=(
            rows,
            rows,
            flat,
            rows,
            rows,
            flat,
            rows,
            rows,
            flat,
            rows,
            rows,
            rows,
            rows,
            columns,
            columns,
            depth,
        ),
        check_vma=False,
    )
```

```python
import functools

import jax
import jax.numpy as jnp
from jax import lax
from jax.experimental import pallas as pl
from jax.experimental.pallas import tpu as pltpu
from jax.sharding import PartitionSpec as P

HEADS = 16
NOPE = 128
ROPE = 64
VDIM = 128
KV_RANK = 512
CONTS = 2


EPSILON = 1e-06
THETA = 10000.0
NEGATIVE = -1e30
BOTH = ("expert", "shard")
BF = jnp.bfloat16
F32 = jnp.float32


def rms_forward(values, gain_row):
    inverse = lax.rsqrt(jnp.mean(values * values, axis=-1, keepdims=True) + EPSILON)
    return (values * inverse * gain_row, inverse)


def rms_backward(values, inverse, gain_row, upstream):
    normed = values * inverse
    scaled = upstream * gain_row
    value_grad = inverse * (scaled - normed * jnp.mean(scaled * normed, axis=-1, keepdims=True))
    return (value_grad, jnp.sum(upstream * normed, axis=0))


def rope_tables(positions, width):
    half_width = width // 2
    frequency = THETA ** (-2.0 * jnp.arange(half_width, dtype=jnp.float32) / width)
    angles = positions.astype(jnp.float32)[:, None] * frequency[None, :]
    return (jnp.cos(angles), jnp.sin(angles))


def rotate(values, cosine_table, sine_table):
    half_width = values.shape[-1] // 2
    first_half = values[..., :half_width]
    second = values[..., half_width:]
    return jnp.concatenate(
        [
            first_half * cosine_table - second * sine_table,
            second * cosine_table + first_half * sine_table,
        ],
        axis=-1,
    )


def positions_of(group_ids):
    length = group_ids.shape[0]
    token_index = jnp.arange(length, dtype=jnp.int32)
    labels = jnp.arange(CONTS + 1, dtype=jnp.int32)
    member = (group_ids[:, None] == labels[None, :]).astype(jnp.int32)
    counts = jnp.sum(member, axis=0)
    starts = jnp.cumsum(counts) - counts
    start_of = jnp.sum(member * starts[None, :], axis=1)
    return token_index - start_of + jnp.where(group_ids > 0, counts[0], 0)


def kept_pairs(choice_ids, rank_row, choice_hot, capacity):
    row_count, top_count, expert_total = choice_hot.shape
    per_k = jnp.sum(choice_hot, axis=0)
    before_k = jnp.cumsum(per_k, axis=0) - per_k
    lower = (rank_row[None, :] < rank_row[:, None]).astype(F32)
    same_k = jnp.dot(
        lower.astype(BF),
        choice_hot.reshape(row_count, top_count * expert_total).astype(BF),
        preferred_element_type=F32,
    ).reshape(row_count, top_count, expert_total)
    place = jnp.sum((same_k + before_k[None]) * choice_hot, axis=-1)
    return (place < capacity).astype(F32)


def mm(a, b):
    return jnp.dot(a, b, preferred_element_type=F32)


def mm_nt(a, b):
    return lax.dot_general(a, b, (((1,), (1,)), ((), ())), preferred_element_type=F32)


def mm_tn(a, b):
    return lax.dot_general(a, b, (((0,), (0,)), ((), ())), preferred_element_type=F32)


def gather(value, axes):
    return lax.all_gather(value, axes, axis=0, tiled=True)


def scatter_sum(value, axes):
    return lax.psum_scatter(value, axes, scatter_dimension=0, tiled=True)


HBM = pl.BlockSpec(memory_space=pl.ANY)
VMEM = pl.BlockSpec(memory_space=pltpu.VMEM)


class Place:
    def __init__(self):
        e, s = lax.axis_index("expert"), lax.axis_index("shard")
        self.z, self.y, self.x, self.c = e // 2, e % 2, s // 2, s % 2

    def at(self, z=None, y=None, x=None, c=None):
        z = self.z if z is None else z
        y = self.y if y is None else y
        x = self.x if x is None else x
        c = self.c if c is None else c
        return {"expert": 2 * z + y, "shard": 2 * x + c}


def greet(partners):
    barrier = pltpu.get_barrier_semaphore()
    for partner in partners:
        pl.semaphore_signal(
            barrier, inc=1, device_id=partner, device_id_type=pl.DeviceIdType.MESH
        )
    pl.semaphore_wait(barrier, len(partners))


def remote(src, dst, send, recv, where):
    return pltpu.make_async_remote_copy(
        src_ref=src,
        dst_ref=dst,
        send_sem=send,
        recv_sem=recv,
        device_id=where,
        device_id_type=pl.DeviceIdType.MESH,
    )


def gather_all_kernel(lines, chunks, src, dst, own_sem, zs, zr, xs, xr, ys, yr, ds_, dr, cs, cr):
    me = Place()
    z, y, x, c = me.z, me.y, me.x, me.c
    rows, width = src.shape
    step_rows = rows // chunks
    half = width // 256 * 128
    others = [lax.rem(z + 1 + j, lines) for j in range(lines - 1)]
    to_x, to_y, to_c = me.at(x=1 - x), me.at(y=1 - y), me.at(c=1 - c)
    greet([me.at(z=o) for o in others] + [to_x, to_y, to_c])
    cuts = (pl.ds(0, half), pl.ds(half, width - half))

    def block(zz, yy, xx, k, cols=None, cc=None):
        return dst.at[
            zz, yy, xx, c if cc is None else cc,
            pl.ds(k * step_rows, step_rows),
            pl.ds(0, width) if cols is None else cuts[cols],
        ]

    own = pltpu.make_async_copy(src, dst.at[z, y, x, c], own_sem)
    own.start()
    pending = []

    def go(copy):
        copy.start()
        pending.append(copy)
        return copy

    order = [None] + list(range(lines - 1))

    def piece(k):
        return src.at[pl.ds(k * step_rows, step_rows)]

    def z_start(k):
        for j, o in enumerate(others):
            go(remote(piece(k), block(z, y, x, k), zs.at[k, j], zr.at[k, z], me.at(z=o)))
        go(remote(piece(k), block(z, y, x, k), xs.at[k, lines - 1], xr.at[k, z], to_x))
        go(remote(piece(k), block(z, y, x, k), ys.at[k, lines - 1], yr.at[k, z], to_y))

    def z_land(k):
        for j, o in reversed(list(enumerate(others))):
            b = block(o, y, x, k)
            remote(b, b, zs.at[k, j], zr.at[k, o], me.at(z=o)).wait_recv()
            go(remote(b, b, xs.at[k, j], xr.at[k, o], to_x))
            go(remote(b, b, ys.at[k, j], yr.at[k, o], to_y))

    def core_send(k, slot, yy, xx):
        b = dst.at[:, yy, xx, c, pl.ds(k * step_rows, step_rows)]
        go(remote(b, b, cs.at[k, slot], cr.at[k, slot], to_c))

    def xy_land(k):
        for j, o in [(lines - 1, z)] + list(reversed(list(enumerate(others)))):
            b = block(o, y, 1 - x, k)
            remote(b, b, xs.at[k, j], xr.at[k, o], to_x).wait_recv()
            b = block(o, y, 1 - x, k, 0)
            go(remote(b, b, ds_.at[k, j, 0], dr.at[k, o, 0], to_y))
            b = block(o, 1 - y, x, k)
            remote(b, b, ys.at[k, j], yr.at[k, o], to_y).wait_recv()
            b = block(o, 1 - y, x, k, 1)
            go(remote(b, b, ds_.at[k, j, 1], dr.at[k, o, 1], to_x))
        core_send(k, 1, y, 1 - x)
        core_send(k, 2, 1 - y, x)

    def diag_land(k):
        for j, o in [(lines - 1, z)] + list(reversed(list(enumerate(others)))):
            for h, w in ((0, to_y), (1, to_x)):
                b = block(o, 1 - y, 1 - x, k, h)
                remote(b, b, ds_.at[k, j, h], dr.at[k, o, h], w).wait_recv()
        core_send(k, 3, 1 - y, 1 - x)

    for step in range(chunks + 2):
        if step < chunks:
            z_start(step)
        if step < chunks:
            z_land(step)
            if step == 0:
                own.wait()
            core_send(step, 0, y, x)
        if 1 <= step <= chunks:
            xy_land(step - 1)
        if step >= 2:
            diag_land(step - 2)
    for k in range(chunks):
        for slot, (yy, xx) in enumerate(((y, x), (y, 1 - x), (1 - y, x), (1 - y, 1 - x))):
            b = dst.at[:, yy, xx, 1 - c, pl.ds(k * step_rows, step_rows)]
            remote(b, b, cs.at[k, slot], cr.at[k, slot], to_c).wait_recv()
    for copy in pending:
        copy.wait_send()


def gather_all(value, lines, ident, chunks=4):
    rows, width = value.shape
    dma = pltpu.SemaphoreType.DMA
    out = pl.pallas_call(
        functools.partial(gather_all_kernel, lines, chunks),
        out_shape=jax.ShapeDtypeStruct((lines, 2, 2, 2, rows, width), value.dtype),
        in_specs=[HBM],
        out_specs=HBM,
        scratch_shapes=[
            dma,
            dma((chunks, lines)), dma((chunks, lines)),
            dma((chunks, lines)), dma((chunks, lines)),
            dma((chunks, lines)), dma((chunks, lines)),
            dma((chunks, lines, 2)), dma((chunks, lines, 2)),
            dma((chunks, 4)), dma((chunks, 4)),
        ],
        compiler_params=pltpu.CompilerParams(collective_id=ident, has_side_effects=True),
    )(value)
    return out.reshape(lines * 8 * rows, width)


def add_into(target, other, rows):
    @pl.loop(0, rows // 16)
    def _(i):
        at = pl.ds(pl.multiple_of(i * 16, 16), 16)
        target[at] = (target[at].astype(F32) + other[at].astype(F32)).astype(target.dtype)


def sum_all_kernel(
    lines, cuts, part, out, acc, cbuf, xbuf, ybuf, zbuf, xdiag, ydiag,
    ls, cs, cr, xs, xr, ys, yr, zs, zr, xds, xdr, yds, ydr,
):
    me = Place()
    z, y, x, c = me.z, me.y, me.x, me.c
    rows, width = out.shape
    cut = rows // cuts
    half = width // 256 * 128
    others = [lax.rem(z + 1 + j, lines) for j in range(lines - 1)]
    to_x, to_y, to_c = me.at(x=1 - x), me.at(y=1 - y), me.at(c=1 - c)
    greet([me.at(z=o) for o in others] + [to_x, to_y, to_c])
    steps = [(o, k) for o in others + [z] for k in range(cuts)]
    cols = (pl.ds(0, half), pl.ds(half, width - half))
    sides = ((1 - y, 1 - x), (1 - y, x), (y, 1 - x), (y, x))
    pending = []

    def go(copy):
        copy.start()
        pending.append(copy)

    def span(k):
        return pl.ds(k * cut, cut)

    def load(n, side):
        o, k = steps[n]
        yy, xx = sides[side]
        return pltpu.make_async_copy(
            part.at[o, yy, xx, c, span(k)], acc.at[o, yy, xx, span(k)], ls.at[n, side]
        )

    def to_core(n, side):
        o, k = steps[n]
        yy, xx = sides[side]
        return remote(
            part.at[o, yy, xx, 1 - c, span(k)],
            cbuf.at[o, yy, xx, span(k)],
            cs.at[n, side],
            cr.at[n, side],
            to_c,
        )

    def both_cores(n, side):
        o, k = steps[n]
        yy, xx = sides[side]
        load(n, side).wait()
        to_core(n, side).wait_recv()
        add_into(acc.at[o, yy, xx, span(k)], cbuf.at[o, yy, xx, span(k)], cut)

    def diag_sends(n):
        o, k = steps[n]
        block = acc.at[o, 1 - y, 1 - x, span(k)]
        return (
            remote(block.at[:, cols[0]], xdiag.at[o, span(k)], xds.at[n], xdr.at[n], to_x),
            remote(block.at[:, cols[1]], ydiag.at[o, span(k)], yds.at[n], ydr.at[n], to_y),
        )

    def side_sends(n):
        o, k = steps[n]
        return (
            remote(acc.at[o, y, 1 - x, span(k)], xbuf.at[o, span(k)], xs.at[n], xr.at[n], to_x),
            remote(acc.at[o, 1 - y, x, span(k)], ybuf.at[o, span(k)], ys.at[n], yr.at[n], to_y),
        )

    def z_copy(n):
        o, k = steps[n]
        return remote(
            acc.at[o, y, x, span(k)], zbuf.at[z, span(k)], zs.at[n], zr.at[z, k], me.at(z=o)
        )

    def first(n):
        both_cores(n, 0)
        for copy in diag_sends(n):
            go(copy)

    def second(n):
        o, k = steps[n]
        both_cores(n, 1)
        both_cores(n, 2)
        from_x, from_y = diag_sends(n)
        from_x.wait_recv()
        add_into(acc.at[o, 1 - y, x, span(k), cols[0]], xdiag.at[o, span(k)], cut)
        from_y.wait_recv()
        add_into(acc.at[o, y, 1 - x, span(k), cols[1]], ydiag.at[o, span(k)], cut)
        for copy in side_sends(n):
            go(copy)

    def third(n):
        o, k = steps[n]
        both_cores(n, 3)
        from_x, from_y = side_sends(n)
        from_x.wait_recv()
        from_y.wait_recv()
        add_into(acc.at[o, y, x, span(k)], xbuf.at[o, span(k)], cut)
        add_into(acc.at[o, y, x, span(k)], ybuf.at[o, span(k)], cut)
        if n < (lines - 1) * cuts:
            go(z_copy(n))

    total = len(steps)
    for n in range(total + 2):
        for back, side_list in ((0, (0,)), (1, (1, 2)), (2, (3,))):
            if 0 <= n - back < total:
                for side in side_list:
                    go(to_core(n - back, side))
                    load(n - back, side).start()
    for n in range(total + 2):
        if n < total:
            first(n)
        if 0 <= n - 1 < total:
            second(n - 1)
        if 0 <= n - 2 < total:
            third(n - 2)
    for k in range(cuts):
        for o in others:
            block = zbuf.at[o, span(k)]
            remote(block, block, zs.at[0], zr.at[o, k], me.at(z=o)).wait_recv()

    @pl.loop(0, rows // 16)
    def _(i):
        at = pl.ds(pl.multiple_of(i * 16, 16), 16)
        value = acc[z, y, x, at].astype(F32)
        for o in others:
            value = value + zbuf[o, at].astype(F32)
        out[at] = value.astype(out.dtype)

    for copy in pending:
        copy.wait_send()


def sum_all(part, lines, rows, ident, cuts=2):
    width = part.shape[-1]
    part = part.reshape(lines, 2, 2, 2, rows, width)
    dma = pltpu.SemaphoreType.DMA
    n = lines * cuts
    buf = lambda *lead: pltpu.VMEM(lead + (rows, width), part.dtype)
    half = width // 256 * 128
    diag = lambda size: pltpu.VMEM((lines, rows, size), part.dtype)
    return pl.pallas_call(
        functools.partial(sum_all_kernel, lines, cuts),
        out_shape=jax.ShapeDtypeStruct((rows, width), F32),
        in_specs=[HBM],
        out_specs=VMEM,
        scratch_shapes=[
            buf(lines, 2, 2), buf(lines, 2, 2), buf(lines), buf(lines), buf(lines),
            diag(half), diag(width - half),
            dma((n, 4)), dma((n, 4)), dma((n, 4)),
            dma((n,)), dma((n,)), dma((n,)), dma((n,)), dma((n,)), dma((lines, cuts)),
            dma((n,)), dma((n,)), dma((n,)), dma((n,)),
        ],
        compiler_params=pltpu.CompilerParams(
            collective_id=ident, has_side_effects=True, vmem_limit_bytes=56 << 20
        ),
    )(part)


def gather_group_kernel(cuts, src, dst, own_sem, send, recv):
    me = Place()
    x, c = me.x, me.c
    to_x, to_c = me.at(x=1 - x), me.at(c=1 - c)
    greet([to_x, to_c])
    cut = src.shape[0] // cuts
    span = lambda k: pl.ds(k * cut, cut)
    own = pltpu.make_async_copy(src, dst.at[x, c], own_sem)
    own.start()
    over_x = [
        remote(src.at[span(k)], dst.at[x, c, span(k)], send.at[0, k], recv.at[0, k], to_x)
        for k in range(cuts)
    ]
    for copy in over_x:
        copy.start()
    over_c = remote(src, dst.at[x, c], send.at[1, 0], recv.at[1, 0], to_c)
    over_c.start()
    relays = []
    for k in range(cuts):
        far = dst.at[1 - x, c, span(k)]
        remote(far, far, send.at[0, k], recv.at[0, k], to_x).wait_recv()
        relays.append(remote(far, far, send.at[2, k], recv.at[2, k], to_c))
        relays[-1].start()
    far = dst.at[x, 1 - c]
    remote(far, far, send.at[1, 0], recv.at[1, 0], to_c).wait_recv()
    for k in range(cuts):
        far = dst.at[1 - x, 1 - c, span(k)]
        remote(far, far, send.at[2, k], recv.at[2, k], to_c).wait_recv()
    own.wait()
    for copy in over_x + [over_c] + relays:
        copy.wait_send()


def gather_group(value, ident, cuts=4):
    rows, width = value.shape
    dma = pltpu.SemaphoreType.DMA
    out = pl.pallas_call(
        functools.partial(gather_group_kernel, cuts),
        out_shape=jax.ShapeDtypeStruct((2, 2, rows, width), value.dtype),
        in_specs=[HBM],
        out_specs=HBM,
        scratch_shapes=[dma, dma((3, cuts)), dma((3, cuts))],
        compiler_params=pltpu.CompilerParams(collective_id=ident, has_side_effects=True),
    )(value)
    return out.reshape(4 * rows, width)


def sum_group_kernel(cuts, part, out, cbuf, xbuf, xsum, cs, cr, xs, xr):
    me = Place()
    x, c = me.x, me.c
    rows, width = out.shape
    cut = rows // cuts
    to_x, to_c = me.at(x=1 - x), me.at(c=1 - c)
    greet([to_x, to_c])
    span = lambda k: pl.ds(k * cut, cut)
    core = lambda k, far: remote(
        part.at[1 - x if far else x, 1 - c, span(k)],
        cbuf.at[far, span(k)],
        cs.at[k, far],
        cr.at[k, far],
        to_c,
    )
    over = lambda k: remote(xsum.at[span(k)], xbuf.at[span(k)], xs.at[k], xr.at[k], to_x)
    for k in range(cuts):
        core(k, 1).start()
    for k in range(cuts):
        core(k, 0).start()

    def add(k, target, one, two):
        @pl.loop(0, cut // 16)
        def _(i):
            at = pl.ds(pl.multiple_of(k * cut + i * 16, 16), 16)
            target[at] = (one[at].astype(F32) + two[at].astype(F32)).astype(target.dtype)

    for k in range(cuts):
        core(k, 1).wait_recv()
        add(k, xsum, part.at[1 - x, c], cbuf.at[1])
        over(k).start()
    for k in range(cuts):
        core(k, 0).wait_recv()
        add(k, out, part.at[x, c], cbuf.at[0])
    for k in range(cuts):
        over(k).wait_recv()
        add(k, out, out, xbuf)
    for k in range(cuts):
        core(k, 1).wait_send()
        core(k, 0).wait_send()
        over(k).wait_send()


def sum_group(part, ident, cuts=4):
    rows, width = part.shape[0] // 4, part.shape[1]
    dma = pltpu.SemaphoreType.DMA
    buf = lambda *lead: pltpu.VMEM(lead + (rows, width), part.dtype)
    return pl.pallas_call(
        functools.partial(sum_group_kernel, cuts),
        out_shape=jax.ShapeDtypeStruct((rows, width), F32),
        in_specs=[VMEM],
        out_specs=VMEM,
        scratch_shapes=[
            buf(2), buf(), buf(),
            dma((cuts, 2)), dma((cuts, 2)), dma((cuts,)), dma((cuts,)),
        ],
        compiler_params=pltpu.CompilerParams(
            collective_id=ident, has_side_effects=True, vmem_limit_bytes=32 << 20
        ),
    )(part.reshape(2, 2, rows, width))


def add_blocks(target, one, two):
    if len(target.shape) > 2:
        for i in range(target.shape[0]):
            add_blocks(target.at[i], one.at[i], two.at[i])
        return
    rows = target.shape[0]
    step = 16 if rows % 16 == 0 else rows

    @pl.loop(0, rows // step)
    def _(i):
        at = pl.ds(pl.multiple_of(i * step, step), step)
        target[at] = (one[at].astype(F32) + two[at].astype(F32)).astype(target.dtype)


class Copies:
    def __init__(self):
        self.started = []

    def go(self, copy):
        copy.start()
        self.started.append(copy)

    def finish(self):
        for copy in self.started:
            copy.wait_send()


def start_kernel(lines, with_o, *refs):
    jobs = 3
    tok, kva, *sources = refs[: 2 + jobs]
    refs = refs[2 + jobs :]
    if with_o:
        o_src, refs = refs[0], refs[1:]
    tok_dst, kva_dst, *dests = refs[: 2 + jobs]
    refs = refs[2 + jobs :]
    if with_o:
        o_dst, refs = refs[0], refs[1:]
    own_sem, gs, gr, zs, zr, ys, yr, ts, tr, ks, kr, kzs, kzr, kys, kyr = refs[:15]
    if with_o:
        o_own, ocs, ocr, ozs, ozr, oys, oyr = refs[15:]
    me = Place()
    z, y, x, c = me.z, me.y, me.x, me.c
    others = [lax.rem(z + 1 + j, lines) for j in range(lines - 1)]
    near = [(x, 1 - c), (1 - x, c), (1 - x, 1 - c)]
    to_near = [me.at(x=xx, c=cc) for xx, cc in near]
    to_y, to_x, to_c = me.at(y=1 - y), to_near[1], to_near[0]
    greet([me.at(z=o) for o in others] + [to_y] + to_near)
    copies = Copies()
    go = copies.go

    locals_ = [
        pltpu.make_async_copy(src.at[x, c], dst.at[z, y, x, c], own_sem.at[i])
        for i, (src, dst) in enumerate(zip(sources, dests))
    ]
    locals_.append(pltpu.make_async_copy(tok, tok_dst.at[x, c], own_sem.at[jobs]))
    locals_.append(pltpu.make_async_copy(kva, kva_dst.at[z, y, x, c], own_sem.at[jobs + 1]))
    for copy in locals_:
        copy.start()
    near_copy = lambda i, p: remote(
        sources[i].at[near[p][0], near[p][1]],
        dests[i].at[z, y, x, c],
        gs.at[i, p],
        gr.at[i, p],
        to_near[p],
    )
    for i in range(jobs):
        for p in range(3):
            go(near_copy(i, p))
    if with_o:
        o_core = remote(o_src, o_dst.at[z, c], ocs, ocr, to_c)
        o_local = pltpu.make_async_copy(o_src, o_dst.at[z, c], o_own)
        holder = c == y

        @pl.when(jnp.logical_not(holder))
        def _():
            o_core.start()

        @pl.when(holder)
        def _():
            o_local.start()

    kva_z = lambda j, o: remote(
        kva, kva_dst.at[z, y, x, c], kzs.at[j], kzr.at[z], me.at(z=o)
    )
    for j, o in enumerate(others):
        go(kva_z(j, o))
    kva_y = lambda j, o, src: remote(src, kva_dst.at[o, y, x, c], kys.at[j], kyr.at[o], to_y)
    go(kva_y(lines - 1, z, kva))
    tok_copies = [
        remote(tok, tok_dst.at[x, c], ts.at[p], tr.at[p], to_near[p]) for p in range(3)
    ]
    for copy in tok_copies:
        go(copy)
    line_y = lambda i, j, o: remote(
        dests[i].at[o, y], dests[i].at[o, y], ys.at[i, j], yr.at[i, o], to_y
    )
    line_z = lambda i, j, o: remote(
        dests[i].at[z, y], dests[i].at[z, y], zs.at[i, j], zr.at[i, z], me.at(z=o)
    )
    for i in range(jobs):
        locals_[i].wait()
        for p in range(3):
            xx, cc = near[p]
            block = dests[i].at[z, y, xx, cc]
            remote(block, block, gs.at[i, p], gr.at[i, p], to_near[p]).wait_recv()
        for j, o in enumerate(others):
            go(line_z(i, j, o))
        go(line_y(i, lines - 1, z))
    if with_o:
        o_z = lambda j, o: remote(o_dst.at[z], o_dst.at[z], ozs.at[j], ozr.at[z], me.at(z=o))
        o_y = lambda j, o: remote(o_dst.at[o], o_dst.at[o], oys.at[j], oyr.at[o], to_y)

        @pl.when(holder)
        def _():
            o_local.wait()
            block = o_dst.at[z, 1 - c]
            remote(block, block, ocs, ocr, to_c).wait_recv()
            for j, o in enumerate(others):
                o_z(j, o).start()
            o_y(lines - 1, z).start()

    for j, o in reversed(list(enumerate(others))):
        block = kva_dst.at[o, y, x, c]
        remote(block, block, kzs.at[j], kzr.at[o], me.at(z=o)).wait_recv()
        go(kva_y(j, o, block))
        for i in range(jobs):
            block = dests[i].at[o, y]
            remote(block, block, zs.at[i, j], zr.at[i, o], me.at(z=o)).wait_recv()
            go(line_y(i, j, o))
        if with_o:

            @pl.when(holder)
            def _(j=j, o=o):
                block = o_dst.at[o]
                remote(block, block, ozs.at[j], ozr.at[o], me.at(z=o)).wait_recv()
                o_y(j, o).start()

    for o in others + [z]:
        block = kva_dst.at[o, 1 - y, x, c]
        remote(block, block, kys.at[0], kyr.at[o], to_y).wait_recv()
    locals_[jobs + 1].wait()
    plane = kva_dst.at[:, :, x, c]
    go(remote(plane, plane, ks.at[0], kr.at[0], to_x))
    go(remote(plane, plane, ks.at[1], kr.at[1], to_c))
    plane = kva_dst.at[:, :, 1 - x, c]
    remote(plane, plane, ks.at[0], kr.at[0], to_x).wait_recv()
    go(remote(plane, plane, ks.at[2], kr.at[2], to_c))
    for p in range(3):
        xx, cc = near[p]
        block = tok_dst.at[xx, cc]
        remote(block, block, ts.at[p], tr.at[p], to_near[p]).wait_recv()
    locals_[jobs].wait()
    for o in others + [z]:
        for i in range(jobs):
            block = dests[i].at[o, 1 - y]
            remote(block, block, ys.at[i, 0], yr.at[i, o], to_y).wait_recv()
    if with_o:

        @pl.when(jnp.logical_not(holder))
        def _():
            for o in others + [z]:
                remote(o_dst.at[o], o_dst.at[o], oys.at[0], oyr.at[o], to_y).wait_recv()
            o_core.wait_send()

        @pl.when(holder)
        def _():
            for j, o in list(enumerate(others)):
                o_z(j, o).wait_send()
                o_y(j, o).wait_send()
            o_y(lines - 1, z).wait_send()

    for slot, xx in ((1, x), (2, 1 - x)):
        plane = kva_dst.at[:, :, xx, 1 - c]
        remote(plane, plane, ks.at[slot], kr.at[slot], to_c).wait_recv()
    copies.finish()


def start_gather(tokens, kva, column_parts, o_rows, lines, ident):
    jobs = len(column_parts)
    with_o = o_rows is not None
    inputs = [tokens, kva] + column_parts + ([o_rows] if with_o else [])
    shape = lambda lead, v: jax.ShapeDtypeStruct(lead + v.shape, v.dtype)
    outs = [shape((2, 2), tokens), shape((lines, 2, 2, 2), kva)]
    outs += [jax.ShapeDtypeStruct((lines, 2) + v.shape, v.dtype) for v in column_parts]
    if with_o:
        outs.append(shape((lines, 2), o_rows))
    dma = pltpu.SemaphoreType.DMA
    scratch = [
        dma((jobs + 2,)), dma((jobs, 3)), dma((jobs, 3)),
        dma((jobs, lines)), dma((jobs, lines)), dma((jobs, lines)), dma((jobs, lines)),
        dma((3,)), dma((3,)), dma((3,)), dma((3,)),
        dma((lines,)), dma((lines,)), dma((lines,)), dma((lines,)),
    ]
    if with_o:
        scratch += [dma, dma, dma, dma((lines,)), dma((lines,)), dma((lines,)), dma((lines,))]
    return pl.pallas_call(
        functools.partial(start_kernel, lines, with_o),
        out_shape=outs,
        in_specs=[HBM] * len(inputs),
        out_specs=[HBM] * len(outs),
        scratch_shapes=scratch,
        compiler_params=pltpu.CompilerParams(collective_id=ident, has_side_effects=True),
    )(*inputs)


def grads_kernel(lines, kinds, with_o, *refs):
    jobs = len(kinds)
    take = lambda n: [refs.pop(0) for _ in range(n)]
    refs = list(refs)
    parts = take(jobs)
    o_part = take(1)[0] if with_o else None
    outs = take(jobs)
    o_out = take(1)[0] if with_o else None
    accs, ybufs, zbufs, tots = take(jobs), take(jobs), take(jobs), take(jobs)
    if with_o:
        o_acc, o_ybuf, o_zbuf, o_tot = take(4)
    ys, yr, zs, zr, gs, gr = take(6)
    if with_o:
        oys, oyr, ozs, ozr, ocs, ocr = take(6)
    me = Place()
    z, y, x, c = me.z, me.y, me.x, me.c
    others = [lax.rem(z + 1 + j, lines) for j in range(lines - 1)]
    near = [(x, 1 - c), (1 - x, c), (1 - x, 1 - c)]
    to_near = [me.at(x=xx, c=cc) for xx, cc in near]
    to_y, to_c = me.at(y=1 - y), to_near[0]
    greet([me.at(z=o) for o in others] + [to_y] + to_near)
    copies = Copies()
    go = copies.go
    over_y = lambda i, j, o: remote(
        parts[i].at[o, 1 - y], ybufs[i].at[o], ys.at[i, j], yr.at[i, o], to_y
    )
    over_z = lambda i, j, o: remote(
        accs[i].at[o], zbufs[i].at[z], zs.at[i, j], zr.at[i, z], me.at(z=o)
    )
    places = list(enumerate(others)) + [(lines - 1, z)]
    if with_o:
        holder = c == y
        o_over_y = lambda j, o: remote(o_part.at[o], o_ybuf.at[o], oys.at[j], oyr.at[o], to_y)
        o_over_z = lambda j, o: remote(
            o_acc.at[o], o_zbuf.at[z], ozs.at[j], ozr.at[z], me.at(z=o)
        )
    for j, o in places:
        for i in range(jobs):
            go(over_y(i, j, o))
        if with_o:

            @pl.when(jnp.logical_not(holder))
            def _(j=j, o=o):
                o_over_y(j, o).start()

    for j, o in places:
        for i in range(jobs):
            remote(ybufs[i].at[o], ybufs[i].at[o], ys.at[i, j], yr.at[i, o], to_y).wait_recv()
            add_blocks(accs[i].at[o], parts[i].at[o, y], ybufs[i].at[o])
            if j < lines - 1:
                go(over_z(i, j, o))
        if with_o:

            @pl.when(holder)
            def _(j=j, o=o):
                remote(o_ybuf.at[o], o_ybuf.at[o], oys.at[j], oyr.at[o], to_y).wait_recv()
                add_blocks(o_acc.at[o], o_part.at[o], o_ybuf.at[o])
                if j < lines - 1:
                    o_over_z(j, o).start()

    def line_sum(target, acc, zbuf):
        if len(target.shape) > 2:
            for k in range(target.shape[0]):
                line_sum(target.at[k], acc.at[:, k], zbuf.at[:, k])
            return
        rows = target.shape[0]
        step = 16 if rows % 16 == 0 else rows

        @pl.loop(0, rows // step)
        def _(i):
            at = pl.ds(pl.multiple_of(i * step, step), step)
            value = acc[z, at].astype(F32)
            for o in others:
                value = value + zbuf[o, at].astype(F32)
            target[at] = value.astype(target.dtype)

    near_copy = lambda i, p: remote(
        tots[i].at[near[p][0], near[p][1]], outs[i].at[x, c], gs.at[i, p], gr.at[i, p], to_near[p]
    )
    for i in range(jobs):
        for j, o in places[:-1]:
            block = zbufs[i].at[o]
            remote(block, block, zs.at[i, j], zr.at[i, o], me.at(z=o)).wait_recv()
        if kinds[i]:
            for xx in range(2):
                for cc in range(2):
                    line_sum(tots[i].at[xx, cc], accs[i].at[:, xx, cc], zbufs[i].at[:, xx, cc])
            for p in range(3):
                go(near_copy(i, p))
            rows = tots[i].shape[2]
            outs[i][x, c] = tots[i][x, c]
        else:
            line_sum(outs[i], accs[i], zbufs[i])
    if with_o:
        o_core = remote(o_tot.at[1 - c], o_out, ocs, ocr, to_c)

        @pl.when(holder)
        def _():
            for j, o in places[:-1]:
                block = o_zbuf.at[o]
                remote(block, block, ozs.at[j], ozr.at[o], me.at(z=o)).wait_recv()
            line_sum(o_tot.at[1 - c], o_acc.at[:, 1 - c], o_zbuf.at[:, 1 - c])
            o_core.start()
            line_sum(o_out, o_acc.at[:, c], o_zbuf.at[:, c])
            for j, o in places[:-1]:
                o_over_z(j, o).wait_send()
            o_core.wait_send()

        @pl.when(jnp.logical_not(holder))
        def _():
            for j, o in places:
                o_over_y(j, o).wait_send()
            o_core.wait_recv()

    for i in range(jobs):
        if kinds[i]:
            for p in range(3):
                block = outs[i].at[near[p][0], near[p][1]]
                remote(block, block, gs.at[i, p], gr.at[i, p], to_near[p]).wait_recv()
    copies.finish()


def sum_grads(parts, kinds, o_part, lines, ident):
    jobs = len(parts)
    with_o = o_part is not None
    inputs = list(parts) + ([o_part] if with_o else [])
    outs = [jax.ShapeDtypeStruct(p.shape[2:], p.dtype) for p in parts]
    if with_o:
        outs.append(jax.ShapeDtypeStruct(o_part.shape[2:], o_part.dtype))
    dma = pltpu.SemaphoreType.DMA
    line = lambda p: pltpu.VMEM((lines,) + p.shape[2:], p.dtype)
    scratch = [line(p) for p in parts] * 3
    scratch += [pltpu.VMEM(p.shape[2:] if k else (8, 128), p.dtype) for p, k in zip(parts, kinds)]
    if with_o:
        scratch += [pltpu.VMEM(o_part.shape, o_part.dtype)] * 3
        scratch += [pltpu.VMEM(o_part.shape[1:], o_part.dtype)]
    scratch += [dma((jobs, lines))] * 4 + [dma((jobs, 3))] * 2
    if with_o:
        scratch += [dma((lines,))] * 4 + [dma, dma]
    return pl.pallas_call(
        functools.partial(grads_kernel, lines, tuple(kinds), with_o),
        out_shape=outs,
        in_specs=[VMEM] * len(inputs),
        out_specs=[VMEM] * len(outs),
        scratch_shapes=scratch,
        compiler_params=pltpu.CompilerParams(
            collective_id=ident, has_side_effects=True, vmem_limit_bytes=56 << 20
        ),
    )(*inputs)


def ffn_chunk(rows, cots, gates, w_gate, w_up, w_down, widths):
    tokens = rows.shape[0]
    spread = jnp.concatenate(
        [
            jnp.broadcast_to(gates[:, i : i + 1], (tokens, width))
            for i, width in enumerate(widths[:-1])
        ]
        + [jnp.ones((tokens, widths[-1]), F32)],
        axis=1,
    )
    gate_val = mm(rows, w_gate)
    up_val = mm(rows, w_up)
    down_grad = mm_nt(cots, w_down)
    sigmoid = jax.nn.sigmoid(gate_val)
    act = gate_val * sigmoid
    slope = sigmoid * (1.0 + gate_val * (1.0 - sigmoid))
    hidden = (act * up_val).astype(BF).astype(F32)
    scaled_hidden = (hidden * spread).astype(BF)
    part = mm(scaled_hidden, w_down).astype(BF)
    weighted = hidden * down_grad
    starts = [sum(widths[:i]) for i in range(len(widths) - 1)]
    gate_grads = jnp.stack(
        [jnp.sum(weighted[:, b : b + w], axis=1) for b, w in zip(starts, widths)], axis=1
    )
    down_grad = down_grad * spread
    gate_d = (down_grad * up_val * slope).astype(BF)
    up_d = (down_grad * act).astype(BF)
    back = (mm_nt(gate_d, w_gate) + mm_nt(up_d, w_up)).astype(BF)
    return (
        part,
        back,
        gate_grads,
        mm_tn(rows, gate_d),
        mm_tn(rows, up_d),
        mm_tn(scaled_hidden, cots),
    )


def on_device(
    tokens,
    cotangent,
    norm1_gain,
    q_weight,
    kva_weight,
    kv_gain,
    kvb_weight,
    o_weight,
    norm2_gain,
    router_weight,
    shared_gate,
    shared_up,
    shared_down,
    expert_gate,
    expert_up,
    expert_down,
    expert_ids,
    token_rank,
    seq_ids,
):
    expert_count = lax.axis_size("expert")
    shard_count = lax.axis_size("shard")
    device_count = expert_count * shard_count
    expert_at = lax.axis_index("expert")
    shard_at = lax.axis_index("shard")
    tok_rows, width = tokens.shape
    group_len = seq_ids.shape[0]
    local_experts = expert_gate.shape[0]
    all_experts = local_experts * expert_count
    top_count = expert_ids.shape[1]
    capacity = max(2, tok_rows * top_count // all_experts)
    score_scale = (NOPE + ROPE) ** (-0.5)
    own_heads = HEADS // shard_count
    latent_width = kva_weight.shape[1]

    lines = expert_count // 2
    o_rows = o_weight.shape[0]
    o_pairs = VDIM == 2 * o_rows

    def by_head(weight):
        rows = weight.shape[0]
        heads = weight.reshape(rows, own_heads, 2, 2, weight.shape[1] // HEADS)
        return heads.transpose(3, 2, 0, 1, 4).reshape(2, 2, rows, weight.shape[1] // 4)

    small = [norm1_gain, norm2_gain, kv_gain, router_weight]
    small_sizes = [v.size for v in small]

    def pack(values):
        flat = jnp.concatenate(values, axis=-1)
        pad = -flat.shape[-1] % 2048
        flat = jnp.pad(flat, [(0, 0)] * (flat.ndim - 1) + [(0, pad)])
        return flat.reshape(flat.shape[:-1] + (-1, 128))

    def unpack(packed):
        flat = packed.reshape(packed.shape[:-2] + (-1,))
        starts = [sum(small_sizes[:i]) for i in range(len(small_sizes))]
        return [flat[..., b : b + n] for b, n in zip(starts, small_sizes)]

    small_own = pack([v.reshape(-1) for v in small])
    started = start_gather(
        tokens,
        kva_weight,
        [
            jnp.broadcast_to(small_own, (2, 2) + small_own.shape),
            by_head(kvb_weight),
            by_head(q_weight),
        ],
        o_weight if o_pairs else None,
        lines,
        1,
    )
    group_tokens = started[0].reshape(group_len, width)
    kva_all = started[1].reshape(width, latent_width)
    small_all = unpack(started[2].reshape((device_count,) + small_own.shape))
    kvb_mine = started[3].reshape(KV_RANK, -1)
    q_mine = started[4].reshape(width, -1)
    core_at, x_at = shard_at % 2, shard_at // 2
    if o_pairs:
        o_mine = started[5].reshape(own_heads * VDIM, width)
    else:
        o_mine = gather(o_weight, BOTH).reshape(own_heads, 2, 2, VDIM, width)
        o_mine = o_mine[:, core_at, x_at].reshape(own_heads * VDIM, width)
    norm1_scale, norm2_scale, latent_scale = [v.reshape(-1).astype(F32) for v in small_all[:3]]
    router = small_all[3].reshape(width, all_experts)

    positions = positions_of(seq_ids)
    cosine_table, sine_table = rope_tables(positions, ROPE)
    token_index = jnp.arange(group_len, dtype=jnp.int32)
    allowed = (token_index[None, :] <= token_index[:, None]) & (
        (seq_ids[None, :] == 0) | (seq_ids[None, :] == seq_ids[:, None])
    )
    input_rows = tokens.astype(F32)
    group_rows = group_tokens.astype(F32)
    normed_group, _ = rms_forward(group_rows, norm1_scale)
    hidden_one = normed_group.astype(BF)
    query_raw = mm(hidden_one, q_mine).reshape(group_len, own_heads, NOPE + ROPE)
    q_nope = query_raw[:, :, :NOPE].astype(BF)
    q_rope = rotate(
        query_raw[:, :, NOPE:], cosine_table[:, None, :], sine_table[:, None, :]
    ).astype(BF)
    compressed = mm(hidden_one, kva_all)
    latent_norm, inverse_latent = rms_forward(compressed[:, :KV_RANK], latent_scale)
    latent = latent_norm.astype(BF)
    k_rope = rotate(compressed[:, KV_RANK:], cosine_table, sine_table).astype(BF)
    keyval = mm(latent, kvb_mine).astype(BF).reshape(group_len, own_heads, NOPE + VDIM)
    keys = keyval[:, :, :NOPE]
    values = keyval[:, :, NOPE:]
    scores = jnp.einsum("qhd,khd->hqk", q_nope, keys, preferred_element_type=F32)
    scores = scores + jnp.einsum("qhd,kd->hqk", q_rope, k_rope, preferred_element_type=F32)
    scores = jnp.where(allowed[None], scores * score_scale, NEGATIVE)
    top_score = jnp.max(scores, axis=-1, keepdims=True)
    log_total = top_score + jnp.log(jnp.sum(jnp.exp(scores - top_score), axis=-1, keepdims=True))
    soft_probs = jnp.exp(scores - log_total)
    prob_low = soft_probs.astype(BF)
    attended = (
        jnp.einsum("hqk,khd->qhd", prob_low, values, preferred_element_type=F32)
        .astype(BF)
        .reshape(group_len, own_heads * VDIM)
    )
    projected = sum_group(mm(attended, o_mine).astype(BF), 2)
    mixed = input_rows + projected

    normed_two, inverse_two = rms_forward(mixed, norm2_scale)
    hidden_two = normed_two.astype(BF)
    logits = mm(hidden_two, router)
    choice_hot = (
        expert_ids[:, :, None] == jnp.arange(all_experts, dtype=jnp.int32)[None, None, :]
    ).astype(F32)
    chosen = jnp.sum(choice_hot * logits[:, None, :], axis=-1)
    gate_probs = jax.nn.softmax(chosen, axis=-1)
    kept = kept_pairs(expert_ids, token_rank, choice_hot, capacity)
    gate_table = jnp.sum(choice_hot * (gate_probs * kept)[:, :, None], axis=1)

    shared_width = shared_down.shape[0]
    both_shared = jnp.stack([shared_gate, shared_up]).reshape(
        2, shared_gate.shape[0], device_count, shared_width
    )
    both_shared = lax.all_to_all(
        both_shared.transpose(2, 0, 1, 3), BOTH, split_axis=0, concat_axis=0
    )
    both_shared = both_shared.transpose(1, 0, 2, 3).reshape(2, width, shared_width)
    own_width = expert_gate.shape[2]
    widths = [own_width] * local_experts + [shared_width]
    w_gate = jnp.concatenate([expert_gate[i] for i in range(local_experts)] + [both_shared[0]], 1)
    w_up = jnp.concatenate([expert_up[i] for i in range(local_experts)] + [both_shared[1]], 1)
    w_down = jnp.concatenate([expert_down[i] for i in range(local_experts)] + [shared_down], 0)
    def ffn(rows, cots, table):
        high = table.astype(BF)
        low = (table - high.astype(F32)).astype(BF)
        spare = jnp.zeros((table.shape[0], 128 - 2 * all_experts), BF)
        cots_all = gather(cots, BOTH)
        all_values = gather_all(jnp.concatenate([rows, high, low, spare], axis=1), lines, 3)
        rows_all = all_values[:, :width]
        gates_all = all_values[:, width:].astype(F32)
        gates_mine = lax.dynamic_slice_in_dim(
            gates_all, expert_at * local_experts, local_experts, 1
        ) + lax.dynamic_slice_in_dim(
            gates_all, all_experts + expert_at * local_experts, local_experts, 1
        )
        out_part, back_part, gate_grads, *weight_grads = ffn_chunk(
            rows_all, cots_all, gates_mine, w_gate, w_up, w_down, widths
        )
        gate_grad_table = jnp.where(
            (jnp.arange(128) // local_experts == expert_at)[None, :],
            jnp.tile(gate_grads, (1, 128 // local_experts)),
            0.0,
        ).astype(BF)
        back_sum = sum_all(
            jnp.concatenate([back_part, gate_grad_table], axis=1), lines, rows.shape[0], 4
        )
        return scatter_sum(out_part, BOTH), back_sum, weight_grads

    rounds = max(1, tok_rows * device_count // 4096)
    if rounds == 1:
        out_sum, back_sum, weight_grads = ffn(hidden_two, cotangent, gate_table)
    else:

        def one_round(total, part):
            out_rows, back_rows, grads = ffn(*part)
            return [t + g for t, g in zip(total, grads)], (out_rows, back_rows)

        in_rounds = lambda value: value.reshape((rounds, -1) + value.shape[1:])
        zeros = [jnp.zeros(w.shape, F32) for w in (w_gate, w_up, w_down)]
        weight_grads, (out_sum, back_sum) = lax.scan(
            one_round, zeros, (in_rounds(hidden_two), in_rounds(cotangent), in_rounds(gate_table))
        )
        out_sum = out_sum.reshape((tok_rows,) + out_sum.shape[2:])
        back_sum = back_sum.reshape((tok_rows,) + back_sum.shape[2:])
    out_sum, back_sum = out_sum.astype(F32), back_sum.astype(F32)
    w_gate_grad, w_up_grad, w_down_grad = weight_grads
    output = (mixed + out_sum).astype(BF)

    def split_experts(grad, axis):
        pieces = [
            lax.slice_in_dim(grad, i * own_width, (i + 1) * own_width, axis=axis)
            for i in range(local_experts)
        ]
        shared = lax.slice_in_dim(grad, local_experts * own_width, None, axis=axis)
        return jnp.stack(pieces), shared

    egate_grad, sgate_mine = split_experts(w_gate_grad, 1)
    eup_grad, sup_mine = split_experts(w_up_grad, 1)
    edown_grad, sdown_grad = split_experts(w_down_grad, 0)
    shared_grads = (
        jnp.stack([sgate_mine, sup_mine])
        .reshape(2, device_count, width // device_count, shared_width)
        .transpose(1, 0, 2, 3)
    )
    shared_grads = lax.all_to_all(shared_grads.astype(BF), BOTH, split_axis=0, concat_axis=0)
    shared_grads = shared_grads.astype(F32).transpose(1, 2, 0, 3).reshape(
        2, width // device_count, device_count * shared_width
    )

    upstream = cotangent.astype(F32)
    gate_grad = jnp.sum(
        choice_hot * back_sum[:, None, width : width + all_experts], axis=-1
    ) * kept
    chosen_grad = gate_probs * (gate_grad - jnp.sum(gate_probs * gate_grad, axis=-1, keepdims=True))
    logit_grad = jnp.sum(choice_hot * chosen_grad[:, :, None], axis=1).astype(BF)
    router_part = mm_tn(hidden_two, logit_grad)
    hidden_two_grad = back_sum[:, :width] + mm_nt(logit_grad, router)
    mixed_norm_grad, norm2_part = rms_backward(mixed, inverse_two, norm2_scale, hidden_two_grad)
    mixed_grad = upstream + mixed_norm_grad

    mixed_grad_group = gather_group(mixed_grad.astype(BF), 5)
    o_part = mm_tn(attended, mixed_grad_group)
    attended_grad = (
        mm_nt(mixed_grad_group, o_mine).astype(BF).reshape(group_len, own_heads, VDIM)
    )
    prob_grad = jnp.einsum("qhd,khd->hqk", attended_grad, values, preferred_element_type=F32)
    values_grad = jnp.einsum("hqk,qhd->khd", prob_low, attended_grad, preferred_element_type=F32)
    score_grad = (
        soft_probs * (prob_grad - jnp.sum(soft_probs * prob_grad, axis=-1, keepdims=True))
    ).astype(BF)
    q_nope_grad = (
        jnp.einsum("hqk,khd->qhd", score_grad, keys, preferred_element_type=F32) * score_scale
    )
    q_rope_grad = (
        jnp.einsum("hqk,kd->qhd", score_grad, k_rope, preferred_element_type=F32) * score_scale
    )
    keys_grad = (
        jnp.einsum("hqk,qhd->khd", score_grad, q_nope, preferred_element_type=F32) * score_scale
    )
    rope_grad = (
        jnp.einsum("hqk,qhd->kd", score_grad, q_rope, preferred_element_type=F32) * score_scale
    )
    keyval_grad = (
        jnp.concatenate([keys_grad, values_grad], axis=-1)
        .reshape(group_len, own_heads * (NOPE + VDIM))
        .astype(BF)
    )
    kvb_part = mm_tn(latent, keyval_grad)
    latent_part = jnp.concatenate([mm_nt(keyval_grad, kvb_mine), rope_grad], axis=1).astype(BF)
    latent_sum = sum_group(
        jnp.pad(latent_part, ((0, 0), (0, -latent_part.shape[1] % 128))), 6
    )[:, :latent_width]
    own_start = shard_at * tok_rows
    own_rows = lambda value: lax.dynamic_slice_in_dim(value, own_start, tok_rows)
    latent_raw_grad, kv_gain_part = rms_backward(
        own_rows(compressed[:, :KV_RANK]),
        own_rows(inverse_latent),
        latent_scale,
        latent_sum[:, :KV_RANK],
    )
    compressed_grad = jnp.concatenate(
        [
            latent_raw_grad,
            rotate(latent_sum[:, KV_RANK:], own_rows(cosine_table), -own_rows(sine_table)),
        ],
        axis=1,
    ).astype(BF)
    compressed_grad_group = gather_group(
        jnp.pad(compressed_grad, ((0, 0), (0, -latent_width % 128))), 7
    )[:, :latent_width]
    query_grad = jnp.concatenate(
        [q_nope_grad, rotate(q_rope_grad, cosine_table[:, None, :], -sine_table[:, None, :])],
        axis=-1,
    )
    query_grad = query_grad.reshape(group_len, own_heads * (NOPE + ROPE)).astype(BF)
    q_part = mm_tn(hidden_one, query_grad)
    own_columns = lax.dynamic_index_in_dim(
        hidden_one.reshape(group_len, expert_count, shard_count, width // device_count),
        shard_at,
        2,
        keepdims=False,
    ).reshape(group_len, width // shard_count)
    kva_part = mm_tn(own_columns, compressed_grad_group)
    hidden_one_grad = sum_group(mm_nt(query_grad, q_mine).astype(BF), 8) + mm_nt(
        compressed_grad, kva_all
    )
    _, inverse_one = rms_forward(input_rows, norm1_scale)
    input_norm_grad, norm1_part = rms_backward(
        input_rows, inverse_one, norm1_scale, hidden_one_grad
    )
    tokens_grad = mixed_grad + input_norm_grad

    def from_heads(parts):
        rows = parts.shape[2]
        heads = parts.reshape(2, 2, rows, own_heads, -1).transpose(2, 3, 1, 0, 4)
        return heads.reshape(rows, -1).astype(F32)

    line_shape = (lines, 2)
    small_parts = pack(
        [v.reshape(device_count, -1) for v in (norm1_part, norm2_part, kv_gain_part, router_part)]
    )
    parts = [
        kvb_part.astype(BF).reshape(line_shape + (2, 2, kvb_weight.shape[0], -1)),
        kva_part.astype(BF).reshape(line_shape + (width // device_count, latent_width)),
        q_part.astype(BF).reshape(line_shape + (2, 2, q_weight.shape[0], q_mine.shape[1])),
        small_parts.reshape(line_shape + (2, 2) + small_parts.shape[1:]),
    ]
    o_part = o_part.astype(BF).reshape(own_heads, VDIM, width)
    if o_pairs:
        o_sum = o_part.reshape(own_heads, 2, o_rows, width)
    else:
        o_sum = None
        o_wide = jnp.zeros((own_heads, 2, 2, VDIM, width), BF).at[:, core_at, x_at].set(o_part)
        o_grad = scatter_sum(o_wide.reshape(HEADS * VDIM, width), BOTH).astype(F32)
    summed = sum_grads(parts, (True, False, True, True), o_sum, lines, 9)
    kvb_grad = from_heads(summed[0])
    kva_grad = summed[1].astype(F32)
    q_grad = from_heads(summed[2])
    norm1_grad, norm2_grad, kv_gain_grad, router_grad = unpack(jnp.sum(summed[3], axis=(0, 1)))
    router_grad = router_grad.reshape(router_weight.shape)
    if o_pairs:
        o_grad = summed[4].astype(F32)
    return (
        output,
        tokens_grad,
        norm1_grad,
        q_grad,
        kva_grad,
        kv_gain_grad,
        kvb_grad,
        o_grad,
        norm2_grad,
        router_grad,
        shared_grads[0],
        shared_grads[1],
        sdown_grad,
        egate_grad,
        eup_grad,
        edown_grad,
    )


def solution(mesh):
    rows = P(BOTH, None)
    flat = P(BOTH)
    columns = P("expert", None, "shard")
    depth = P("expert", "shard", None)
    return jax.shard_map(
        on_device,
        mesh=mesh,
        in_specs=(
            rows,
            rows,
            flat,
            rows,
            rows,
            flat,
            rows,
            rows,
            flat,
            rows,
            rows,
            rows,
            rows,
            columns,
            columns,
            depth,
            rows,
            flat,
            P("expert"),
        ),
        out_specs=(
            rows,
            rows,
            flat,
            rows,
            rows,
            flat,
            rows,
            rows,
            flat,
            rows,
            rows,
            rows,
            rows,
            columns,
            columns,
            depth,
        ),
        check_vma=False,
    )
```

```python
import functools

import jax
import jax.numpy as jnp
from jax import lax
from jax.experimental import pallas as pl
from jax.experimental.pallas import tpu as pltpu
from jax.sharding import PartitionSpec as P

HEADS = 16
NOPE = 128
ROPE = 64
VDIM = 128
KV_RANK = 512
CONTS = 2


EPSILON = 1e-06
THETA = 10000.0
NEGATIVE = -1e30
BOTH = ("expert", "shard")
BF = jnp.bfloat16
F32 = jnp.float32


def rms_forward(values, gain_row):
    inverse = lax.rsqrt(jnp.mean(values * values, axis=-1, keepdims=True) + EPSILON)
    return (values * inverse * gain_row, inverse)


def rms_backward(values, inverse, gain_row, upstream):
    normed = values * inverse
    scaled = upstream * gain_row
    value_grad = inverse * (scaled - normed * jnp.mean(scaled * normed, axis=-1, keepdims=True))
    return (value_grad, jnp.sum(upstream * normed, axis=0))


def rope_tables(positions, width):
    half_width = width // 2
    frequency = THETA ** (-2.0 * jnp.arange(half_width, dtype=jnp.float32) / width)
    angles = positions.astype(jnp.float32)[:, None] * frequency[None, :]
    return (jnp.cos(angles), jnp.sin(angles))


def rotate(values, cosine_table, sine_table):
    half_width = values.shape[-1] // 2
    first_half = values[..., :half_width]
    second = values[..., half_width:]
    return jnp.concatenate(
        [
            first_half * cosine_table - second * sine_table,
            second * cosine_table + first_half * sine_table,
        ],
        axis=-1,
    )


def positions_of(group_ids):
    length = group_ids.shape[0]
    token_index = jnp.arange(length, dtype=jnp.int32)
    labels = jnp.arange(CONTS + 1, dtype=jnp.int32)
    member = (group_ids[:, None] == labels[None, :]).astype(jnp.int32)
    counts = jnp.sum(member, axis=0)
    starts = jnp.cumsum(counts) - counts
    start_of = jnp.sum(member * starts[None, :], axis=1)
    return token_index - start_of + jnp.where(group_ids > 0, counts[0], 0)


def kept_pairs(choice_ids, rank_row, choice_hot, capacity):
    row_count, top_count, expert_total = choice_hot.shape
    per_k = jnp.sum(choice_hot, axis=0)
    before_k = jnp.cumsum(per_k, axis=0) - per_k
    lower = (rank_row[None, :] < rank_row[:, None]).astype(F32)
    same_k = jnp.dot(
        lower.astype(BF),
        choice_hot.reshape(row_count, top_count * expert_total).astype(BF),
        preferred_element_type=F32,
    ).reshape(row_count, top_count, expert_total)
    place = jnp.sum((same_k + before_k[None]) * choice_hot, axis=-1)
    return (place < capacity).astype(F32)


def mm(a, b):
    return jnp.dot(a, b, preferred_element_type=F32)


def mm_nt(a, b):
    return lax.dot_general(a, b, (((1,), (1,)), ((), ())), preferred_element_type=F32)


def mm_tn(a, b):
    return lax.dot_general(a, b, (((0,), (0,)), ((), ())), preferred_element_type=F32)


def gather(value, axes):
    return lax.all_gather(value, axes, axis=0, tiled=True)


def scatter_sum(value, axes):
    return lax.psum_scatter(value, axes, scatter_dimension=0, tiled=True)


HBM = pl.BlockSpec(memory_space=pl.ANY)
VMEM = pl.BlockSpec(memory_space=pltpu.VMEM)


class Place:
    def __init__(self):
        e, s = lax.axis_index("expert"), lax.axis_index("shard")
        self.z, self.y, self.x, self.c = e // 2, e % 2, s // 2, s % 2

    def at(self, z=None, y=None, x=None, c=None):
        z = self.z if z is None else z
        y = self.y if y is None else y
        x = self.x if x is None else x
        c = self.c if c is None else c
        return {"expert": 2 * z + y, "shard": 2 * x + c}


def greet(partners):
    barrier = pltpu.get_barrier_semaphore()
    for partner in partners:
        pl.semaphore_signal(
            barrier, inc=1, device_id=partner, device_id_type=pl.DeviceIdType.MESH
        )
    pl.semaphore_wait(barrier, len(partners))


def remote(src, dst, send, recv, where):
    return pltpu.make_async_remote_copy(
        src_ref=src,
        dst_ref=dst,
        send_sem=send,
        recv_sem=recv,
        device_id=where,
        device_id_type=pl.DeviceIdType.MESH,
    )


def gather_group_kernel(cuts, spans, *refs):
    refs = list(refs)
    take = lambda n: [refs.pop(0) for _ in range(n)]
    (src,) = take(1)
    work = take(4) if spans else None
    (dst,) = take(1)
    made = take(3) if spans else None
    own_sem, send, recv = take(3)
    me = Place()
    x, c = me.x, me.c
    to_x, to_c = me.at(x=1 - x), me.at(c=1 - c)
    greet([to_x, to_c])
    cut = src.shape[0] // cuts
    span = lambda k: pl.ds(k * cut, cut)
    own = pltpu.make_async_copy(src, dst.at[x, c], own_sem)
    own.start()
    over_x = [
        remote(src.at[span(k)], dst.at[x, c, span(k)], send.at[0, k], recv.at[0, k], to_x)
        for k in range(cuts)
    ]
    for copy in over_x:
        copy.start()
    over_c = remote(src, dst.at[x, c], send.at[1, 0], recv.at[1, 0], to_c)
    over_c.start()
    if spans:
        turns, begin_work, work_turn = grad_worker(work, made, refs[:3], refs[3], spans)
        begin_work()

        @pl.loop(0, turns)
        def _(n):
            work_turn(n)

    relays = []
    for k in range(cuts):
        far = dst.at[1 - x, c, span(k)]
        remote(far, far, send.at[0, k], recv.at[0, k], to_x).wait_recv()
        relays.append(remote(far, far, send.at[2, k], recv.at[2, k], to_c))
        relays[-1].start()
    far = dst.at[x, 1 - c]
    remote(far, far, send.at[1, 0], recv.at[1, 0], to_c).wait_recv()
    for k in range(cuts):
        far = dst.at[1 - x, 1 - c, span(k)]
        remote(far, far, send.at[2, k], recv.at[2, k], to_c).wait_recv()
    own.wait()
    for copy in over_x + [over_c] + relays:
        copy.wait_send()


def gather_group(value, ident, work=None, spans=None, lines=None, cuts=4):
    rows, width = value.shape
    dma = pltpu.SemaphoreType.DMA
    inputs, in_specs = [value], [HBM]
    outs = [jax.ShapeDtypeStruct((2, 2, rows, width), value.dtype)]
    scratch = [dma, dma((3, cuts)), dma((3, cuts))]
    if work:
        inputs += work
        in_specs += [HBM] * 4
        shapes, buffers = work_shapes(work, spans, lines)
        outs += shapes
        scratch += buffers
    out, *made = pl.pallas_call(
        functools.partial(gather_group_kernel, cuts, spans if work else None),
        out_shape=outs,
        in_specs=in_specs,
        out_specs=[HBM] + [VMEM] * (len(outs) - 1),
        scratch_shapes=scratch,
        compiler_params=pltpu.CompilerParams(
            collective_id=ident, has_side_effects=True, vmem_limit_bytes=40 << 20
        ),
    )(*inputs)
    return [out.reshape(4 * rows, width)] + made


def sum_group_kernel(cuts, part, out, cbuf, xbuf, xsum, cs, cr, xs, xr):
    me = Place()
    x, c = me.x, me.c
    rows, width = out.shape
    cut = rows // cuts
    to_x, to_c = me.at(x=1 - x), me.at(c=1 - c)
    greet([to_x, to_c])
    span = lambda k: pl.ds(k * cut, cut)
    core = lambda k, far: remote(
        part.at[1 - x if far else x, 1 - c, span(k)],
        cbuf.at[far, span(k)],
        cs.at[k, far],
        cr.at[k, far],
        to_c,
    )
    over = lambda k: remote(xsum.at[span(k)], xbuf.at[span(k)], xs.at[k], xr.at[k], to_x)
    for k in range(cuts):
        core(k, 1).start()
    for k in range(cuts):
        core(k, 0).start()

    def add(k, target, one, two):
        @pl.loop(0, cut // 16)
        def _(i):
            at = pl.ds(pl.multiple_of(k * cut + i * 16, 16), 16)
            target[at] = (one[at].astype(F32) + two[at].astype(F32)).astype(target.dtype)

    for k in range(cuts):
        core(k, 1).wait_recv()
        add(k, xsum, part.at[1 - x, c], cbuf.at[1])
        over(k).start()
    for k in range(cuts):
        core(k, 0).wait_recv()
        add(k, out, part.at[x, c], cbuf.at[0])
    for k in range(cuts):
        over(k).wait_recv()
        add(k, out, out, xbuf)
    for k in range(cuts):
        core(k, 1).wait_send()
        core(k, 0).wait_send()
        over(k).wait_send()


def sum_group(part, ident, cuts=4):
    rows, width = part.shape[0] // 4, part.shape[1]
    dma = pltpu.SemaphoreType.DMA
    buf = lambda *lead: pltpu.VMEM(lead + (rows, width), part.dtype)
    return pl.pallas_call(
        functools.partial(sum_group_kernel, cuts),
        out_shape=jax.ShapeDtypeStruct((rows, width), F32),
        in_specs=[VMEM],
        out_specs=VMEM,
        scratch_shapes=[
            buf(2), buf(), buf(),
            dma((cuts, 2)), dma((cuts, 2)), dma((cuts,)), dma((cuts,)),
        ],
        compiler_params=pltpu.CompilerParams(
            collective_id=ident, has_side_effects=True, vmem_limit_bytes=32 << 20
        ),
    )(part.reshape(2, 2, rows, width))


def add_blocks(target, one, two):
    if len(target.shape) > 2:
        for i in range(target.shape[0]):
            add_blocks(target.at[i], one.at[i], two.at[i])
        return
    rows = target.shape[0]
    step = 16 if rows % 16 == 0 else rows

    @pl.loop(0, rows // step)
    def _(i):
        at = pl.ds(pl.multiple_of(i * step, step), step)
        target[at] = (one[at].astype(F32) + two[at].astype(F32)).astype(target.dtype)


class Copies:
    def __init__(self):
        self.started = []

    def go(self, copy):
        copy.start()
        self.started.append(copy)

    def finish(self):
        for copy in self.started:
            copy.wait_send()


def start_kernel(lines, counts, with_o, *refs):
    jobs, planes = 3, len(counts)
    refs = list(refs)
    take = lambda n: [refs.pop(0) for _ in range(n)]
    (tok,) = take(1)
    plane_src, sources = take(planes), take(jobs)
    o_src = take(1)[0] if with_o else None
    (tok_dst,) = take(1)
    plane_dst, dests = take(planes), take(jobs)
    o_dst = take(1)[0] if with_o else None
    own_sem, gs, gr, zs, zr, ys, yr, ts, tr = take(9)
    plane_sems = [take(6) for _ in range(planes)]
    if with_o:
        o_own, ocs, ocr, ozs, ozr, oys, oyr = take(7)
    me = Place()
    z, y, x, c = me.z, me.y, me.x, me.c
    others = [lax.rem(z + 1 + j, lines) for j in range(lines - 1)]
    places = list(enumerate(others)) + [(lines - 1, z)]
    near = [(x, 1 - c), (1 - x, c), (1 - x, 1 - c)]
    to_near = [me.at(x=xx, c=cc) for xx, cc in near]
    to_y, to_x, to_c = me.at(y=1 - y), to_near[1], to_near[0]
    greet([me.at(z=o) for o in others] + [to_y] + to_near)
    copies = Copies()
    go = copies.go

    def span(i, k):
        rows = plane_src[i].shape[0] // counts[i]
        return pl.ds(k * rows, rows)

    def plane_z_start(i, k):
        zs_, zr_, ys_, yr_ = plane_sems[i][:4]
        src, dst = plane_src[i].at[span(i, k)], plane_dst[i].at[z, y, x, c, span(i, k)]
        for j, o in enumerate(others):
            go(remote(src, dst, zs_.at[k, j], zr_.at[k, z], me.at(z=o)))
        go(remote(src, dst, ys_.at[k, lines - 1], yr_.at[k, z], to_y))

    def plane_z_land(i, k):
        zs_, zr_, ys_, yr_ = plane_sems[i][:4]
        for j, o in reversed(places[:-1]):
            block = plane_dst[i].at[o, y, x, c, span(i, k)]
            remote(block, block, zs_.at[k, j], zr_.at[k, o], me.at(z=o)).wait_recv()
            go(remote(block, block, ys_.at[k, j], yr_.at[k, o], to_y))

    def plane_y_land(i, k):
        ys_, yr_, ps, pr = plane_sems[i][2:]
        for j, o in places:
            block = plane_dst[i].at[o, 1 - y, x, c, span(i, k)]
            remote(block, block, ys_.at[k, j], yr_.at[k, o], to_y).wait_recv()
        block = plane_dst[i].at[:, :, x, c, span(i, k)]
        go(remote(block, block, ps.at[k, 0], pr.at[k, 0], to_x))
        go(remote(block, block, ps.at[k, 1], pr.at[k, 1], to_c))

    def plane_x_land(i, k):
        ps, pr = plane_sems[i][4:]
        block = plane_dst[i].at[:, :, 1 - x, c, span(i, k)]
        remote(block, block, ps.at[k, 0], pr.at[k, 0], to_x).wait_recv()
        go(remote(block, block, ps.at[k, 2], pr.at[k, 2], to_c))

    def plane_c_land(i, k):
        ps, pr = plane_sems[i][4:]
        for slot, xx in ((1, x), (2, 1 - x)):
            block = plane_dst[i].at[:, :, xx, 1 - c, span(i, k)]
            remote(block, block, ps.at[k, slot], pr.at[k, slot], to_c).wait_recv()

    locals_ = [
        pltpu.make_async_copy(src, dst.at[z, y, x, c], own_sem.at[i])
        for i, (src, dst) in enumerate(
            zip([v.at[x, c] for v in sources] + plane_src, dests + plane_dst)
        )
    ]
    locals_.append(pltpu.make_async_copy(tok, tok_dst.at[x, c], own_sem.at[jobs + planes]))
    for copy in locals_:
        copy.start()

    for i in range(jobs):
        for p in range(3):
            go(
                remote(
                    sources[i].at[near[p][0], near[p][1]],
                    dests[i].at[z, y, x, c],
                    gs.at[i, p],
                    gr.at[i, p],
                    to_near[p],
                )
            )
    last = planes - 1
    plane_z_start(last, 0)
    if counts[last] > 1:
        plane_z_start(last, 1)
    if with_o:
        o_core = remote(o_src, o_dst.at[z, c], ocs, ocr, to_c)
        o_local = pltpu.make_async_copy(o_src, o_dst.at[z, c], o_own)
        holder = c == y

        @pl.when(jnp.logical_not(holder))
        def _():
            o_core.start()

        @pl.when(holder)
        def _():
            o_local.start()

    go(remote(tok, tok_dst.at[x, c], ts.at[1], tr.at[1], to_x))
    go(remote(tok, tok_dst.at[x, c], ts.at[0], tr.at[0], to_c))
    line_y = lambda i, j, o: remote(
        dests[i].at[o, y], dests[i].at[o, y], ys.at[i, j], yr.at[i, o], to_y
    )
    line_z = lambda i, j, o: remote(
        dests[i].at[z, y], dests[i].at[z, y], zs.at[i, j], zr.at[i, z], me.at(z=o)
    )

    def job_start(i):
        locals_[i].wait()
        for p in range(3):
            xx, cc = near[p]
            block = dests[i].at[z, y, xx, cc]
            remote(block, block, gs.at[i, p], gr.at[i, p], to_near[p]).wait_recv()
        for j, o in enumerate(others):
            go(line_z(i, j, o))
        go(line_y(i, lines - 1, z))

    job_start(0)
    job_start(1)
    plane_z_land(last, 0)
    for k in range(1, counts[last]):
        if k + 1 < counts[last]:
            plane_z_start(last, k + 1)
        plane_z_land(last, k)
        if k == 1:
            job_start(2)
        locals_[jobs + last].wait() if k == 1 else None
        plane_y_land(last, k - 1)
    if counts[last] == 1:
        job_start(2)
        locals_[jobs + last].wait()
    if with_o:
        o_z = lambda j, o: remote(o_dst.at[z], o_dst.at[z], ozs.at[j], ozr.at[z], me.at(z=o))
        o_y = lambda j, o: remote(o_dst.at[o], o_dst.at[o], oys.at[j], oyr.at[o], to_y)

        @pl.when(holder)
        def _():
            o_local.wait()
            block = o_dst.at[z, 1 - c]
            remote(block, block, ocs, ocr, to_c).wait_recv()
            for j, o in enumerate(others):
                o_z(j, o).start()
            o_y(lines - 1, z).start()

    for i in range(last):
        for k in range(counts[i]):
            plane_z_start(i, k)
    plane_y_land(last, counts[last] - 1)
    block = tok_dst.at[1 - x, c]
    remote(block, block, ts.at[1], tr.at[1], to_x).wait_recv()
    go(remote(block, block, ts.at[2], tr.at[2], to_c))
    for j, o in reversed(places[:-1]):
        for i in range(jobs):
            block = dests[i].at[o, y]
            remote(block, block, zs.at[i, j], zr.at[i, o], me.at(z=o)).wait_recv()
            go(line_y(i, j, o))
        if with_o:

            @pl.when(holder)
            def _(j=j, o=o):
                block = o_dst.at[o]
                remote(block, block, ozs.at[j], ozr.at[o], me.at(z=o)).wait_recv()
                o_y(j, o).start()

    for i in range(last):
        for k in range(counts[i]):
            plane_z_land(i, k)
    for k in range(counts[last]):
        plane_x_land(last, k)
    for i in range(last):
        locals_[jobs + i].wait()
        for k in range(counts[i]):
            plane_y_land(i, k)
            plane_x_land(i, k)
    for slot, xx in ((0, x), (2, 1 - x)):
        block = tok_dst.at[xx, 1 - c]
        remote(block, block, ts.at[slot], tr.at[slot], to_c).wait_recv()
    locals_[jobs + planes].wait()
    for j, o in places:
        for i in range(jobs):
            block = dests[i].at[o, 1 - y]
            remote(block, block, ys.at[i, j], yr.at[i, o], to_y).wait_recv()
    if with_o:

        @pl.when(jnp.logical_not(holder))
        def _():
            for j, o in places:
                remote(o_dst.at[o], o_dst.at[o], oys.at[j], oyr.at[o], to_y).wait_recv()
            o_core.wait_send()

        @pl.when(holder)
        def _():
            for j, o in enumerate(others):
                o_z(j, o).wait_send()
            for j, o in places:
                o_y(j, o).wait_send()

    for i in range(planes):
        for k in range(counts[i]):
            plane_c_land(i, k)
    copies.finish()


def start_gather(tokens, planes, counts, column_parts, o_rows, lines, ident):
    jobs = len(column_parts)
    with_o = o_rows is not None
    inputs = [tokens] + planes + column_parts + ([o_rows] if with_o else [])
    shape = lambda lead, v: jax.ShapeDtypeStruct(lead + v.shape, v.dtype)
    outs = [shape((2, 2), tokens)] + [shape((lines, 2, 2, 2), v) for v in planes]
    outs += [jax.ShapeDtypeStruct((lines, 2) + v.shape, v.dtype) for v in column_parts]
    if with_o:
        outs.append(shape((lines, 2), o_rows))
    dma = pltpu.SemaphoreType.DMA
    scratch = [
        dma((jobs + len(planes) + 1,)), dma((jobs, 3)), dma((jobs, 3)),
        dma((jobs, lines)), dma((jobs, lines)), dma((jobs, lines)), dma((jobs, lines)),
        dma((3,)), dma((3,)),
    ]
    for n in counts:
        scratch += [dma((n, lines))] * 4 + [dma((n, 3))] * 2
    if with_o:
        scratch += [dma, dma, dma, dma((lines,)), dma((lines,)), dma((lines,)), dma((lines,))]
    return pl.pallas_call(
        functools.partial(start_kernel, lines, tuple(counts), with_o),
        out_shape=outs,
        in_specs=[HBM] * len(inputs),
        out_specs=[HBM] * len(outs),
        scratch_shapes=scratch,
        compiler_params=pltpu.CompilerParams(collective_id=ident, has_side_effects=True),
    )(*inputs)


def grad_worker(work, made, slots, ins, spans):
    values, cots, in_d, hid = work
    rows_in, cots_in, left_in = slots
    depth, width = rows_in.shape[1:]
    early = cots.shape[1]
    inner = hid.shape[1]
    turns = cots.shape[0] // depth
    first, units = spans[0][0], left_in.shape[3]

    def loads(n):
        at = pl.ds(pl.multiple_of(n * depth, depth), depth)
        slot = lax.rem(n, 2)
        pairs = (
            (values.at[at, pl.ds(0, width)], rows_in.at[slot]),
            (cots.at[at], cots_in.at[slot, :, pl.ds(0, early)]),
            (
                values.at[at, pl.ds(width + 128, width - early)],
                cots_in.at[slot, :, pl.ds(early, width - early)],
            ),
            (in_d.at[at, pl.ds(first, units)], left_in.at[slot, 0]),
            (in_d.at[at, pl.ds(inner + first, units)], left_in.at[slot, 1]),
            (hid.at[at, pl.ds(first, units)], left_in.at[slot, 2]),
        )
        return [
            pltpu.make_async_copy(src, dst, ins.at[slot, i]) for i, (src, dst) in enumerate(pairs)
        ]

    def begin():
        for copy in loads(0):
            copy.start()
        for ref in made:
            for i in range(ref.shape[0]):
                ref[i] = jnp.zeros(ref.shape[1:], F32)

    def turn(n):
        slot = lax.rem(n, 2)

        @pl.when(n + 1 < turns)
        def _():
            for copy in loads(n + 1):
                copy.start()

        for copy in loads(n):
            copy.wait()

        @pl.loop(0, width // 512)
        def _(m):
            at = pl.ds(pl.multiple_of(m * 512, 512), 512)
            for which, right in enumerate((rows_in, rows_in, cots_in)):
                ref = made[which]
                part = lax.dot_general(
                    left_in[slot, which],
                    right[slot, :, at],
                    (((0,), (0,)), ((), ())),
                    preferred_element_type=F32,
                )
                for i, (begin, _, kept) in enumerate(spans):
                    begin = begin - first
                    ref[i, :, at] = ref[i, :, at] + part[begin : begin + kept]

    return turns, begin, turn


def work_shapes(work, spans, lines):
    count, width = work[1].shape[0], work[0].shape[1] - 128
    width = (width + work[1].shape[1]) // 2
    units = sum(size for _, size, _ in spans)
    depth = min(512, count // lines)
    shapes = [jax.ShapeDtypeStruct((len(spans), spans[0][2], width), F32)] * 3
    rows = pltpu.VMEM((2, depth, width), BF)
    buffers = [rows, rows, pltpu.VMEM((2, 3, depth, units), BF), pltpu.SemaphoreType.DMA((2, 6))]
    return shapes, buffers


def grads_kernel(lines, kinds, with_o, spans, *refs):
    jobs = len(kinds)
    take = lambda n: [refs.pop(0) for _ in range(n)]
    refs = list(refs)
    parts = take(jobs)
    o_part = take(1)[0] if with_o else None
    work = take(4) if spans else None
    outs = take(jobs)
    o_out = take(1)[0] if with_o else None
    made = take(3) if spans else None
    ybufs, zbufs, tots = take(jobs), take(jobs), take(jobs)
    if with_o:
        o_ybuf, o_zbuf, o_tot = take(3)
    ys, yr, zs, zr, gs, gr = take(6)
    if with_o:
        oys, oyr, ozs, ozr, ocs, ocr = take(6)
    if spans:
        rows_in, cots_in, left_in, ins = take(4)
    accs, o_acc = ybufs, (o_ybuf if with_o else None)
    me = Place()
    z, y, x, c = me.z, me.y, me.x, me.c
    others = [lax.rem(z + 1 + j, lines) for j in range(lines - 1)]
    near = [(x, 1 - c), (1 - x, c), (1 - x, 1 - c)]
    to_near = [me.at(x=xx, c=cc) for xx, cc in near]
    to_y, to_c = me.at(y=1 - y), to_near[0]
    greet([me.at(z=o) for o in others] + [to_y] + to_near)
    copies = Copies()
    go = copies.go
    over_y = lambda i, j, o: remote(
        parts[i].at[o, 1 - y], ybufs[i].at[o], ys.at[i, j], yr.at[i, o], to_y
    )
    over_z = lambda i, j, o: remote(
        accs[i].at[o], zbufs[i].at[z], zs.at[i, j], zr.at[i, z], me.at(z=o)
    )
    places = list(enumerate(others)) + [(lines - 1, z)]
    if with_o:
        holder = c == y
        o_over_y = lambda j, o: remote(o_part.at[o], o_ybuf.at[o], oys.at[j], oyr.at[o], to_y)
        o_over_z = lambda j, o: remote(
            o_acc.at[o], o_zbuf.at[z], ozs.at[j], ozr.at[z], me.at(z=o)
        )
    for j, o in places:
        for i in range(jobs):
            go(over_y(i, j, o))
        if with_o:

            @pl.when(jnp.logical_not(holder))
            def _(j=j, o=o):
                o_over_y(j, o).start()

    if spans:
        turns, begin_work, work_turn = grad_worker(work, made, (rows_in, cots_in, left_in), ins, spans)
        begin_work()

    @pl.loop(0, lines)
    def _(j):
        if spans:
            per_line = turns // lines

            @pl.loop(0, per_line)
            def _(n):
                work_turn(j * per_line + n)

        o = lax.rem(z + 1 + j, lines)
        for i in range(jobs):
            remote(ybufs[i].at[o], ybufs[i].at[o], ys.at[i, j], yr.at[i, o], to_y).wait_recv()
            add_blocks(accs[i].at[o], parts[i].at[o, y], ybufs[i].at[o])

            @pl.when(j < lines - 1)
            def _(i=i):
                over_z(i, j, o).start()

        if with_o:

            @pl.when(holder)
            def _():
                remote(o_ybuf.at[o], o_ybuf.at[o], oys.at[j], oyr.at[o], to_y).wait_recv()
                add_blocks(o_acc.at[o], o_part.at[o], o_ybuf.at[o])

                @pl.when(j < lines - 1)
                def _():
                    o_over_z(j, o).start()

    def line_sum(target, acc, zbuf):
        if len(target.shape) > 2:
            for k in range(target.shape[0]):
                line_sum(target.at[k], acc.at[:, k], zbuf.at[:, k])
            return
        rows = target.shape[0]
        step = 16 if rows % 16 == 0 else rows

        @pl.loop(0, rows // step)
        def _(i):
            at = pl.ds(pl.multiple_of(i * step, step), step)
            value = acc[z, at].astype(F32)
            for o in others:
                value = value + zbuf[o, at].astype(F32)
            target[at] = value.astype(target.dtype)

    near_copy = lambda i, p: remote(
        tots[i].at[near[p][0], near[p][1]], outs[i].at[x, c], gs.at[i, p], gr.at[i, p], to_near[p]
    )
    for i in range(jobs):
        for j, o in places[:-1]:
            block = zbufs[i].at[o]
            remote(block, block, zs.at[i, j], zr.at[i, o], me.at(z=o)).wait_recv()
        if kinds[i]:
            for xx in range(2):
                for cc in range(2):
                    line_sum(tots[i].at[xx, cc], accs[i].at[:, xx, cc], zbufs[i].at[:, xx, cc])
            for p in range(3):
                go(near_copy(i, p))
            rows = tots[i].shape[2]
            outs[i][x, c] = tots[i][x, c]
        else:
            line_sum(outs[i], accs[i], zbufs[i])
    if with_o:
        o_core = remote(o_tot.at[1 - c], o_out, ocs, ocr, to_c)

        @pl.when(holder)
        def _():
            for j, o in places[:-1]:
                block = o_zbuf.at[o]
                remote(block, block, ozs.at[j], ozr.at[o], me.at(z=o)).wait_recv()
            line_sum(o_tot.at[1 - c], o_acc.at[:, 1 - c], o_zbuf.at[:, 1 - c])
            o_core.start()
            line_sum(o_out, o_acc.at[:, c], o_zbuf.at[:, c])
            for j, o in places[:-1]:
                o_over_z(j, o).wait_send()
            o_core.wait_send()

        @pl.when(jnp.logical_not(holder))
        def _():
            for j, o in places:
                o_over_y(j, o).wait_send()
            o_core.wait_recv()

    for i in range(jobs):
        if kinds[i]:
            for p in range(3):
                block = outs[i].at[near[p][0], near[p][1]]
                remote(block, block, gs.at[i, p], gr.at[i, p], to_near[p]).wait_recv()
        for j, o in places[:-1]:
            over_z(i, j, o).wait_send()
    copies.finish()


def sum_grads(parts, kinds, o_part, lines, ident, work=None, spans=None):
    jobs = len(parts)
    with_o = o_part is not None
    inputs = list(parts) + ([o_part] if with_o else [])
    outs = [jax.ShapeDtypeStruct(p.shape[2:], p.dtype) for p in parts]
    if with_o:
        outs.append(jax.ShapeDtypeStruct(o_part.shape[2:], o_part.dtype))
    dma = pltpu.SemaphoreType.DMA
    line = lambda p: pltpu.VMEM((lines,) + p.shape[2:], p.dtype)
    scratch = [line(p) for p in parts] * 2
    scratch += [pltpu.VMEM(p.shape[2:] if k else (8, 128), p.dtype) for p, k in zip(parts, kinds)]
    if with_o:
        scratch += [pltpu.VMEM(o_part.shape, o_part.dtype)] * 2
        scratch += [pltpu.VMEM(o_part.shape[1:], o_part.dtype)]
    scratch += [dma((jobs, lines))] * 4 + [dma((jobs, 3))] * 2
    if with_o:
        scratch += [dma((lines,))] * 4 + [dma, dma]
    in_specs = [VMEM] * len(inputs)
    if work:
        inputs += work
        in_specs += [HBM] * 4
        shapes, buffers = work_shapes(work, spans, lines)
        outs += shapes
        scratch += buffers
    return pl.pallas_call(
        functools.partial(grads_kernel, lines, tuple(kinds), with_o, spans if work else None),
        out_shape=outs,
        in_specs=in_specs,
        out_specs=[VMEM] * len(outs),
        scratch_shapes=scratch,
        compiler_params=pltpu.CompilerParams(
            collective_id=ident, has_side_effects=True, vmem_limit_bytes=62 << 20
        ),
    )(*inputs)


def nt(a, b):
    return lax.dot_general(a, b, (((1,), (1,)), ((), ())), preferred_element_type=F32)


def hidden_kernel(
    lines, chunks, spans, local_experts,
    src, cots, spread, e_gate, e_up, e_down, s_in, s_down,
    dst, hid, in_d, gate_g, w_in_out, w_down_out,
    h_in, c_in, hid_out, in_out, g_out, w_in, w_down,
    w_sem, own_sem, hs, cins, sts, zs, zr, xs, xr, ys, yr, ds_, dr, cs, cr,
):
    me = Place()
    z, y, x, c = me.z, me.y, me.x, me.c
    expert_at = 2 * z + y
    rows, wide = src.shape
    width, early = w_down.shape[1], cots.shape[-1]
    inner = w_down.shape[0]
    step_rows = rows // chunks
    units = lines * 2 * step_rows
    others = [lax.rem(z + 1 + j, lines) for j in range(lines - 1)]
    places = [(lines - 1, z)] + list(reversed(list(enumerate(others))))
    to_x, to_y, to_c = me.at(x=1 - x), me.at(y=1 - y), me.at(c=1 - c)
    greet([me.at(z=o) for o in others] + [to_x, to_y, to_c])
    half = wide // 256 * 128
    cuts = (pl.ds(0, half), pl.ds(half, wide - half))
    side_of = lambda side: (lax.rem(y + side // 2, 2), lax.rem(x + lax.rem(side, 2), 2))

    def span(k):
        return pl.ds(pl.multiple_of(k * step_rows, step_rows), step_rows)

    def block(zz, yy, xx, k, cols=None):
        if cols is None:
            return dst.at[zz, yy, xx, c, span(k)]
        return dst.at[zz, yy, xx, c, span(k), cuts[cols]]

    own = pltpu.make_async_copy(src, dst.at[z, y, x, c], own_sem)
    own.start()
    piece = lambda k: src.at[span(k)]
    z_copy = lambda k, j, o: remote(
        piece(k), block(z, y, x, k), zs.at[k, j], zr.at[k, z], me.at(z=o)
    )
    x_copy = lambda k, j, o, b: remote(b, block(o, y, x, k), xs.at[k, j], xr.at[k, o], to_x)
    y_copy = lambda k, j, o, b: remote(b, block(o, y, x, k), ys.at[k, j], yr.at[k, o], to_y)

    def diag_copy(k, j, o, h):
        b = block(o, y, 1 - x, k, 0) if h == 0 else block(o, 1 - y, x, k, 1)
        return remote(b, b, ds_.at[k, j, h], dr.at[k, o, h], to_y if h == 0 else to_x)

    def core_copy(k, side, cc):
        yy, xx = side_of(side)
        b = dst.at[:, yy, xx, cc, span(k)]
        return remote(b, b, cs.at[k, side], cr.at[k, side], to_c)

    def z_land(k):
        for j, o in places[1:]:
            b = block(o, y, x, k)
            remote(b, b, zs.at[k, j], zr.at[k, o], me.at(z=o)).wait_recv()
            x_copy(k, j, o, b).start()
            y_copy(k, j, o, b).start()
        core_copy(k, 0, c).start()

    def xy_land(k):
        for j, o in places:
            b = block(o, y, 1 - x, k)
            remote(b, b, xs.at[k, j], xr.at[k, o], to_x).wait_recv()
            diag_copy(k, j, o, 0).start()
            b = block(o, 1 - y, x, k)
            remote(b, b, ys.at[k, j], yr.at[k, o], to_y).wait_recv()
            diag_copy(k, j, o, 1).start()
        core_copy(k, 1, c).start()
        core_copy(k, 2, c).start()

    def diag_land(k):
        for j, o in places:
            for h, w in ((0, to_y), (1, to_x)):
                b = block(o, 1 - y, 1 - x, k, h)
                remote(b, b, ds_.at[k, j, h], dr.at[k, o, h], w).wait_recv()
        core_copy(k, 3, c).start()

    def loads(k, side):
        yy, xx = side_of(side)
        return (
            pltpu.make_async_copy(dst.at[:, yy, xx, :, span(k)], h_in.at[side], hs.at[side]),
            pltpu.make_async_copy(cots.at[:, yy, xx, :, span(k)], c_in.at[side], cins.at[side]),
        )

    def fetch(k, side):
        core_copy(k, side, 1 - c).wait_recv()
        for copy in loads(k, side):
            copy.start()

    def stores(k, side):
        yy, xx = side_of(side)
        pairs = ((hid_out, hid), (in_out, in_d), (g_out, gate_g))
        return [
            pltpu.make_async_copy(v.at[side], ref.at[:, yy, xx, :, span(k)], sts.at[side, i])
            for i, (v, ref) in enumerate(pairs)
        ]

    def unit(k, side):
        for copy in loads(k, side):
            copy.wait()
        h = h_in[side, :, :, :, :width].reshape(units, width)
        gates = h_in[side, :, :, :, width : width + 128].reshape(units, 128)
        late = h_in[side, :, :, :, width + 128 :].reshape(units, width - early)
        scale = jnp.dot(gates, spread[...], preferred_element_type=F32)
        both = nt(h, w_in[...])
        down = nt(c_in[side].reshape(units, early), w_down[:, :early])
        down = down + nt(late, w_down[:, early:])
        columns = lax.broadcasted_iota(jnp.int32, (units, 128), 1)
        sums = jnp.zeros((units, 128), F32)
        for i, (begin, size) in enumerate(spans):
            at = slice(begin, begin + size)
            up_at = slice(inner + begin, inner + begin + size)
            g, u, d = both[:, at], both[:, up_at], down[:, at]
            sig = 1.0 / (1.0 + jnp.exp(-g))
            act = g * sig
            value = (act * u).astype(BF).astype(F32)
            shape = (lines, 2, step_rows, size)
            if i < local_experts:
                total = jnp.sum(value * d, axis=1, keepdims=True)
                sums = jnp.where(columns == expert_at * local_experts + i, total, sums)
                value = value * scale[:, at]
                d = d * scale[:, at]
            hid_out[side, :, :, :, at] = value.astype(BF).reshape(shape)
            in_out[side, :, :, :, at] = (
                (d * u * (sig + act * (1.0 - sig))).astype(BF).reshape(shape)
            )
            in_out[side, :, :, :, up_at] = (d * act).astype(BF).reshape(shape)
        g_out[side] = sums.astype(BF).reshape(lines, 2, step_rows, 128)
        for copy in stores(k, side):
            copy.start()

    def z_start(k):
        for j, o in enumerate(others):
            z_copy(k, j, o).start()

    z_start(0)
    for k in range(chunks):
        x_copy(k, lines - 1, z, piece(k)).start()
        y_copy(k, lines - 1, z, piece(k)).start()

    fills = []
    for i, (begin, size) in enumerate(spans):
        for target, start, source in (
            (w_in, 0, e_gate.at[i] if i < local_experts else s_in.at[0]),
            (w_in, inner, e_up.at[i] if i < local_experts else s_in.at[1]),
            (w_down, 0, e_down.at[i] if i < local_experts else s_down),
        ):
            held = source.shape[0]
            fills.append(
                pltpu.make_async_copy(
                    source, target.at[pl.ds(start + begin, held)], w_sem.at[2 + len(fills)]
                )
            )
            fills[-1].start()
            if size > held:
                target[start + begin + held : start + begin + size] = jnp.zeros(
                    (size - held, width), BF
                )
    for copy in fills:
        copy.wait()
    keep = [
        pltpu.make_async_copy(w_in, w_in_out, w_sem.at[0]),
        pltpu.make_async_copy(w_down, w_down_out, w_sem.at[1]),
    ]
    for copy in keep:
        copy.start()

    own.wait()
    z_land(0)
    if chunks > 1:
        z_start(1)
    fetch(0, 0)
    valid = lambda k: (k >= 0) & (k < chunks)

    @pl.loop(0, chunks + 2)
    def _(t):
        @pl.loop(0, 4)
        def _(side):
            k = t - (side + 1) // 2

            @pl.when(valid(k))
            def _():
                @pl.when(k >= 1)
                def _():
                    for copy in stores(k - 1, side):
                        copy.wait()

                unit(k, side)

            @pl.when((side == 0) & valid(t - 1))
            def _():
                fetch(t - 1, 2)

            @pl.when((side == 1) & valid(t - 2))
            def _():
                fetch(t - 2, 3)

        @pl.when(valid(t + 1))
        def _():
            z_land(t + 1)

        @pl.when(valid(t + 2))
        def _():
            z_start(t + 2)

        @pl.when(valid(t))
        def _():
            xy_land(t)

        @pl.when(valid(t + 1))
        def _():
            fetch(t + 1, 0)

        @pl.when(valid(t - 1))
        def _():
            diag_land(t - 1)

        @pl.when(valid(t))
        def _():
            fetch(t, 1)

    for copy in keep:
        copy.wait()
    for side in range(4):
        for copy in stores(chunks - 1, side):
            copy.wait()

    @pl.loop(0, chunks)
    def _(k):
        for j, o in enumerate(others):
            z_copy(k, j, o).wait_send()
        for j, o in places:
            b = piece(k) if j == lines - 1 else block(o, y, x, k)
            x_copy(k, j, o, b).wait_send()
            y_copy(k, j, o, b).wait_send()
            diag_copy(k, j, o, 0).wait_send()
            diag_copy(k, j, o, 1).wait_send()
        for side in range(4):
            core_copy(k, side, c).wait_send()


def gather_hidden(
    value, cots, spread, e_gate, e_up, e_down, s_in, s_down, spans, local_experts, lines, ident
):
    rows, wide = value.shape
    width, early = e_down.shape[2], cots.shape[1]
    inner = spans[-1][0] + spans[-1][1]
    step_rows = min(rows, max(16, 128 // lines))
    chunks = rows // step_rows
    lead = (lines, 2, 2, 2, rows)
    dma = pltpu.SemaphoreType.DMA
    slot = lambda n: pltpu.VMEM((4, lines, 2, step_rows, n), BF)
    line = dma((chunks, lines))
    return pl.pallas_call(
        functools.partial(hidden_kernel, lines, chunks, spans, local_experts),
        out_shape=[
            jax.ShapeDtypeStruct(lead + (n,), BF) for n in (wide, inner, 2 * inner, 128)
        ]
        + [
            jax.ShapeDtypeStruct((2 * inner, width), BF),
            jax.ShapeDtypeStruct((inner, width), BF),
        ],
        in_specs=[HBM, HBM, VMEM] + [HBM] * 5,
        out_specs=[HBM] * 6,
        scratch_shapes=[
            slot(wide), slot(early), slot(inner), slot(2 * inner), slot(128),
            pltpu.VMEM((2 * inner, width), BF), pltpu.VMEM((inner, width), BF),
            dma((2 + 3 * len(spans),)), dma, dma((4,)), dma((4,)), dma((4, 3)),
            line, line, line, line, line, line,
            dma((chunks, lines, 2)), dma((chunks, lines, 2)), dma((chunks, 4)), dma((chunks, 4)),
        ],
        compiler_params=pltpu.CompilerParams(
            collective_id=ident, has_side_effects=True, vmem_limit_bytes=60 << 20
        ),
    )(value, cots.reshape(lead + (early,)), spread, e_gate, e_up, e_down, s_in, s_down)


def back_kernel(
    lines,
    hid, in_d, gate_g, w_in, w_down,
    out, parts,
    hid_in, d_in, g_in, part_out, sbuf, acc, cbuf, xbuf, ybuf, zbuf, xdiag, ydiag,
    ins, sts, cs, cr, xs, xr, ys, yr, zs, zr, xds, xdr, yds, ydr,
):
    me = Place()
    z, y, x, c = me.z, me.y, me.x, me.c
    rows, wide = out.shape
    width = wide - 128
    half = wide // 256 * 128
    others = [lax.rem(z + 1 + j, lines) for j in range(lines - 1)]
    to_x, to_y, to_c = me.at(x=1 - x), me.at(y=1 - y), me.at(c=1 - c)
    greet([me.at(z=o) for o in others] + [to_x, to_y, to_c])
    cols = (pl.ds(0, half), pl.ds(half, wide - half))
    lag = (0, 1, 1, 2)
    place = lambda n: lax.rem(z + 1 + n, lines)

    def side_of(side):
        return (
            lax.rem(y + 1 - side // 2, 2),
            lax.rem(x + 1 - lax.rem(side, 2), 2),
        )

    def loads(n, side):
        yy, xx = side_of(side)
        pairs = ((hid, hid_in), (in_d, d_in), (gate_g, g_in))
        return [
            pltpu.make_async_copy(ref.at[place(n), yy, xx], v.at[side], ins.at[side, i])
            for i, (ref, v) in enumerate(pairs)
        ]

    def store(n, side):
        yy, xx = side_of(side)
        return pltpu.make_async_copy(
            part_out.at[side], parts.at[place(n), yy, xx], sts.at[side]
        )

    def to_core(n, side):
        yy, xx = side_of(side)
        return remote(
            sbuf.at[side], cbuf.at[place(n), yy, xx], cs.at[side], cr.at[n, side], to_c
        )

    def unit(n, side):
        yy, xx = side_of(side)
        for copy in loads(n, side):
            copy.wait()
        inner = w_down.shape[0]
        grads = d_in[side].reshape(2 * rows, 2 * inner)
        value = hid_in[side].reshape(2 * rows, inner)
        piece = 512
        for begin in range(0, width, piece):
            at = slice(begin, begin + piece)
            back = jnp.dot(grads, w_in[:, at], preferred_element_type=F32).astype(BF).reshape(2, rows, piece)

            @pl.when(c == 0)
            def _():
                acc[place(n), yy, xx, :, at] = back[0]
                sbuf[side, :, at] = back[1]

            @pl.when(c == 1)
            def _():
                acc[place(n), yy, xx, :, at] = back[1]
                sbuf[side, :, at] = back[0]

            part_out[side, :, :, at] = (
                jnp.dot(value, w_down[:, at], preferred_element_type=F32)
                .astype(BF)
                .reshape(2, rows, piece)
            )
        acc[place(n), yy, xx, :, width:] = g_in[side, c]
        sbuf[side, :, width:] = g_in[side, 1 - c]

    def sums(target, *terms):
        @pl.loop(0, rows // 16)
        def _(i):
            at = pl.ds(pl.multiple_of(i * 16, 16), 16)
            total = terms[0][at].astype(F32)
            for term in terms[1:]:
                total = total + term[at].astype(F32)
            target[at] = total.astype(BF)

    def diag_sends(n):
        o = place(n)
        far = acc.at[o, 1 - y, 1 - x]
        return (
            remote(far.at[:, cols[0]], xdiag.at[o], xds.at[n], xdr.at[n], to_x),
            remote(far.at[:, cols[1]], ydiag.at[o], yds.at[n], ydr.at[n], to_y),
        )

    def side_sends(n):
        o = place(n)
        return (
            remote(acc.at[o, y, 1 - x], xbuf.at[o], xs.at[n], xr.at[n], to_x),
            remote(acc.at[o, 1 - y, x], ybuf.at[o], ys.at[n], yr.at[n], to_y),
        )

    def z_copy(n):
        return remote(
            acc.at[place(n), y, x], zbuf.at[z], zs.at[n], zr.at[z], me.at(z=place(n))
        )

    def first(n):
        to_core(n, 0).wait_recv()
        mine, other = acc.at[place(n), 1 - y, 1 - x], cbuf.at[place(n), 1 - y, 1 - x]
        sums(mine, mine, other)
        for copy in diag_sends(n):
            copy.start()

    def second(n):
        o = place(n)
        mine, other = acc.at[o, 1 - y, x], cbuf.at[o, 1 - y, x]
        to_core(n, 1).wait_recv()
        diag_sends(n)[0].wait_recv()
        sums(mine.at[:, cols[0]], mine.at[:, cols[0]], other.at[:, cols[0]], xdiag.at[o])
        sums(mine.at[:, cols[1]], mine.at[:, cols[1]], other.at[:, cols[1]])
        side_sends(n)[1].start()

    def third(n):
        o = place(n)
        mine, other = acc.at[o, y, 1 - x], cbuf.at[o, y, 1 - x]
        to_core(n, 2).wait_recv()
        diag_sends(n)[1].wait_recv()
        sums(mine.at[:, cols[0]], mine.at[:, cols[0]], other.at[:, cols[0]])
        sums(mine.at[:, cols[1]], mine.at[:, cols[1]], other.at[:, cols[1]], ydiag.at[o])
        side_sends(n)[0].start()

    def fourth(n):
        o = place(n)
        mine, other = acc.at[o, y, x], cbuf.at[o, y, x]
        to_core(n, 3).wait_recv()
        for copy in side_sends(n):
            copy.wait_recv()
        sums(mine, mine, other, xbuf.at[o], ybuf.at[o])

        @pl.when(n < lines - 1)
        def _():
            z_copy(n).start()

    valid = lambda n: (n >= 0) & (n < lines)
    for side in range(4):
        for copy in loads(0, side):
            copy.start()

    @pl.loop(0, lines + 3)
    def _(t):
        @pl.loop(0, 4)
        def _(side):
            n = t - (side + 1) // 2

            @pl.when(valid(n))
            def _():
                @pl.when(n >= 1)
                def _():
                    store(n - 1, side).wait()
                    to_core(n - 1, side).wait_send()

                unit(n, side)
                to_core(n, side).start()
                store(n, side).start()

                @pl.when(n + 1 < lines)
                def _():
                    for copy in loads(n + 1, side):
                        copy.start()

            for turn, (behind, act) in enumerate(((3, fourth), (0, first), (1, second), (1, third))):

                @pl.when((side == turn) & valid(t - behind))
                def _(behind=behind, act=act):
                    act(t - behind)

    for side in range(4):
        store(lines - 1, side).wait()
        to_core(lines - 1, side).wait_send()
    for o in others:
        remote(zbuf.at[o], zbuf.at[o], zs.at[0], zr.at[o], me.at(z=o)).wait_recv()

    @pl.loop(0, rows // 16)
    def _(i):
        at = pl.ds(pl.multiple_of(i * 16, 16), 16)
        total = acc[z, y, x, at].astype(F32)
        for o in others:
            total = total + zbuf[o, at].astype(F32)
        out[at] = total

    @pl.loop(0, lines)
    def _(n):
        for copy in diag_sends(n) + side_sends(n):
            copy.wait_send()

        @pl.when(n < lines - 1)
        def _():
            z_copy(n).wait_send()


def sum_back(hid, in_d, gate_g, w_in, w_down, ident):
    lines, rows, inner = hid.shape[0], hid.shape[4], hid.shape[5]
    width = w_in.shape[1]
    wide = width + 128
    half = wide // 256 * 128
    dma = pltpu.SemaphoreType.DMA
    buf = lambda *shape: pltpu.VMEM(shape, BF)
    line = dma((lines,))
    return pl.pallas_call(
        functools.partial(back_kernel, lines),
        out_shape=[
            jax.ShapeDtypeStruct((rows, wide), F32),
            jax.ShapeDtypeStruct((lines, 2, 2, 2, rows, width), BF),
        ],
        in_specs=[HBM] * 3 + [VMEM] * 2,
        out_specs=[VMEM, HBM],
        scratch_shapes=[
            buf(4, 2, rows, inner), buf(4, 2, rows, 2 * inner),
            buf(4, 2, rows, 128), buf(4, 2, rows, width), buf(4, rows, wide),
            buf(lines, 2, 2, rows, wide), buf(lines, 2, 2, rows, wide),
            buf(lines, rows, wide), buf(lines, rows, wide), buf(lines, rows, wide),
            buf(lines, rows, half), buf(lines, rows, wide - half),
            dma((4, 3)), dma((4,)), dma((4,)), dma((lines, 4)),
            line, line, line, line, line, line, line, line, line, line,
        ],
        compiler_params=pltpu.CompilerParams(
            collective_id=ident, has_side_effects=True, vmem_limit_bytes=62 << 20
        ),
    )(hid, in_d, gate_g, w_in, w_down)


def on_device(
    tokens,
    cotangent,
    norm1_gain,
    q_weight,
    kva_weight,
    kv_gain,
    kvb_weight,
    o_weight,
    norm2_gain,
    router_weight,
    shared_gate,
    shared_up,
    shared_down,
    expert_gate,
    expert_up,
    expert_down,
    expert_ids,
    token_rank,
    seq_ids,
):
    expert_count = lax.axis_size("expert")
    shard_count = lax.axis_size("shard")
    device_count = expert_count * shard_count
    expert_at = lax.axis_index("expert")
    shard_at = lax.axis_index("shard")
    tok_rows, width = tokens.shape
    group_len = seq_ids.shape[0]
    local_experts = expert_gate.shape[0]
    all_experts = local_experts * expert_count
    top_count = expert_ids.shape[1]
    capacity = max(2, tok_rows * top_count // all_experts)
    score_scale = (NOPE + ROPE) ** (-0.5)
    own_heads = HEADS // shard_count
    latent_width = kva_weight.shape[1]

    lines = expert_count // 2
    o_rows = o_weight.shape[0]
    o_pairs = VDIM == 2 * o_rows

    def by_head(weight):
        rows = weight.shape[0]
        heads = weight.reshape(rows, own_heads, 2, 2, weight.shape[1] // HEADS)
        return heads.transpose(3, 2, 0, 1, 4).reshape(2, 2, rows, weight.shape[1] // 4)

    small = [norm1_gain, norm2_gain, kv_gain, router_weight]
    small_sizes = [v.size for v in small]

    def pack(values):
        flat = jnp.concatenate(values, axis=-1)
        pad = -flat.shape[-1] % 2048
        flat = jnp.pad(flat, [(0, 0)] * (flat.ndim - 1) + [(0, pad)])
        return flat.reshape(flat.shape[:-1] + (-1, 128))

    def unpack(packed):
        flat = packed.reshape(packed.shape[:-2] + (-1,))
        starts = [sum(small_sizes[:i]) for i in range(len(small_sizes))]
        return [flat[..., b : b + n] for b, n in zip(starts, small_sizes)]

    small_own = pack([v.reshape(-1) for v in small])
    rounds = max(1, tok_rows * device_count // 4096)
    planes = [kva_weight]
    started = start_gather(
        tokens,
        planes,
        [1],
        [
            jnp.broadcast_to(small_own, (2, 2) + small_own.shape),
            by_head(kvb_weight),
            by_head(q_weight),
        ],
        o_weight if o_pairs else None,
        lines,
        1,
    )
    group_tokens = started[0].reshape(group_len, width)
    kva_all = started[1].reshape(width, latent_width)
    small_set, kvb_set, q_set, *o_set = started[1 + len(planes) :]
    small_all = unpack(small_set.reshape((device_count,) + small_own.shape))
    kvb_mine = kvb_set.reshape(KV_RANK, -1)
    q_mine = q_set.reshape(width, -1)
    core_at, x_at = shard_at % 2, shard_at // 2
    if o_pairs:
        o_mine = o_set[0].reshape(own_heads * VDIM, width)
    else:
        o_mine = gather(o_weight, BOTH).reshape(own_heads, 2, 2, VDIM, width)
        o_mine = o_mine[:, core_at, x_at].reshape(own_heads * VDIM, width)
    norm1_scale, norm2_scale, latent_scale = [v.reshape(-1).astype(F32) for v in small_all[:3]]
    router = small_all[3].reshape(width, all_experts)

    positions = positions_of(seq_ids)
    cosine_table, sine_table = rope_tables(positions, ROPE)
    token_index = jnp.arange(group_len, dtype=jnp.int32)
    allowed = (token_index[None, :] <= token_index[:, None]) & (
        (seq_ids[None, :] == 0) | (seq_ids[None, :] == seq_ids[:, None])
    )
    input_rows = tokens.astype(F32)
    group_rows = group_tokens.astype(F32)
    normed_group, _ = rms_forward(group_rows, norm1_scale)
    hidden_one = normed_group.astype(BF)
    query_raw = mm(hidden_one, q_mine).reshape(group_len, own_heads, NOPE + ROPE)
    q_nope = query_raw[:, :, :NOPE].astype(BF)
    q_rope = rotate(
        query_raw[:, :, NOPE:], cosine_table[:, None, :], sine_table[:, None, :]
    ).astype(BF)
    compressed = mm(hidden_one, kva_all)
    latent_norm, inverse_latent = rms_forward(compressed[:, :KV_RANK], latent_scale)
    latent = latent_norm.astype(BF)
    k_rope = rotate(compressed[:, KV_RANK:], cosine_table, sine_table).astype(BF)
    keyval = mm(latent, kvb_mine).astype(BF).reshape(group_len, own_heads, NOPE + VDIM)
    keys = keyval[:, :, :NOPE]
    values = keyval[:, :, NOPE:]
    scores = jnp.einsum("qhd,khd->hqk", q_nope, keys, preferred_element_type=F32)
    scores = scores + jnp.einsum("qhd,kd->hqk", q_rope, k_rope, preferred_element_type=F32)
    scores = jnp.where(allowed[None], scores * score_scale, NEGATIVE)
    top_score = jnp.max(scores, axis=-1, keepdims=True)
    log_total = top_score + jnp.log(jnp.sum(jnp.exp(scores - top_score), axis=-1, keepdims=True))
    soft_probs = jnp.exp(scores - log_total)
    prob_low = soft_probs.astype(BF)
    attended = (
        jnp.einsum("hqk,khd->qhd", prob_low, values, preferred_element_type=F32)
        .astype(BF)
        .reshape(group_len, own_heads * VDIM)
    )
    projected = sum_group(mm(attended, o_mine).astype(BF), 2)
    mixed = input_rows + projected

    normed_two, inverse_two = rms_forward(mixed, norm2_scale)
    hidden_two = normed_two.astype(BF)
    logits = mm(hidden_two, router)
    choice_hot = (
        expert_ids[:, :, None] == jnp.arange(all_experts, dtype=jnp.int32)[None, None, :]
    ).astype(F32)
    chosen = jnp.sum(choice_hot * logits[:, None, :], axis=-1)
    gate_probs = jax.nn.softmax(chosen, axis=-1)
    kept = kept_pairs(expert_ids, token_rank, choice_hot, capacity)
    gate_table = jnp.sum(choice_hot * (gate_probs * kept)[:, :, None], axis=1)

    shared_width = shared_down.shape[0]
    both_shared = jnp.stack([shared_gate, shared_up]).reshape(
        2, shared_gate.shape[0], device_count, shared_width
    )
    both_shared = lax.all_to_all(
        both_shared.transpose(2, 0, 1, 3), BOTH, split_axis=0, concat_axis=0
    )
    both_shared = both_shared.transpose(1, 0, 2, 3).reshape(2, width, shared_width)
    own_width = expert_gate.shape[2]
    sizes = [own_width + -own_width % 128] * local_experts + [shared_width + -shared_width % 128]
    spans = tuple((sum(sizes[:i]), size) for i, size in enumerate(sizes))

    spare = -shared_width % 128
    shared_in = jnp.pad(both_shared.swapaxes(1, 2), ((0, 0), (0, spare), (0, 0)))
    shared_out = jnp.pad(shared_down, ((0, spare), (0, 0)))
    unit_expert = jnp.concatenate(
        [jnp.full((size,), expert_at * local_experts + i) for i, size in enumerate(sizes[:-1])]
        + [jnp.full((sizes[-1],), -1)]
    )
    column = jnp.arange(128)[:, None]
    spread = (
        (column == unit_expert) | ((column == unit_expert + all_experts) & (unit_expert >= 0))
    ).astype(BF)

    early = width // 2

    def ffn(rows, cots, table):
        cots_all = gather(cots[:, :early] + 0 * group_tokens[0, 0], BOTH)
        high = table.astype(BF)
        low = (table - high.astype(F32)).astype(BF)
        spare = jnp.zeros((table.shape[0], 128 - 2 * all_experts), BF)
        values, hid, in_d, gate_g, w_in, w_down = gather_hidden(
            jnp.concatenate([rows, high, low, spare, cots[:, early:]], axis=1),
            cots_all,
            spread,
            expert_gate.swapaxes(1, 2),
            expert_up.swapaxes(1, 2),
            expert_down,
            shared_in,
            shared_out,
            spans,
            local_experts,
            lines,
            3,
        )
        back_sum, out_part = lax.optimization_barrier(
            sum_back(hid, in_d, gate_g, w_in, w_down, 4)
        )
        flat = lambda v: v.reshape(cots_all.shape[0], -1)
        work = [flat(values), cots_all, flat(in_d), flat(hid)]
        return scatter_sum(flat(out_part), BOTH), back_sum, work

    tail = spans[-1][0]
    inner = tail + spans[-1][1]
    expert_spans = tuple(span + (own_width,) for span in spans[:-1])
    shared_spans = (spans[-1] + (shared_width,),)
    if rounds == 1:
        out_sum, back_sum, work = ffn(hidden_two, cotangent, gate_table)
    else:

        def one_round(total, part):
            out_rows, back_rows, (values, cots, in_d, hid) = ffn(*part)
            rows = values[:, :width]
            cots = jnp.concatenate([cots, values[:, width + 128 :]], axis=1)
            grads = [mm_tn(in_d, rows), mm_tn(hid, cots)]
            return [t + g for t, g in zip(total, grads)], (out_rows, back_rows)

        in_rounds = lambda value: value.reshape((rounds, -1) + value.shape[1:])
        zeros = [jnp.zeros((2 * inner, width), F32), jnp.zeros((inner, width), F32)]
        (w_in_grad, w_down_grad), (out_sum, back_sum) = lax.scan(
            one_round, zeros, (in_rounds(hidden_two), in_rounds(cotangent), in_rounds(gate_table))
        )
        out_sum = out_sum.reshape((tok_rows,) + out_sum.shape[2:])
        back_sum = back_sum.reshape((tok_rows,) + back_sum.shape[2:])
        w_in_grad = w_in_grad.reshape(2, inner, width)
        cut = lambda grad: jnp.stack(
            [grad[spans[i][0] : spans[i][0] + own_width] for i in range(local_experts)]
        )
        expert_grads = [cut(w_in_grad[0]), cut(w_in_grad[1]), cut(w_down_grad)]
        shared_made = [v[tail : tail + shared_width] for v in (*w_in_grad, w_down_grad)]
        work = None
    out_sum, back_sum = out_sum.astype(F32), back_sum.astype(F32)
    output = (mixed + out_sum).astype(BF)

    upstream = cotangent.astype(F32)
    gate_grad = jnp.sum(
        choice_hot * back_sum[:, None, width : width + all_experts], axis=-1
    ) * kept
    chosen_grad = gate_probs * (gate_grad - jnp.sum(gate_probs * gate_grad, axis=-1, keepdims=True))
    logit_grad = jnp.sum(choice_hot * chosen_grad[:, :, None], axis=1).astype(BF)
    router_part = mm_tn(hidden_two, logit_grad)
    hidden_two_grad = back_sum[:, :width] + mm_nt(logit_grad, router)
    mixed_norm_grad, norm2_part = rms_backward(mixed, inverse_two, norm2_scale, hidden_two_grad)
    mixed_grad = upstream + mixed_norm_grad

    mixed_grad_group, *made = gather_group(mixed_grad.astype(BF), 5, work, shared_spans, lines)
    if work:
        shared_made = [v[0] for v in made]
    shared_grad = jnp.stack(shared_made[:2]).astype(BF)
    shared_grad = shared_grad.reshape(2, shared_width, device_count, -1).transpose(2, 0, 3, 1)
    shared_grad = lax.all_to_all(shared_grad, BOTH, split_axis=0, concat_axis=0)
    shared_grad = shared_grad.astype(F32).transpose(1, 2, 0, 3).reshape(
        2, width // device_count, device_count * shared_width
    )
    sdown_grad = shared_made[2]
    o_part = mm_tn(attended, mixed_grad_group)
    attended_grad = (
        mm_nt(mixed_grad_group, o_mine).astype(BF).reshape(group_len, own_heads, VDIM)
    )
    prob_grad = jnp.einsum("qhd,khd->hqk", attended_grad, values, preferred_element_type=F32)
    values_grad = jnp.einsum("hqk,qhd->khd", prob_low, attended_grad, preferred_element_type=F32)
    score_grad = (
        soft_probs * (prob_grad - jnp.sum(soft_probs * prob_grad, axis=-1, keepdims=True))
    ).astype(BF)
    q_nope_grad = (
        jnp.einsum("hqk,khd->qhd", score_grad, keys, preferred_element_type=F32) * score_scale
    )
    q_rope_grad = (
        jnp.einsum("hqk,kd->qhd", score_grad, k_rope, preferred_element_type=F32) * score_scale
    )
    keys_grad = (
        jnp.einsum("hqk,qhd->khd", score_grad, q_nope, preferred_element_type=F32) * score_scale
    )
    rope_grad = (
        jnp.einsum("hqk,qhd->kd", score_grad, q_rope, preferred_element_type=F32) * score_scale
    )
    keyval_grad = (
        jnp.concatenate([keys_grad, values_grad], axis=-1)
        .reshape(group_len, own_heads * (NOPE + VDIM))
        .astype(BF)
    )
    kvb_part = mm_tn(latent, keyval_grad)
    latent_part = jnp.concatenate([mm_nt(keyval_grad, kvb_mine), rope_grad], axis=1).astype(BF)
    latent_sum = sum_group(
        jnp.pad(latent_part, ((0, 0), (0, -latent_part.shape[1] % 128))), 6
    )[:, :latent_width]
    own_start = shard_at * tok_rows
    own_rows = lambda value: lax.dynamic_slice_in_dim(value, own_start, tok_rows)
    latent_raw_grad, kv_gain_part = rms_backward(
        own_rows(compressed[:, :KV_RANK]),
        own_rows(inverse_latent),
        latent_scale,
        latent_sum[:, :KV_RANK],
    )
    compressed_grad = jnp.concatenate(
        [
            latent_raw_grad,
            rotate(latent_sum[:, KV_RANK:], own_rows(cosine_table), -own_rows(sine_table)),
        ],
        axis=1,
    ).astype(BF)
    compressed_grad_group = gather_group(
        jnp.pad(compressed_grad, ((0, 0), (0, -latent_width % 128))), 7
    )[0][:, :latent_width]
    query_grad = jnp.concatenate(
        [q_nope_grad, rotate(q_rope_grad, cosine_table[:, None, :], -sine_table[:, None, :])],
        axis=-1,
    )
    query_grad = query_grad.reshape(group_len, own_heads * (NOPE + ROPE)).astype(BF)
    q_part = mm_tn(hidden_one, query_grad)
    kva_part = mm_tn(hidden_one, compressed_grad_group).astype(BF)
    kva_part = lax.dynamic_index_in_dim(
        kva_part.reshape(expert_count, shard_count, width // device_count, latent_width),
        shard_at,
        1,
        keepdims=False,
    )
    hidden_one_grad = sum_group(mm_nt(query_grad, q_mine).astype(BF), 8) + mm_nt(
        compressed_grad, kva_all
    )
    _, inverse_one = rms_forward(input_rows, norm1_scale)
    input_norm_grad, norm1_part = rms_backward(
        input_rows, inverse_one, norm1_scale, hidden_one_grad
    )
    tokens_grad = mixed_grad + input_norm_grad

    def from_heads(parts):
        rows = parts.shape[2]
        heads = parts.reshape(2, 2, rows, own_heads, -1).transpose(2, 3, 1, 0, 4)
        return heads.reshape(rows, -1).astype(F32)

    line_shape = (lines, 2)
    small_parts = pack(
        [v.reshape(device_count, -1) for v in (norm1_part, norm2_part, kv_gain_part, router_part)]
    )
    parts = [
        kvb_part.astype(BF).reshape(line_shape + (2, 2, kvb_weight.shape[0], -1)),
        kva_part.reshape(line_shape + (width // device_count, latent_width)),
        q_part.astype(BF).reshape(line_shape + (2, 2, q_weight.shape[0], q_mine.shape[1])),
        small_parts.reshape(line_shape + (2, 2) + small_parts.shape[1:]),
    ]
    o_part = o_part.astype(BF).reshape(own_heads, VDIM, width)
    if o_pairs:
        o_sum = o_part.reshape(own_heads, 2, o_rows, width)
    else:
        o_sum = None
        o_wide = jnp.zeros((own_heads, 2, 2, VDIM, width), BF).at[:, core_at, x_at].set(o_part)
        o_grad = scatter_sum(o_wide.reshape(HEADS * VDIM, width), BOTH).astype(F32)
    summed = sum_grads(
        parts, (True, False, True, True), o_sum, lines, 9, work, expert_spans
    )
    if work:
        expert_grads = summed[-3:]
    kvb_grad = from_heads(summed[0])
    kva_grad = summed[1].astype(F32)
    q_grad = from_heads(summed[2])
    norm1_grad, norm2_grad, kv_gain_grad, router_grad = unpack(jnp.sum(summed[3], axis=(0, 1)))
    router_grad = router_grad.reshape(router_weight.shape)
    if o_pairs:
        o_grad = summed[4].astype(F32)
    return (
        output,
        tokens_grad,
        norm1_grad,
        q_grad,
        kva_grad,
        kv_gain_grad,
        kvb_grad,
        o_grad,
        norm2_grad,
        router_grad,
        shared_grad[0],
        shared_grad[1],
        sdown_grad,
        expert_grads[0].swapaxes(1, 2),
        expert_grads[1].swapaxes(1, 2),
        expert_grads[2],
    )


def solution(mesh):
    rows = P(BOTH, None)
    flat = P(BOTH)
    columns = P("expert", None, "shard")
    depth = P("expert", "shard", None)
    return jax.shard_map(
        on_device,
        mesh=mesh,
        in_specs=(
            rows,
            rows,
            flat,
            rows,
            rows,
            flat,
            rows,
            rows,
            flat,
            rows,
            rows,
            rows,
            rows,
            columns,
            columns,
            depth,
            rows,
            flat,
            P("expert"),
        ),
        out_specs=(
            rows,
            rows,
            flat,
            rows,
            rows,
            flat,
            rows,
            rows,
            flat,
            rows,
            rows,
            rows,
            rows,
            columns,
            columns,
            depth,
        ),
        check_vma=False,
    )
```

```python
import functools

import jax
import jax.numpy as jnp
from jax import lax
from jax.experimental import pallas as pl
from jax.experimental.pallas import tpu as pltpu
from jax.sharding import PartitionSpec as P

HEADS = 16
NOPE = 128
ROPE = 64
VDIM = 128
KV_RANK = 512
CONTS = 2


EPSILON = 1e-06
THETA = 10000.0
NEGATIVE = -1e30
BOTH = ("expert", "shard")
BF = jnp.bfloat16
F32 = jnp.float32


def rms_forward(values, gain_row):
    inverse = lax.rsqrt(jnp.mean(values * values, axis=-1, keepdims=True) + EPSILON)
    return (values * inverse * gain_row, inverse)


def rms_backward(values, inverse, gain_row, upstream):
    normed = values * inverse
    scaled = upstream * gain_row
    value_grad = inverse * (scaled - normed * jnp.mean(scaled * normed, axis=-1, keepdims=True))
    return (value_grad, jnp.sum(upstream * normed, axis=0))


def rope_tables(positions, width):
    half_width = width // 2
    frequency = THETA ** (-2.0 * jnp.arange(half_width, dtype=jnp.float32) / width)
    angles = positions.astype(jnp.float32)[:, None] * frequency[None, :]
    return (jnp.cos(angles), jnp.sin(angles))


def rotate(values, cosine_table, sine_table):
    half_width = values.shape[-1] // 2
    first_half = values[..., :half_width]
    second = values[..., half_width:]
    return jnp.concatenate(
        [
            first_half * cosine_table - second * sine_table,
            second * cosine_table + first_half * sine_table,
        ],
        axis=-1,
    )


def positions_of(group_ids):
    length = group_ids.shape[0]
    token_index = jnp.arange(length, dtype=jnp.int32)
    labels = jnp.arange(CONTS + 1, dtype=jnp.int32)
    member = (group_ids[:, None] == labels[None, :]).astype(jnp.int32)
    counts = jnp.sum(member, axis=0)
    starts = jnp.cumsum(counts) - counts
    start_of = jnp.sum(member * starts[None, :], axis=1)
    return token_index - start_of + jnp.where(group_ids > 0, counts[0], 0)


def kept_pairs(choice_ids, rank_row, choice_hot, capacity):
    row_count, top_count, expert_total = choice_hot.shape
    per_k = jnp.sum(choice_hot, axis=0)
    before_k = jnp.cumsum(per_k, axis=0) - per_k
    lower = (rank_row[None, :] < rank_row[:, None]).astype(F32)
    same_k = jnp.dot(
        lower.astype(BF),
        choice_hot.reshape(row_count, top_count * expert_total).astype(BF),
        preferred_element_type=F32,
    ).reshape(row_count, top_count, expert_total)
    place = jnp.sum((same_k + before_k[None]) * choice_hot, axis=-1)
    return (place < capacity).astype(F32)


def mm(a, b):
    return jnp.dot(a, b, preferred_element_type=F32)


def mm_nt(a, b):
    return lax.dot_general(a, b, (((1,), (1,)), ((), ())), preferred_element_type=F32)


def mm_tn(a, b):
    return lax.dot_general(a, b, (((0,), (0,)), ((), ())), preferred_element_type=F32)


def gather(value, axes):
    return lax.all_gather(value, axes, axis=0, tiled=True)


def scatter_sum(value, axes):
    return lax.psum_scatter(value, axes, scatter_dimension=0, tiled=True)


HBM = pl.BlockSpec(memory_space=pl.ANY)
VMEM = pl.BlockSpec(memory_space=pltpu.VMEM)


class Place:
    def __init__(self):
        e, s = lax.axis_index("expert"), lax.axis_index("shard")
        self.z, self.y, self.x, self.c = e // 2, e % 2, s // 2, s % 2

    def at(self, z=None, y=None, x=None, c=None):
        z = self.z if z is None else z
        y = self.y if y is None else y
        x = self.x if x is None else x
        c = self.c if c is None else c
        return {"expert": 2 * z + y, "shard": 2 * x + c}


def greet(partners):
    barrier = pltpu.get_barrier_semaphore()
    for partner in partners:
        pl.semaphore_signal(
            barrier, inc=1, device_id=partner, device_id_type=pl.DeviceIdType.MESH
        )
    pl.semaphore_wait(barrier, len(partners))


def remote(src, dst, send, recv, where):
    return pltpu.make_async_remote_copy(
        src_ref=src,
        dst_ref=dst,
        send_sem=send,
        recv_sem=recv,
        device_id=where,
        device_id_type=pl.DeviceIdType.MESH,
    )


def gather_group_kernel(cuts, spans, *refs):
    refs = list(refs)
    take = lambda n: [refs.pop(0) for _ in range(n)]
    (src,) = take(1)
    work = take(4) if spans else None
    (dst,) = take(1)
    made = take(3) if spans else None
    own_sem, send, recv = take(3)
    me = Place()
    x, c = me.x, me.c
    to_x, to_c = me.at(x=1 - x), me.at(c=1 - c)
    greet([to_x, to_c])
    cut = src.shape[0] // cuts
    span = lambda k: pl.ds(k * cut, cut)
    own = pltpu.make_async_copy(src, dst.at[x, c], own_sem)
    own.start()
    over_x = [
        remote(src.at[span(k)], dst.at[x, c, span(k)], send.at[0, k], recv.at[0, k], to_x)
        for k in range(cuts)
    ]
    for copy in over_x:
        copy.start()
    over_c = remote(src, dst.at[x, c], send.at[1, 0], recv.at[1, 0], to_c)
    over_c.start()
    if spans:
        turns, begin_work, work_turn = grad_worker(work, made, refs[:3], refs[3], spans)
        begin_work()

        @pl.loop(0, turns)
        def _(n):
            work_turn(n)

    relays = []
    for k in range(cuts):
        far = dst.at[1 - x, c, span(k)]
        remote(far, far, send.at[0, k], recv.at[0, k], to_x).wait_recv()
        relays.append(remote(far, far, send.at[2, k], recv.at[2, k], to_c))
        relays[-1].start()
    far = dst.at[x, 1 - c]
    remote(far, far, send.at[1, 0], recv.at[1, 0], to_c).wait_recv()
    for k in range(cuts):
        far = dst.at[1 - x, 1 - c, span(k)]
        remote(far, far, send.at[2, k], recv.at[2, k], to_c).wait_recv()
    own.wait()
    for copy in over_x + [over_c] + relays:
        copy.wait_send()


def gather_group(value, ident, work=None, spans=None, lines=None, cuts=4):
    rows, width = value.shape
    dma = pltpu.SemaphoreType.DMA
    inputs, in_specs = [value], [HBM]
    outs = [jax.ShapeDtypeStruct((2, 2, rows, width), value.dtype)]
    scratch = [dma, dma((3, cuts)), dma((3, cuts))]
    if work:
        inputs += work
        in_specs += [HBM] * 4
        shapes, buffers = work_shapes(work, spans, lines)
        outs += shapes
        scratch += buffers
    out, *made = pl.pallas_call(
        functools.partial(gather_group_kernel, cuts, spans if work else None),
        out_shape=outs,
        in_specs=in_specs,
        out_specs=[HBM] + [VMEM] * (len(outs) - 1),
        scratch_shapes=scratch,
        compiler_params=pltpu.CompilerParams(
            collective_id=ident, has_side_effects=True, vmem_limit_bytes=40 << 20
        ),
    )(*inputs)
    return [out.reshape(4 * rows, width)] + made


def sum_group_kernel(cuts, part, out, cbuf, xbuf, xsum, cs, cr, xs, xr):
    me = Place()
    x, c = me.x, me.c
    rows, width = out.shape
    cut = rows // cuts
    to_x, to_c = me.at(x=1 - x), me.at(c=1 - c)
    greet([to_x, to_c])
    span = lambda k: pl.ds(k * cut, cut)
    core = lambda k, far: remote(
        part.at[1 - x if far else x, 1 - c, span(k)],
        cbuf.at[far, span(k)],
        cs.at[k, far],
        cr.at[k, far],
        to_c,
    )
    over = lambda k: remote(xsum.at[span(k)], xbuf.at[span(k)], xs.at[k], xr.at[k], to_x)
    for k in range(cuts):
        core(k, 1).start()
    for k in range(cuts):
        core(k, 0).start()

    def add(k, target, one, two):
        @pl.loop(0, cut // 16)
        def _(i):
            at = pl.ds(pl.multiple_of(k * cut + i * 16, 16), 16)
            target[at] = (one[at].astype(F32) + two[at].astype(F32)).astype(target.dtype)

    for k in range(cuts):
        core(k, 1).wait_recv()
        add(k, xsum, part.at[1 - x, c], cbuf.at[1])
        over(k).start()
    for k in range(cuts):
        core(k, 0).wait_recv()
        add(k, out, part.at[x, c], cbuf.at[0])
    for k in range(cuts):
        over(k).wait_recv()
        add(k, out, out, xbuf)
    for k in range(cuts):
        core(k, 1).wait_send()
        core(k, 0).wait_send()
        over(k).wait_send()


def sum_group(part, ident, cuts=4):
    rows, width = part.shape[0] // 4, part.shape[1]
    dma = pltpu.SemaphoreType.DMA
    buf = lambda *lead: pltpu.VMEM(lead + (rows, width), part.dtype)
    return pl.pallas_call(
        functools.partial(sum_group_kernel, cuts),
        out_shape=jax.ShapeDtypeStruct((rows, width), F32),
        in_specs=[VMEM],
        out_specs=VMEM,
        scratch_shapes=[
            buf(2), buf(), buf(),
            dma((cuts, 2)), dma((cuts, 2)), dma((cuts,)), dma((cuts,)),
        ],
        compiler_params=pltpu.CompilerParams(
            collective_id=ident, has_side_effects=True, vmem_limit_bytes=32 << 20
        ),
    )(part.reshape(2, 2, rows, width))


def rows_loop(target, act):
    if len(target.shape) > 2:
        for i in range(target.shape[0]):
            rows_loop(target.at[i], lambda at, i=i: act((i,) + at))
        return
    rows = target.shape[0]
    step = 16 if rows % 16 == 0 else rows

    @pl.loop(0, rows // step)
    def _(i):
        act((pl.ds(pl.multiple_of(i * step, step), step),))


def add_blocks(target, one, two):
    def act(at):
        target[at] = (one[at].astype(F32) + two[at].astype(F32)).astype(target.dtype)

    rows_loop(target, act)


def add_three(target, one, two, three):
    def act(at):
        total = one[at].astype(F32) + two[at].astype(F32) + three[at].astype(F32)
        target[at] = total.astype(target.dtype)

    rows_loop(target, act)


class Copies:
    def __init__(self):
        self.started = []

    def go(self, copy):
        copy.start()
        self.started.append(copy)

    def finish(self):
        for copy in self.started:
            copy.wait_send()


def start_kernel(lines, counts, with_o, *refs):
    jobs, planes = 3, len(counts)
    refs = list(refs)
    take = lambda n: [refs.pop(0) for _ in range(n)]
    (tok,) = take(1)
    plane_src, sources = take(planes), take(jobs)
    o_src = take(1)[0] if with_o else None
    (tok_dst,) = take(1)
    plane_dst, dests = take(planes), take(jobs)
    o_dst = take(1)[0] if with_o else None
    own_sem, gs, gr, zs, zr, ys, yr, ts, tr = take(9)
    plane_sems = [take(6) for _ in range(planes)]
    if with_o:
        o_own, ocs, ocr, ozs, ozr, oys, oyr = take(7)
    me = Place()
    z, y, x, c = me.z, me.y, me.x, me.c
    others = [lax.rem(z + 1 + j, lines) for j in range(lines - 1)]
    places = list(enumerate(others)) + [(lines - 1, z)]
    near = [(x, 1 - c), (1 - x, c), (1 - x, 1 - c)]
    to_near = [me.at(x=xx, c=cc) for xx, cc in near]
    to_y, to_x, to_c = me.at(y=1 - y), to_near[1], to_near[0]
    greet([me.at(z=o) for o in others] + [to_y] + to_near)
    copies = Copies()
    go = copies.go

    def span(i, k):
        rows = plane_src[i].shape[0] // counts[i]
        return pl.ds(k * rows, rows)

    def plane_z_start(i, k):
        zs_, zr_, ys_, yr_ = plane_sems[i][:4]
        src, dst = plane_src[i].at[span(i, k)], plane_dst[i].at[z, y, x, c, span(i, k)]
        for j, o in enumerate(others):
            go(remote(src, dst, zs_.at[k, j], zr_.at[k, z], me.at(z=o)))
        go(remote(src, dst, ys_.at[k, lines - 1], yr_.at[k, z], to_y))

    def plane_z_land(i, k):
        zs_, zr_, ys_, yr_ = plane_sems[i][:4]
        for j, o in reversed(places[:-1]):
            block = plane_dst[i].at[o, y, x, c, span(i, k)]
            remote(block, block, zs_.at[k, j], zr_.at[k, o], me.at(z=o)).wait_recv()
            go(remote(block, block, ys_.at[k, j], yr_.at[k, o], to_y))

    def plane_y_land(i, k):
        ys_, yr_, ps, pr = plane_sems[i][2:]
        for j, o in places:
            block = plane_dst[i].at[o, 1 - y, x, c, span(i, k)]
            remote(block, block, ys_.at[k, j], yr_.at[k, o], to_y).wait_recv()
        block = plane_dst[i].at[:, :, x, c, span(i, k)]
        go(remote(block, block, ps.at[k, 0], pr.at[k, 0], to_x))
        go(remote(block, block, ps.at[k, 1], pr.at[k, 1], to_c))

    def plane_x_land(i, k):
        ps, pr = plane_sems[i][4:]
        block = plane_dst[i].at[:, :, 1 - x, c, span(i, k)]
        remote(block, block, ps.at[k, 0], pr.at[k, 0], to_x).wait_recv()
        go(remote(block, block, ps.at[k, 2], pr.at[k, 2], to_c))

    def plane_c_land(i, k):
        ps, pr = plane_sems[i][4:]
        for slot, xx in ((1, x), (2, 1 - x)):
            block = plane_dst[i].at[:, :, xx, 1 - c, span(i, k)]
            remote(block, block, ps.at[k, slot], pr.at[k, slot], to_c).wait_recv()

    locals_ = [
        pltpu.make_async_copy(src, dst.at[z, y, x, c], own_sem.at[i])
        for i, (src, dst) in enumerate(
            zip([v.at[x, c] for v in sources] + plane_src, dests + plane_dst)
        )
    ]
    locals_.append(pltpu.make_async_copy(tok, tok_dst.at[x, c], own_sem.at[jobs + planes]))
    for copy in locals_:
        copy.start()

    for i in range(jobs):
        for p in range(3):
            go(
                remote(
                    sources[i].at[near[p][0], near[p][1]],
                    dests[i].at[z, y, x, c],
                    gs.at[i, p],
                    gr.at[i, p],
                    to_near[p],
                )
            )
    last = planes - 1
    plane_z_start(last, 0)
    if counts[last] > 1:
        plane_z_start(last, 1)
    if with_o:
        o_core = remote(o_src, o_dst.at[z, c], ocs, ocr, to_c)
        o_local = pltpu.make_async_copy(o_src, o_dst.at[z, c], o_own)
        holder = c == y

        @pl.when(jnp.logical_not(holder))
        def _():
            o_core.start()

        @pl.when(holder)
        def _():
            o_local.start()

    go(remote(tok, tok_dst.at[x, c], ts.at[1], tr.at[1], to_x))
    go(remote(tok, tok_dst.at[x, c], ts.at[0], tr.at[0], to_c))
    line_y = lambda i, j, o: remote(
        dests[i].at[o, y], dests[i].at[o, y], ys.at[i, j], yr.at[i, o], to_y
    )
    line_z = lambda i, j, o: remote(
        dests[i].at[z, y], dests[i].at[z, y], zs.at[i, j], zr.at[i, z], me.at(z=o)
    )

    def job_start(i):
        locals_[i].wait()
        for p in range(3):
            xx, cc = near[p]
            block = dests[i].at[z, y, xx, cc]
            remote(block, block, gs.at[i, p], gr.at[i, p], to_near[p]).wait_recv()
        for j, o in enumerate(others):
            go(line_z(i, j, o))
        go(line_y(i, lines - 1, z))

    job_start(0)
    job_start(1)
    plane_z_land(last, 0)
    for k in range(1, counts[last]):
        if k + 1 < counts[last]:
            plane_z_start(last, k + 1)
        plane_z_land(last, k)
        if k == 1:
            job_start(2)
        locals_[jobs + last].wait() if k == 1 else None
        plane_y_land(last, k - 1)
    if counts[last] == 1:
        job_start(2)
        locals_[jobs + last].wait()
    if with_o:
        o_z = lambda j, o: remote(o_dst.at[z], o_dst.at[z], ozs.at[j], ozr.at[z], me.at(z=o))
        o_y = lambda j, o: remote(o_dst.at[o], o_dst.at[o], oys.at[j], oyr.at[o], to_y)

        @pl.when(holder)
        def _():
            o_local.wait()
            block = o_dst.at[z, 1 - c]
            remote(block, block, ocs, ocr, to_c).wait_recv()
            for j, o in enumerate(others):
                o_z(j, o).start()
            o_y(lines - 1, z).start()

    for i in range(last):
        for k in range(counts[i]):
            plane_z_start(i, k)
    plane_y_land(last, counts[last] - 1)
    block = tok_dst.at[1 - x, c]
    remote(block, block, ts.at[1], tr.at[1], to_x).wait_recv()
    go(remote(block, block, ts.at[2], tr.at[2], to_c))
    for j, o in reversed(places[:-1]):
        for i in range(jobs):
            block = dests[i].at[o, y]
            remote(block, block, zs.at[i, j], zr.at[i, o], me.at(z=o)).wait_recv()
            go(line_y(i, j, o))
        if with_o:

            @pl.when(holder)
            def _(j=j, o=o):
                block = o_dst.at[o]
                remote(block, block, ozs.at[j], ozr.at[o], me.at(z=o)).wait_recv()
                o_y(j, o).start()

    for i in range(last):
        for k in range(counts[i]):
            plane_z_land(i, k)
    for k in range(counts[last]):
        plane_x_land(last, k)
    for i in range(last):
        locals_[jobs + i].wait()
        for k in range(counts[i]):
            plane_y_land(i, k)
            plane_x_land(i, k)
    for slot, xx in ((0, x), (2, 1 - x)):
        block = tok_dst.at[xx, 1 - c]
        remote(block, block, ts.at[slot], tr.at[slot], to_c).wait_recv()
    locals_[jobs + planes].wait()
    for j, o in places:
        for i in range(jobs):
            block = dests[i].at[o, 1 - y]
            remote(block, block, ys.at[i, j], yr.at[i, o], to_y).wait_recv()
    if with_o:

        @pl.when(jnp.logical_not(holder))
        def _():
            for j, o in places:
                remote(o_dst.at[o], o_dst.at[o], oys.at[j], oyr.at[o], to_y).wait_recv()
            o_core.wait_send()

        @pl.when(holder)
        def _():
            for j, o in enumerate(others):
                o_z(j, o).wait_send()
            for j, o in places:
                o_y(j, o).wait_send()

    for i in range(planes):
        for k in range(counts[i]):
            plane_c_land(i, k)
    copies.finish()


def start_gather(tokens, planes, counts, column_parts, o_rows, lines, ident):
    jobs = len(column_parts)
    with_o = o_rows is not None
    inputs = [tokens] + planes + column_parts + ([o_rows] if with_o else [])
    shape = lambda lead, v: jax.ShapeDtypeStruct(lead + v.shape, v.dtype)
    outs = [shape((2, 2), tokens)] + [shape((lines, 2, 2, 2), v) for v in planes]
    outs += [jax.ShapeDtypeStruct((lines, 2) + v.shape, v.dtype) for v in column_parts]
    if with_o:
        outs.append(shape((lines, 2), o_rows))
    dma = pltpu.SemaphoreType.DMA
    scratch = [
        dma((jobs + len(planes) + 1,)), dma((jobs, 3)), dma((jobs, 3)),
        dma((jobs, lines)), dma((jobs, lines)), dma((jobs, lines)), dma((jobs, lines)),
        dma((3,)), dma((3,)),
    ]
    for n in counts:
        scratch += [dma((n, lines))] * 4 + [dma((n, 3))] * 2
    if with_o:
        scratch += [dma, dma, dma, dma((lines,)), dma((lines,)), dma((lines,)), dma((lines,))]
    return pl.pallas_call(
        functools.partial(start_kernel, lines, tuple(counts), with_o),
        out_shape=outs,
        in_specs=[HBM] * len(inputs),
        out_specs=[HBM] * len(outs),
        scratch_shapes=scratch,
        compiler_params=pltpu.CompilerParams(collective_id=ident, has_side_effects=True),
    )(*inputs)


def grad_worker(work, made, slots, ins, spans):
    values, cots, in_d, hid = work
    rows_in, cots_in, left_in = slots
    depth, width = rows_in.shape[1:]
    early = cots.shape[1]
    inner = hid.shape[1]
    turns = cots.shape[0] // depth
    first, units = spans[0][0], left_in.shape[3]

    def loads(n):
        at = pl.ds(pl.multiple_of(n * depth, depth), depth)
        slot = lax.rem(n, 2)
        pairs = (
            (values.at[at, pl.ds(0, width)], rows_in.at[slot]),
            (cots.at[at], cots_in.at[slot, :, pl.ds(0, early)]),
            (
                values.at[at, pl.ds(width + 128, width - early)],
                cots_in.at[slot, :, pl.ds(early, width - early)],
            ),
            (in_d.at[at, pl.ds(first, units)], left_in.at[slot, 0]),
            (in_d.at[at, pl.ds(inner + first, units)], left_in.at[slot, 1]),
            (hid.at[at, pl.ds(first, units)], left_in.at[slot, 2]),
        )
        return [
            pltpu.make_async_copy(src, dst, ins.at[slot, i]) for i, (src, dst) in enumerate(pairs)
        ]

    def begin():
        for copy in loads(0):
            copy.start()
        for ref in made:
            for i in range(ref.shape[0]):
                ref[i] = jnp.zeros(ref.shape[1:], F32)

    def turn(n):
        slot = lax.rem(n, 2)

        @pl.when(n + 1 < turns)
        def _():
            for copy in loads(n + 1):
                copy.start()

        for copy in loads(n):
            copy.wait()

        @pl.loop(0, width // 512)
        def _(m):
            at = pl.ds(pl.multiple_of(m * 512, 512), 512)
            for which, right in enumerate((rows_in, rows_in, cots_in)):
                ref = made[which]
                part = lax.dot_general(
                    left_in[slot, which],
                    right[slot, :, at],
                    (((0,), (0,)), ((), ())),
                    preferred_element_type=F32,
                )
                for i, (begin, _, kept) in enumerate(spans):
                    begin = begin - first
                    ref[i, :, at] = ref[i, :, at] + part[begin : begin + kept]

    return turns, begin, turn


def work_shapes(work, spans, lines):
    count, width = work[1].shape[0], work[0].shape[1] - 128
    width = (width + work[1].shape[1]) // 2
    units = sum(size for _, size, _ in spans)
    depth = min(512, count // lines)
    shapes = [jax.ShapeDtypeStruct((len(spans), spans[0][2], width), F32)] * 3
    rows = pltpu.VMEM((2, depth, width), BF)
    buffers = [rows, rows, pltpu.VMEM((2, 3, depth, units), BF), pltpu.SemaphoreType.DMA((2, 6))]
    return shapes, buffers


def grads_kernel(lines, plane, with_o, spans, *refs):
    jobs = 4
    refs = list(refs)
    take = lambda n: [refs.pop(0) for _ in range(n)]
    parts = take(jobs)
    (rows_part,) = take(1)
    o_part = take(1)[0] if with_o else None
    work = take(4) if spans else None
    outs = take(jobs)
    (rows_out,) = take(1)
    o_out = take(1)[0] if with_o else None
    made = take(3) if spans else None
    ybufs, zbufs, tots = take(jobs), take(jobs), take(jobs)
    p_own, p_core, p_x, r_own, r_core, r_x = take(6)
    ys, yr, zs, zr, gs, gr, ls, ss, sr = take(9)
    if with_o:
        o_ybuf, o_zbuf, o_tot, oys, oyr, ozs, ozr, ocs, ocr = take(9)
    if spans:
        rows_in, cots_in, left_in, ins = take(4)
    me = Place()
    z, y, x, c = me.z, me.y, me.x, me.c
    others = [lax.rem(z + 1 + j, lines) for j in range(lines - 1)]
    places = list(enumerate(others)) + [(lines - 1, z)]
    near = [(x, 1 - c), (1 - x, c), (1 - x, 1 - c)]
    to_near = [me.at(x=xx, c=cc) for xx, cc in near]
    to_y, to_x, to_c = me.at(y=1 - y), to_near[1], to_near[0]
    greet([me.at(z=o) for o in others] + [to_y] + to_near)
    copies = Copies()
    go = copies.go
    plain = [i for i in range(jobs) if i != plane]

    group = (
        (parts[plane], p_own, p_core, p_x, lambda ref, xx, cc: ref.at[:, :, xx, cc]),
        (rows_part, r_own, r_core, r_x, lambda ref, xx, cc: ref.at[xx, cc]),
    )
    core_copy = lambda i, far: remote(
        group[i][4](group[i][0], 1 - x if far else x, 1 - c),
        group[i][2].at[far],
        ss.at[i, far],
        sr.at[i, far],
        to_c,
    )
    own_copy = lambda i, far: pltpu.make_async_copy(
        group[i][4](group[i][0], 1 - x if far else x, c), group[i][1].at[far], ls.at[i, far]
    )
    x_copy = lambda i: remote(group[i][1].at[1], group[i][3], ss.at[i, 2], sr.at[i, 2], to_x)
    for far in (1, 0):
        for i in range(2):
            go(core_copy(i, far))
            own_copy(i, far).start()

    def over_y(i, j, o):
        source = p_own.at[0, o, 1 - y] if i == plane else parts[i].at[o, 1 - y]
        return remote(source, ybufs[i].at[o], ys.at[i, j], yr.at[i, o], to_y)

    def over_z(i, j, o):
        return remote(ybufs[i].at[o], zbufs[i].at[z], zs.at[i, j], zr.at[i, z], me.at(z=o))

    if with_o:
        holder = c == y
        o_over_y = lambda j, o: remote(o_part.at[o], o_ybuf.at[o], oys.at[j], oyr.at[o], to_y)
        o_over_z = lambda j, o: remote(
            o_ybuf.at[o], o_zbuf.at[z], ozs.at[j], ozr.at[z], me.at(z=o)
        )
    for j, o in places:
        for i in plain:
            go(over_y(i, j, o))
        if with_o:

            @pl.when(jnp.logical_not(holder))
            def _(j=j, o=o):
                o_over_y(j, o).start()

    if spans:
        turns, begin_work, work_turn = grad_worker(work, made, (rows_in, cots_in, left_in), ins, spans)
        begin_work()

    @pl.loop(0, lines)
    def _(j):
        if spans:
            per_line = turns // lines

            @pl.loop(0, per_line)
            def _(n):
                work_turn(j * per_line + n)

        @pl.when(j == 0)
        def _():
            for i in range(2):
                core_copy(i, 1).wait_recv()
                own_copy(i, 1).wait()
                add_blocks(group[i][1].at[1], group[i][1].at[1], group[i][2].at[1])
                x_copy(i).start()

        @pl.when(j == 1)
        def _():
            core_copy(0, 0).wait_recv()
            own_copy(0, 0).wait()
            x_copy(0).wait_recv()
            add_three(p_own.at[0], p_own.at[0], p_core.at[0], p_x)
            for k, o in places:
                over_y(plane, k, o).start()

        @pl.when(j == 2)
        def _():
            core_copy(1, 0).wait_recv()
            own_copy(1, 0).wait()
            x_copy(1).wait_recv()
            add_three(rows_out, r_own.at[0], r_core.at[0], r_x)

        o = lax.rem(z + 1 + j, lines)
        for i in plain:
            over_y(i, j, o).wait_recv()
            add_blocks(ybufs[i].at[o], parts[i].at[o, y], ybufs[i].at[o])

            @pl.when(j < lines - 1)
            def _(i=i):
                over_z(i, j, o).start()

        if with_o:

            @pl.when(holder)
            def _():
                o_over_y(j, o).wait_recv()
                add_blocks(o_ybuf.at[o], o_part.at[o], o_ybuf.at[o])

                @pl.when(j < lines - 1)
                def _():
                    o_over_z(j, o).start()

    for j, o in places:
        over_y(plane, j, o).wait_recv()
        add_blocks(ybufs[plane].at[o], p_own.at[0, o, y], ybufs[plane].at[o])
        if j < lines - 1:
            over_z(plane, j, o).start()

    def line_sum(target, acc, zbuf):
        if len(target.shape) > 2:
            for k in range(target.shape[0]):
                line_sum(target.at[k], acc.at[:, k], zbuf.at[:, k])
            return
        rows = target.shape[0]
        step = 16 if rows % 16 == 0 else rows

        @pl.loop(0, rows // step)
        def _(i):
            at = pl.ds(pl.multiple_of(i * step, step), step)
            value = acc[z, at].astype(F32)
            for o in others:
                value = value + zbuf[o, at].astype(F32)
            target[at] = value.astype(target.dtype)

    near_copy = lambda i, p: remote(
        tots[i].at[near[p][0], near[p][1]], outs[i].at[x, c], gs.at[i, p], gr.at[i, p], to_near[p]
    )
    for i in plain + [plane]:
        for j, o in places[:-1]:
            block = zbufs[i].at[o]
            remote(block, block, zs.at[i, j], zr.at[i, o], me.at(z=o)).wait_recv()
        if i == plane:
            line_sum(outs[i], ybufs[i], zbufs[i])
        else:
            line_sum(tots[i], ybufs[i], zbufs[i])
            for p in range(3):
                go(near_copy(i, p))
            outs[i][x, c] = tots[i][x, c]
    if with_o:
        o_core = remote(o_tot.at[1 - c], o_out, ocs, ocr, to_c)

        @pl.when(holder)
        def _():
            for j, o in places[:-1]:
                block = o_zbuf.at[o]
                remote(block, block, ozs.at[j], ozr.at[o], me.at(z=o)).wait_recv()
            line_sum(o_tot.at[1 - c], o_ybuf.at[:, 1 - c], o_zbuf.at[:, 1 - c])
            o_core.start()
            line_sum(o_out, o_ybuf.at[:, c], o_zbuf.at[:, c])
            for j, o in places[:-1]:
                o_over_z(j, o).wait_send()
            o_core.wait_send()

        @pl.when(jnp.logical_not(holder))
        def _():
            for j, o in places:
                o_over_y(j, o).wait_send()
            o_core.wait_recv()

    for i in plain:
        for p in range(3):
            block = outs[i].at[near[p][0], near[p][1]]
            remote(block, block, gs.at[i, p], gr.at[i, p], to_near[p]).wait_recv()
    for i in range(jobs):
        for j, o in places[:-1]:
            over_z(i, j, o).wait_send()
    for j, o in places:
        over_y(plane, j, o).wait_send()
    for i in range(2):
        x_copy(i).wait_send()
    copies.finish()


def sum_grads(parts, plane, rows_part, o_part, lines, ident, work=None, spans=None):
    jobs = len(parts)
    with_o = o_part is not None
    inputs = list(parts) + [rows_part] + ([o_part] if with_o else [])
    in_specs = [HBM if i == plane else VMEM for i in range(jobs)] + [HBM] + [VMEM] * with_o
    block = lambda i: parts[i].shape[4:] if i == plane else parts[i].shape[2:]
    outs = [jax.ShapeDtypeStruct(block(i), parts[i].dtype) for i in range(jobs)]
    outs.append(jax.ShapeDtypeStruct(rows_part.shape[2:], F32))
    if with_o:
        outs.append(jax.ShapeDtypeStruct(o_part.shape[2:], o_part.dtype))
    dma = pltpu.SemaphoreType.DMA
    buf = lambda lead, i: pltpu.VMEM(lead + block(i), parts[i].dtype)
    scratch = [buf((lines,), i) for i in range(jobs)] * 2
    scratch += [pltpu.VMEM((8, 128), BF) if i == plane else buf((), i) for i in range(jobs)]
    scratch += [buf((2, lines, 2), plane), buf((2, lines, 2), plane), buf((lines, 2), plane)]
    rows = lambda *lead: pltpu.VMEM(lead + rows_part.shape[2:], rows_part.dtype)
    scratch += [rows(2), rows(2), rows()]
    scratch += [dma((jobs, lines))] * 4 + [dma((jobs, 3))] * 2
    scratch += [dma((2, 2)), dma((2, 3)), dma((2, 3))]
    if with_o:
        scratch += [pltpu.VMEM(o_part.shape, o_part.dtype)] * 2
        scratch += [pltpu.VMEM(o_part.shape[1:], o_part.dtype)]
        scratch += [dma((lines,))] * 4 + [dma, dma]
    out_specs = [VMEM] * len(outs)
    if work:
        inputs += work
        in_specs += [HBM] * 4
        shapes, buffers = work_shapes(work, spans, lines)
        outs += shapes
        out_specs += [VMEM] * 3
        scratch += buffers
    return pl.pallas_call(
        functools.partial(grads_kernel, lines, plane, with_o, spans if work else None),
        out_shape=outs,
        in_specs=in_specs,
        out_specs=out_specs,
        scratch_shapes=scratch,
        compiler_params=pltpu.CompilerParams(
            collective_id=ident, has_side_effects=True, vmem_limit_bytes=63 << 20
        ),
    )(*inputs)


def nt(a, b):
    return lax.dot_general(a, b, (((1,), (1,)), ((), ())), preferred_element_type=F32)


def hidden_kernel(
    lines, chunks, spans, local_experts,
    src, cots, spread, e_gate, e_up, e_down, s_in, s_down,
    dst, hid, in_d, gate_g, w_in_out, parts,
    h_in, c_in, hid_out, in_out, g_out, part_out, w_in, w_down,
    w_sem, own_sem, hs, cins, sts, zs, zr, xs, xr, ys, yr, ds_, dr, cs, cr,
):
    me = Place()
    z, y, x, c = me.z, me.y, me.x, me.c
    expert_at = 2 * z + y
    rows, wide = src.shape
    width, early = w_down.shape[1], cots.shape[-1]
    inner = w_down.shape[0]
    step_rows = rows // chunks
    units = lines * 2 * step_rows
    others = [lax.rem(z + 1 + j, lines) for j in range(lines - 1)]
    places = [(lines - 1, z)] + list(reversed(list(enumerate(others))))
    to_x, to_y, to_c = me.at(x=1 - x), me.at(y=1 - y), me.at(c=1 - c)
    greet([me.at(z=o) for o in others] + [to_x, to_y, to_c])
    half = wide // 256 * 128
    cuts = (pl.ds(0, half), pl.ds(half, wide - half))
    side_of = lambda side: (lax.rem(y + side // 2, 2), lax.rem(x + lax.rem(side, 2), 2))

    def span(k):
        return pl.ds(pl.multiple_of(k * step_rows, step_rows), step_rows)

    def block(zz, yy, xx, k, cols=None):
        if cols is None:
            return dst.at[zz, yy, xx, c, span(k)]
        return dst.at[zz, yy, xx, c, span(k), cuts[cols]]

    own = pltpu.make_async_copy(src, dst.at[z, y, x, c], own_sem)
    own.start()
    piece = lambda k: src.at[span(k)]
    z_copy = lambda k, j, o: remote(
        piece(k), block(z, y, x, k), zs.at[k, j], zr.at[k, z], me.at(z=o)
    )
    x_copy = lambda k, j, o, b: remote(b, block(o, y, x, k), xs.at[k, j], xr.at[k, o], to_x)
    y_copy = lambda k, j, o, b: remote(b, block(o, y, x, k), ys.at[k, j], yr.at[k, o], to_y)

    def diag_copy(k, j, o, h):
        b = block(o, y, 1 - x, k, 0) if h == 0 else block(o, 1 - y, x, k, 1)
        return remote(b, b, ds_.at[k, j, h], dr.at[k, o, h], to_y if h == 0 else to_x)

    def core_copy(k, side, cc):
        yy, xx = side_of(side)
        b = dst.at[:, yy, xx, cc, span(k)]
        return remote(b, b, cs.at[k, side], cr.at[k, side], to_c)

    def z_land(k):
        for j, o in places[1:]:
            b = block(o, y, x, k)
            remote(b, b, zs.at[k, j], zr.at[k, o], me.at(z=o)).wait_recv()
            x_copy(k, j, o, b).start()
            y_copy(k, j, o, b).start()
        core_copy(k, 0, c).start()

    def xy_land(k):
        for j, o in places:
            b = block(o, y, 1 - x, k)
            remote(b, b, xs.at[k, j], xr.at[k, o], to_x).wait_recv()
            diag_copy(k, j, o, 0).start()
            b = block(o, 1 - y, x, k)
            remote(b, b, ys.at[k, j], yr.at[k, o], to_y).wait_recv()
            diag_copy(k, j, o, 1).start()
        core_copy(k, 1, c).start()
        core_copy(k, 2, c).start()

    def diag_land(k):
        for j, o in places:
            for h, w in ((0, to_y), (1, to_x)):
                b = block(o, 1 - y, 1 - x, k, h)
                remote(b, b, ds_.at[k, j, h], dr.at[k, o, h], w).wait_recv()
        core_copy(k, 3, c).start()

    def loads(k, side):
        yy, xx = side_of(side)
        return (
            pltpu.make_async_copy(dst.at[:, yy, xx, :, span(k)], h_in.at[side], hs.at[side]),
            pltpu.make_async_copy(cots.at[:, yy, xx, :, span(k)], c_in.at[side], cins.at[side]),
        )

    def fetch(k, side):
        core_copy(k, side, 1 - c).wait_recv()
        for copy in loads(k, side):
            copy.start()

    def stores(k, side):
        yy, xx = side_of(side)
        pairs = ((hid_out, hid), (in_out, in_d), (g_out, gate_g), (part_out, parts))
        return [
            pltpu.make_async_copy(v.at[side], ref.at[:, yy, xx, :, span(k)], sts.at[side, i])
            for i, (v, ref) in enumerate(pairs)
        ]

    def unit(k, side):
        for copy in loads(k, side):
            copy.wait()
        h = h_in[side, :, :, :, :width].reshape(units, width)
        gates = h_in[side, :, :, :, width : width + 128].reshape(units, 128)
        late = h_in[side, :, :, :, width + 128 :].reshape(units, width - early)
        scale = jnp.dot(gates, spread[...], preferred_element_type=F32)
        both = nt(h, w_in[...])
        down = nt(c_in[side].reshape(units, early), w_down[:, :early])
        down = down + nt(late, w_down[:, early:])
        columns = lax.broadcasted_iota(jnp.int32, (units, 128), 1)
        sums = jnp.zeros((units, 128), F32)
        for i, (begin, size) in enumerate(spans):
            at = slice(begin, begin + size)
            up_at = slice(inner + begin, inner + begin + size)
            g, u, d = both[:, at], both[:, up_at], down[:, at]
            sig = 1.0 / (1.0 + jnp.exp(-g))
            act = g * sig
            value = (act * u).astype(BF).astype(F32)
            shape = (lines, 2, step_rows, size)
            if i < local_experts:
                total = jnp.sum(value * d, axis=1, keepdims=True)
                sums = jnp.where(columns == expert_at * local_experts + i, total, sums)
                value = value * scale[:, at]
                d = d * scale[:, at]
            hid_out[side, :, :, :, at] = value.astype(BF).reshape(shape)
            in_out[side, :, :, :, at] = (
                (d * u * (sig + act * (1.0 - sig))).astype(BF).reshape(shape)
            )
            in_out[side, :, :, :, up_at] = (d * act).astype(BF).reshape(shape)
        g_out[side] = sums.astype(BF).reshape(lines, 2, step_rows, 128)
        hidden = hid_out[side].reshape(units, inner)
        for begin in range(0, width, 512):
            at = slice(begin, begin + 512)
            part = jnp.dot(hidden, w_down[:, at], preferred_element_type=F32)
            part_out[side, :, :, :, at] = part.astype(BF).reshape(lines, 2, step_rows, 512)
        for copy in stores(k, side):
            copy.start()

    def z_start(k):
        for j, o in enumerate(others):
            z_copy(k, j, o).start()

    z_start(0)
    for k in range(chunks):
        x_copy(k, lines - 1, z, piece(k)).start()
        y_copy(k, lines - 1, z, piece(k)).start()

    fills = []
    for i, (begin, size) in enumerate(spans):
        for target, start, source in (
            (w_in, 0, e_gate.at[i] if i < local_experts else s_in.at[0]),
            (w_in, inner, e_up.at[i] if i < local_experts else s_in.at[1]),
            (w_down, 0, e_down.at[i] if i < local_experts else s_down),
        ):
            held = source.shape[0]
            fills.append(
                pltpu.make_async_copy(
                    source, target.at[pl.ds(start + begin, held)], w_sem.at[2 + len(fills)]
                )
            )
            fills[-1].start()
            if size > held:
                target[start + begin + held : start + begin + size] = jnp.zeros(
                    (size - held, width), BF
                )
    for copy in fills:
        copy.wait()
    keep = pltpu.make_async_copy(w_in, w_in_out, w_sem.at[0])
    keep.start()

    own.wait()
    z_land(0)
    if chunks > 1:
        z_start(1)
    fetch(0, 0)
    valid = lambda k: (k >= 0) & (k < chunks)

    @pl.loop(0, chunks + 2)
    def _(t):
        @pl.loop(0, 4)
        def _(side):
            k = t - (side + 1) // 2

            @pl.when(valid(k))
            def _():
                @pl.when(k >= 1)
                def _():
                    for copy in stores(k - 1, side):
                        copy.wait()

                unit(k, side)

            @pl.when((side == 0) & valid(t - 1))
            def _():
                fetch(t - 1, 2)

            @pl.when((side == 1) & valid(t - 2))
            def _():
                fetch(t - 2, 3)

        @pl.when(valid(t + 1))
        def _():
            z_land(t + 1)

        @pl.when(valid(t + 2))
        def _():
            z_start(t + 2)

        @pl.when(valid(t))
        def _():
            xy_land(t)

        @pl.when(valid(t + 1))
        def _():
            fetch(t + 1, 0)

        @pl.when(valid(t - 1))
        def _():
            diag_land(t - 1)

        @pl.when(valid(t))
        def _():
            fetch(t, 1)

    keep.wait()
    for side in range(4):
        for copy in stores(chunks - 1, side):
            copy.wait()

    @pl.loop(0, chunks)
    def _(k):
        for j, o in enumerate(others):
            z_copy(k, j, o).wait_send()
        for j, o in places:
            b = piece(k) if j == lines - 1 else block(o, y, x, k)
            x_copy(k, j, o, b).wait_send()
            y_copy(k, j, o, b).wait_send()
            diag_copy(k, j, o, 0).wait_send()
            diag_copy(k, j, o, 1).wait_send()
        for side in range(4):
            core_copy(k, side, c).wait_send()


def gather_hidden(
    value, cots, spread, e_gate, e_up, e_down, s_in, s_down, spans, local_experts, lines, ident
):
    rows, wide = value.shape
    width, early = e_down.shape[2], cots.shape[1]
    inner = spans[-1][0] + spans[-1][1]
    step_rows = min(rows, max(16, 128 // lines))
    chunks = rows // step_rows
    lead = (lines, 2, 2, 2, rows)
    dma = pltpu.SemaphoreType.DMA
    slot = lambda n: pltpu.VMEM((4, lines, 2, step_rows, n), BF)
    line = dma((chunks, lines))
    return pl.pallas_call(
        functools.partial(hidden_kernel, lines, chunks, spans, local_experts),
        out_shape=[
            jax.ShapeDtypeStruct(lead + (n,), BF) for n in (wide, inner, 2 * inner, 128)
        ]
        + [
            jax.ShapeDtypeStruct((2 * inner, width), BF),
            jax.ShapeDtypeStruct(lead + (width,), BF),
        ],
        in_specs=[HBM, HBM, VMEM] + [HBM] * 5,
        out_specs=[HBM] * 6,
        scratch_shapes=[
            slot(wide), slot(early), slot(inner), slot(2 * inner), slot(128), slot(width),
            pltpu.VMEM((2 * inner, width), BF), pltpu.VMEM((inner, width), BF),
            dma((2 + 3 * len(spans),)), dma, dma((4,)), dma((4,)), dma((4, 4)),
            line, line, line, line, line, line,
            dma((chunks, lines, 2)), dma((chunks, lines, 2)), dma((chunks, 4)), dma((chunks, 4)),
        ],
        compiler_params=pltpu.CompilerParams(
            collective_id=ident, has_side_effects=True, vmem_limit_bytes=60 << 20
        ),
    )(value, cots.reshape(lead + (early,)), spread, e_gate, e_up, e_down, s_in, s_down)


def back_kernel(
    lines,
    in_d, gate_g, w_in, passed,
    out, passed_on,
    d_in, g_in, sbuf, acc, cbuf, xbuf, ybuf, zbuf, xdiag, ydiag,
    ins, cs, cr, xs, xr, ys, yr, zs, zr, xds, xdr, yds, ydr,
):
    me = Place()
    z, y, x, c = me.z, me.y, me.x, me.c
    rows, wide = out.shape
    width = wide - 128
    half = wide // 256 * 128
    others = [lax.rem(z + 1 + j, lines) for j in range(lines - 1)]
    to_x, to_y, to_c = me.at(x=1 - x), me.at(y=1 - y), me.at(c=1 - c)
    greet([me.at(z=o) for o in others] + [to_x, to_y, to_c])
    cols = (pl.ds(0, half), pl.ds(half, wide - half))
    lag = (0, 1, 1, 2)
    place = lambda n: lax.rem(z + 1 + n, lines)

    def side_of(side):
        return (
            lax.rem(y + 1 - side // 2, 2),
            lax.rem(x + 1 - lax.rem(side, 2), 2),
        )

    def loads(n, side):
        yy, xx = side_of(side)
        pairs = ((in_d, d_in), (gate_g, g_in))
        return [
            pltpu.make_async_copy(ref.at[place(n), yy, xx], v.at[side], ins.at[side, i])
            for i, (ref, v) in enumerate(pairs)
        ]

    def to_core(n, side):
        yy, xx = side_of(side)
        return remote(
            sbuf.at[side], cbuf.at[place(n), yy, xx], cs.at[side], cr.at[n, side], to_c
        )

    def unit(n, side):
        yy, xx = side_of(side)
        for copy in loads(n, side):
            copy.wait()
        grads = d_in[side].reshape(2 * rows, w_in.shape[0])
        piece = 512
        for begin in range(0, width, piece):
            at = slice(begin, begin + piece)
            back = jnp.dot(grads, w_in[:, at], preferred_element_type=F32).astype(BF).reshape(2, rows, piece)

            @pl.when(c == 0)
            def _():
                acc[place(n), yy, xx, :, at] = back[0]
                sbuf[side, :, at] = back[1]

            @pl.when(c == 1)
            def _():
                acc[place(n), yy, xx, :, at] = back[1]
                sbuf[side, :, at] = back[0]

        acc[place(n), yy, xx, :, width:] = g_in[side, c]
        sbuf[side, :, width:] = g_in[side, 1 - c]

    def sums(target, *terms):
        @pl.loop(0, rows // 16)
        def _(i):
            at = pl.ds(pl.multiple_of(i * 16, 16), 16)
            total = terms[0][at].astype(F32)
            for term in terms[1:]:
                total = total + term[at].astype(F32)
            target[at] = total.astype(BF)

    def diag_sends(n):
        o = place(n)
        far = acc.at[o, 1 - y, 1 - x]
        return (
            remote(far.at[:, cols[0]], xdiag.at[o], xds.at[n], xdr.at[n], to_x),
            remote(far.at[:, cols[1]], ydiag.at[o], yds.at[n], ydr.at[n], to_y),
        )

    def side_sends(n):
        o = place(n)
        return (
            remote(acc.at[o, y, 1 - x], xbuf.at[o], xs.at[n], xr.at[n], to_x),
            remote(acc.at[o, 1 - y, x], ybuf.at[o], ys.at[n], yr.at[n], to_y),
        )

    def z_copy(n):
        return remote(
            acc.at[place(n), y, x], zbuf.at[z], zs.at[n], zr.at[z], me.at(z=place(n))
        )

    def first(n):
        to_core(n, 0).wait_recv()
        mine, other = acc.at[place(n), 1 - y, 1 - x], cbuf.at[place(n), 1 - y, 1 - x]
        sums(mine, mine, other)
        for copy in diag_sends(n):
            copy.start()

    def second(n):
        o = place(n)
        mine, other = acc.at[o, 1 - y, x], cbuf.at[o, 1 - y, x]
        to_core(n, 1).wait_recv()
        diag_sends(n)[0].wait_recv()
        sums(mine.at[:, cols[0]], mine.at[:, cols[0]], other.at[:, cols[0]], xdiag.at[o])
        sums(mine.at[:, cols[1]], mine.at[:, cols[1]], other.at[:, cols[1]])
        side_sends(n)[1].start()

    def third(n):
        o = place(n)
        mine, other = acc.at[o, y, 1 - x], cbuf.at[o, y, 1 - x]
        to_core(n, 2).wait_recv()
        diag_sends(n)[1].wait_recv()
        sums(mine.at[:, cols[0]], mine.at[:, cols[0]], other.at[:, cols[0]])
        sums(mine.at[:, cols[1]], mine.at[:, cols[1]], other.at[:, cols[1]], ydiag.at[o])
        side_sends(n)[0].start()

    def fourth(n):
        o = place(n)
        mine, other = acc.at[o, y, x], cbuf.at[o, y, x]
        to_core(n, 3).wait_recv()
        for copy in side_sends(n):
            copy.wait_recv()
        sums(mine, mine, other, xbuf.at[o], ybuf.at[o])

        @pl.when(n < lines - 1)
        def _():
            z_copy(n).start()

    valid = lambda n: (n >= 0) & (n < lines)
    for side in range(4):
        for copy in loads(0, side):
            copy.start()

    @pl.loop(0, lines + 3)
    def _(t):
        @pl.loop(0, 4)
        def _(side):
            n = t - (side + 1) // 2

            @pl.when(valid(n))
            def _():
                @pl.when(n >= 1)
                def _():
                    to_core(n - 1, side).wait_send()

                unit(n, side)
                to_core(n, side).start()

                @pl.when(n + 1 < lines)
                def _():
                    for copy in loads(n + 1, side):
                        copy.start()

            for turn, (behind, act) in enumerate(((3, fourth), (0, first), (1, second), (1, third))):

                @pl.when((side == turn) & valid(t - behind))
                def _(behind=behind, act=act):
                    act(t - behind)

    for side in range(4):
        to_core(lines - 1, side).wait_send()
    for o in others:
        remote(zbuf.at[o], zbuf.at[o], zs.at[0], zr.at[o], me.at(z=o)).wait_recv()

    @pl.loop(0, rows // 16)
    def _(i):
        at = pl.ds(pl.multiple_of(i * 16, 16), 16)
        total = acc[z, y, x, at].astype(F32)
        for o in others:
            total = total + zbuf[o, at].astype(F32)
        out[at] = total

    @pl.loop(0, lines)
    def _(n):
        for copy in diag_sends(n) + side_sends(n):
            copy.wait_send()

        @pl.when(n < lines - 1)
        def _():
            z_copy(n).wait_send()


def layout_kernel(own_heads, q, kvb, kva, o, shared, q_out, kvb_out, kva_out, o_out, gate_out, up_out):
    for source, target in ((q, q_out), (kvb, kvb_out)):
        size = source.shape[3] // own_heads
        held = [[source[xx, cc].astype(F32) for cc in range(2)] for xx in range(2)]
        pieces = [
            held[xx][cc][:, i * size : (i + 1) * size]
            for i in range(own_heads)
            for cc in range(2)
            for xx in range(2)
        ]
        target[...] = jnp.concatenate(pieces, axis=1)
    kva_out[...] = kva[...].astype(F32)
    o_out[...] = o[...].astype(F32)
    for which, target in enumerate((gate_out, up_out)):
        pieces = [shared[i, which].astype(F32) for i in range(shared.shape[0])]
        target[...] = jnp.concatenate(pieces, axis=1)


def lay_out(q, kvb, kva, o, shared, own_heads):
    flat = lambda rows, columns: jax.ShapeDtypeStruct((rows, columns), F32)
    hidden = shared.shape[0] * shared.shape[3]
    return pl.pallas_call(
        functools.partial(layout_kernel, own_heads),
        out_shape=[
            flat(q.shape[2], 4 * q.shape[3]),
            flat(kvb.shape[2], 4 * kvb.shape[3]),
            flat(*kva.shape),
            flat(*o.shape),
            flat(shared.shape[2], hidden),
            flat(shared.shape[2], hidden),
        ],
        in_specs=[VMEM] * 5,
        out_specs=[VMEM] * 6,
        compiler_params=pltpu.CompilerParams(vmem_limit_bytes=32 << 20),
    )(q, kvb, kva, o, shared)


def sum_back(in_d, gate_g, w_in, passed, ident):
    lines, rows, inner = in_d.shape[0], in_d.shape[4], in_d.shape[5]
    width = w_in.shape[1]
    wide = width + 128
    half = wide // 256 * 128
    dma = pltpu.SemaphoreType.DMA
    buf = lambda *shape: pltpu.VMEM(shape, BF)
    line = dma((lines,))
    return pl.pallas_call(
        functools.partial(back_kernel, lines),
        out_shape=[
            jax.ShapeDtypeStruct((rows, wide), F32),
            jax.ShapeDtypeStruct(passed.shape, passed.dtype),
        ],
        in_specs=[HBM] * 2 + [VMEM, HBM],
        out_specs=[VMEM, HBM],
        input_output_aliases={3: 1},
        scratch_shapes=[
            buf(4, 2, rows, inner), buf(4, 2, rows, 128), buf(4, rows, wide),
            buf(lines, 2, 2, rows, wide), buf(lines, 2, 2, rows, wide),
            buf(lines, rows, wide), buf(lines, rows, wide), buf(lines, rows, wide),
            buf(lines, rows, half), buf(lines, rows, wide - half),
            dma((4, 2)), dma((4,)), dma((lines, 4)),
            line, line, line, line, line, line, line, line, line, line,
        ],
        compiler_params=pltpu.CompilerParams(
            collective_id=ident, has_side_effects=True, vmem_limit_bytes=60 << 20
        ),
    )(in_d, gate_g, w_in, passed)


def on_device(
    tokens,
    cotangent,
    norm1_gain,
    q_weight,
    kva_weight,
    kv_gain,
    kvb_weight,
    o_weight,
    norm2_gain,
    router_weight,
    shared_gate,
    shared_up,
    shared_down,
    expert_gate,
    expert_up,
    expert_down,
    expert_ids,
    token_rank,
    seq_ids,
):
    expert_count = lax.axis_size("expert")
    shard_count = lax.axis_size("shard")
    device_count = expert_count * shard_count
    expert_at = lax.axis_index("expert")
    shard_at = lax.axis_index("shard")
    tok_rows, width = tokens.shape
    group_len = seq_ids.shape[0]
    local_experts = expert_gate.shape[0]
    all_experts = local_experts * expert_count
    top_count = expert_ids.shape[1]
    capacity = max(2, tok_rows * top_count // all_experts)
    score_scale = (NOPE + ROPE) ** (-0.5)
    own_heads = HEADS // shard_count
    latent_width = kva_weight.shape[1]

    lines = expert_count // 2
    o_rows = o_weight.shape[0]
    o_pairs = VDIM == 2 * o_rows

    def by_head(weight):
        rows = weight.shape[0]
        heads = weight.reshape(rows, own_heads, 2, 2, weight.shape[1] // HEADS)
        return heads.transpose(3, 2, 0, 1, 4).reshape(2, 2, rows, weight.shape[1] // 4)

    small = [norm1_gain, norm2_gain, kv_gain, router_weight]
    small_sizes = [v.size for v in small]

    def pack(values):
        flat = jnp.concatenate(values, axis=-1)
        pad = -flat.shape[-1] % 2048
        flat = jnp.pad(flat, [(0, 0)] * (flat.ndim - 1) + [(0, pad)])
        return flat.reshape(flat.shape[:-1] + (-1, 128))

    def unpack(packed):
        flat = packed.reshape(packed.shape[:-2] + (-1,))
        starts = [sum(small_sizes[:i]) for i in range(len(small_sizes))]
        return [flat[..., b : b + n] for b, n in zip(starts, small_sizes)]

    shared_width = shared_down.shape[0]
    both_shared = jnp.stack([shared_gate, shared_up]).reshape(
        2, shared_gate.shape[0], device_count, shared_width
    )
    both_shared = lax.all_to_all(
        both_shared.transpose(2, 0, 1, 3), BOTH, split_axis=0, concat_axis=0
    )
    both_shared = both_shared.transpose(1, 0, 2, 3).reshape(2, width, shared_width)
    small_own = pack([v.reshape(-1) for v in small])
    rounds = max(1, tok_rows * device_count // 4096)
    started = start_gather(
        tokens,
        [kva_weight],
        [1],
        [
            jnp.broadcast_to(small_own, (2, 2) + small_own.shape),
            by_head(kvb_weight),
            by_head(q_weight),
        ],
        o_weight if o_pairs else None,
        lines,
        1,
    )
    group_tokens = started[0].reshape(group_len, width)
    kva_all = started[1].reshape(width, latent_width)
    small_set, kvb_set, q_set, *o_set = started[2:]
    small_all = unpack(small_set.reshape((device_count,) + small_own.shape))
    kvb_mine = kvb_set.reshape(KV_RANK, -1)
    q_mine = q_set.reshape(width, -1)
    core_at, x_at = shard_at % 2, shard_at // 2
    if o_pairs:
        o_mine = o_set[0].reshape(own_heads * VDIM, width)
    else:
        o_mine = gather(o_weight, BOTH).reshape(own_heads, 2, 2, VDIM, width)
        o_mine = o_mine[:, core_at, x_at].reshape(own_heads * VDIM, width)
    norm1_scale, norm2_scale, latent_scale = [v.reshape(-1).astype(F32) for v in small_all[:3]]
    router = small_all[3].reshape(width, all_experts)

    positions = positions_of(seq_ids)
    cosine_table, sine_table = rope_tables(positions, ROPE)
    token_index = jnp.arange(group_len, dtype=jnp.int32)
    allowed = (token_index[None, :] <= token_index[:, None]) & (
        (seq_ids[None, :] == 0) | (seq_ids[None, :] == seq_ids[:, None])
    )
    input_rows = tokens.astype(F32)
    group_rows = group_tokens.astype(F32)
    normed_group, inverse_group = rms_forward(group_rows, norm1_scale)
    hidden_one = normed_group.astype(BF)
    query_raw = mm(hidden_one, q_mine).reshape(group_len, own_heads, NOPE + ROPE)
    q_nope = query_raw[:, :, :NOPE].astype(BF)
    q_rope = rotate(
        query_raw[:, :, NOPE:], cosine_table[:, None, :], sine_table[:, None, :]
    ).astype(BF)
    compressed = mm(hidden_one, kva_all)
    latent_norm, inverse_latent = rms_forward(compressed[:, :KV_RANK], latent_scale)
    latent = latent_norm.astype(BF)
    k_rope = rotate(compressed[:, KV_RANK:], cosine_table, sine_table).astype(BF)
    keyval = mm(latent, kvb_mine).astype(BF).reshape(group_len, own_heads, NOPE + VDIM)
    keys = keyval[:, :, :NOPE]
    values = keyval[:, :, NOPE:]
    scores = jnp.einsum("qhd,khd->hqk", q_nope, keys, preferred_element_type=F32)
    scores = scores + jnp.einsum("qhd,kd->hqk", q_rope, k_rope, preferred_element_type=F32)
    scores = jnp.where(allowed[None], scores * score_scale, NEGATIVE)
    top_score = jnp.max(scores, axis=-1, keepdims=True)
    log_total = top_score + jnp.log(jnp.sum(jnp.exp(scores - top_score), axis=-1, keepdims=True))
    soft_probs = jnp.exp(scores - log_total)
    prob_low = soft_probs.astype(BF)
    attended = (
        jnp.einsum("hqk,khd->qhd", prob_low, values, preferred_element_type=F32)
        .astype(BF)
        .reshape(group_len, own_heads * VDIM)
    )
    projected = sum_group(mm(attended, o_mine).astype(BF), 2)
    mixed = input_rows + projected

    normed_two, inverse_two = rms_forward(mixed, norm2_scale)
    hidden_two = normed_two.astype(BF)
    logits = mm(hidden_two, router)
    choice_hot = (
        expert_ids[:, :, None] == jnp.arange(all_experts, dtype=jnp.int32)[None, None, :]
    ).astype(F32)
    chosen = jnp.sum(choice_hot * logits[:, None, :], axis=-1)
    gate_probs = jax.nn.softmax(chosen, axis=-1)
    kept = kept_pairs(expert_ids, token_rank, choice_hot, capacity)
    gate_table = jnp.sum(choice_hot * (gate_probs * kept)[:, :, None], axis=1)

    own_width = expert_gate.shape[2]
    sizes = [own_width + -own_width % 128] * local_experts + [shared_width + -shared_width % 128]
    spans = tuple((sum(sizes[:i]), size) for i, size in enumerate(sizes))

    spare = -shared_width % 128
    shared_in = jnp.pad(both_shared.swapaxes(1, 2), ((0, 0), (0, spare), (0, 0)))
    shared_out = jnp.pad(shared_down, ((0, spare), (0, 0)))
    unit_expert = jnp.concatenate(
        [jnp.full((size,), expert_at * local_experts + i) for i, size in enumerate(sizes[:-1])]
        + [jnp.full((sizes[-1],), -1)]
    )
    column = jnp.arange(128)[:, None]
    spread = (
        (column == unit_expert) | ((column == unit_expert + all_experts) & (unit_expert >= 0))
    ).astype(BF)

    early = width // 2

    def ffn(rows, cots, table):
        cots_all = gather(cots[:, :early] + 0 * group_tokens[0, 0], BOTH)
        high = table.astype(BF)
        low = (table - high.astype(F32)).astype(BF)
        spare = jnp.zeros((table.shape[0], 128 - 2 * all_experts), BF)
        values, hid, in_d, gate_g, w_in, out_part = gather_hidden(
            jnp.concatenate([rows, high, low, spare, cots[:, early:]], axis=1),
            cots_all,
            spread,
            expert_gate.swapaxes(1, 2),
            expert_up.swapaxes(1, 2),
            expert_down,
            shared_in,
            shared_out,
            spans,
            local_experts,
            lines,
            3,
        )
        back_sum, out_part = sum_back(in_d, gate_g, w_in, out_part, 4)
        flat = lambda v: v.reshape(cots_all.shape[0], -1)
        work = [flat(values), cots_all, flat(in_d), flat(hid)]
        return scatter_sum(flat(out_part), BOTH), back_sum, work

    tail = spans[-1][0]
    inner = tail + spans[-1][1]
    expert_spans = tuple(span + (own_width,) for span in spans[:-1])
    shared_spans = (spans[-1] + (shared_width,),)
    if rounds == 1:
        out_sum, back_sum, work = ffn(hidden_two, cotangent, gate_table)
    else:

        def one_round(total, part):
            out_rows, back_rows, (values, cots, in_d, hid) = ffn(*part)
            rows = values[:, :width]
            cots = jnp.concatenate([cots, values[:, width + 128 :]], axis=1)
            grads = [mm_tn(in_d, rows), mm_tn(hid, cots)]
            return [t + g for t, g in zip(total, grads)], (out_rows, back_rows)

        in_rounds = lambda value: value.reshape((rounds, -1) + value.shape[1:])
        zeros = [jnp.zeros((2 * inner, width), F32), jnp.zeros((inner, width), F32)]
        (w_in_grad, w_down_grad), (out_sum, back_sum) = lax.scan(
            one_round, zeros, (in_rounds(hidden_two), in_rounds(cotangent), in_rounds(gate_table))
        )
        out_sum = out_sum.reshape((tok_rows,) + out_sum.shape[2:])
        back_sum = back_sum.reshape((tok_rows,) + back_sum.shape[2:])
        w_in_grad = w_in_grad.reshape(2, inner, width)
        cut = lambda grad: jnp.stack(
            [grad[spans[i][0] : spans[i][0] + own_width] for i in range(local_experts)]
        )
        expert_grads = [cut(w_in_grad[0]), cut(w_in_grad[1]), cut(w_down_grad)]
        shared_made = [v[tail : tail + shared_width] for v in (*w_in_grad, w_down_grad)]
        work = None
    out_sum, back_sum = out_sum.astype(F32), back_sum.astype(F32)
    output = (mixed + out_sum).astype(BF)

    upstream = cotangent.astype(F32)
    gate_grad = jnp.sum(
        choice_hot * back_sum[:, None, width : width + all_experts], axis=-1
    ) * kept
    chosen_grad = gate_probs * (gate_grad - jnp.sum(gate_probs * gate_grad, axis=-1, keepdims=True))
    logit_grad = jnp.sum(choice_hot * chosen_grad[:, :, None], axis=1).astype(BF)
    router_part = mm_tn(hidden_two, logit_grad)
    hidden_two_grad = back_sum[:, :width] + mm_nt(logit_grad, router)
    mixed_norm_grad, norm2_part = rms_backward(mixed, inverse_two, norm2_scale, hidden_two_grad)
    mixed_grad = upstream + mixed_norm_grad

    mixed_grad_group, *made = gather_group(mixed_grad.astype(BF), 5, work, shared_spans, lines)
    if work:
        shared_made = [v[0] for v in made]
    shared_grad = jnp.stack(shared_made[:2]).astype(BF)
    shared_grad = shared_grad.reshape(2, shared_width, device_count, -1).transpose(2, 0, 3, 1)
    shared_grad = lax.all_to_all(shared_grad, BOTH, split_axis=0, concat_axis=0)
    sdown_grad = shared_made[2]
    o_part = mm_tn(attended, mixed_grad_group)
    attended_grad = (
        mm_nt(mixed_grad_group, o_mine).astype(BF).reshape(group_len, own_heads, VDIM)
    )
    prob_grad = jnp.einsum("qhd,khd->hqk", attended_grad, values, preferred_element_type=F32)
    values_grad = jnp.einsum("hqk,qhd->khd", prob_low, attended_grad, preferred_element_type=F32)
    score_grad = (
        soft_probs * (prob_grad - jnp.sum(soft_probs * prob_grad, axis=-1, keepdims=True))
    ).astype(BF)
    q_nope_grad = (
        jnp.einsum("hqk,khd->qhd", score_grad, keys, preferred_element_type=F32) * score_scale
    )
    q_rope_grad = (
        jnp.einsum("hqk,kd->qhd", score_grad, k_rope, preferred_element_type=F32) * score_scale
    )
    keys_grad = (
        jnp.einsum("hqk,qhd->khd", score_grad, q_nope, preferred_element_type=F32) * score_scale
    )
    rope_grad = (
        jnp.einsum("hqk,qhd->kd", score_grad, q_rope, preferred_element_type=F32) * score_scale
    )
    keyval_grad = (
        jnp.concatenate([keys_grad, values_grad], axis=-1)
        .reshape(group_len, own_heads * (NOPE + VDIM))
        .astype(BF)
    )
    kvb_part = mm_tn(latent, keyval_grad)
    latent_raw_part, kv_gain_part = rms_backward(
        compressed[:, :KV_RANK], inverse_latent, latent_scale, mm_nt(keyval_grad, kvb_mine)
    )
    compressed_part = jnp.concatenate(
        [latent_raw_part, rotate(rope_grad, cosine_table, -sine_table)], axis=1
    ).astype(BF)
    query_grad = jnp.concatenate(
        [q_nope_grad, rotate(q_rope_grad, cosine_table[:, None, :], -sine_table[:, None, :])],
        axis=-1,
    )
    query_grad = query_grad.reshape(group_len, own_heads * (NOPE + ROPE)).astype(BF)
    q_part = mm_tn(hidden_one, query_grad)
    kva_part = mm_tn(hidden_one, compressed_part)
    hidden_one_part = mm_nt(query_grad, q_mine) + mm_nt(compressed_part, kva_all)
    norm1_part = jnp.sum(hidden_one_part * (group_rows * inverse_group), axis=0)

    def from_heads(parts):
        rows = parts.shape[2]
        heads = parts.reshape(2, 2, rows, own_heads, -1).transpose(2, 3, 1, 0, 4)
        return heads.reshape(rows, -1).astype(F32)

    line_shape = (lines, 2)
    small_parts = pack(
        [v.reshape(device_count, -1) for v in (norm1_part, norm2_part, kv_gain_part, router_part)]
    )
    parts = [
        kvb_part.astype(BF).reshape(line_shape + (2, 2, kvb_weight.shape[0], -1)),
        kva_part.astype(BF).reshape(line_shape + (2, 2, width // device_count, latent_width)),
        q_part.astype(BF).reshape(line_shape + (2, 2, q_weight.shape[0], q_mine.shape[1])),
        small_parts.reshape(line_shape + (2, 2) + small_parts.shape[1:]),
    ]
    o_part = o_part.astype(BF).reshape(own_heads, VDIM, width)
    if o_pairs:
        o_sum = o_part.reshape(own_heads, 2, o_rows, width)
    else:
        o_sum = None
        o_wide = jnp.zeros((own_heads, 2, 2, VDIM, width), BF).at[:, core_at, x_at].set(o_part)
        o_grad = scatter_sum(o_wide.reshape(HEADS * VDIM, width), BOTH).astype(F32)
    summed = sum_grads(
        parts,
        1,
        hidden_one_part.astype(BF).reshape(2, 2, tok_rows, width),
        o_sum,
        lines,
        9,
        work,
        expert_spans,
    )
    _, inverse_one = rms_forward(input_rows, norm1_scale)
    input_norm_grad, _ = rms_backward(input_rows, inverse_one, norm1_scale, summed[4])
    tokens_grad = mixed_grad + input_norm_grad
    if work:
        expert_grads = summed[-3:]
    norm1_grad, norm2_grad, kv_gain_grad, router_grad = unpack(jnp.sum(summed[3], axis=(0, 1)))
    router_grad = router_grad.reshape(router_weight.shape)
    if o_pairs:
        q_grad, kvb_grad, kva_grad, o_grad, sgate_grad, sup_grad = lay_out(
            summed[2], summed[0], summed[1], summed[5], shared_grad, own_heads
        )
    else:
        kvb_grad = from_heads(summed[0])
        kva_grad = summed[1].astype(F32)
        q_grad = from_heads(summed[2])
        sgate_grad, sup_grad = (
            shared_grad.astype(F32)
            .transpose(1, 2, 0, 3)
            .reshape(2, width // device_count, device_count * shared_width)
        )
    return (
        output,
        tokens_grad,
        norm1_grad,
        q_grad,
        kva_grad,
        kv_gain_grad,
        kvb_grad,
        o_grad,
        norm2_grad,
        router_grad,
        sgate_grad,
        sup_grad,
        sdown_grad,
        expert_grads[0].swapaxes(1, 2),
        expert_grads[1].swapaxes(1, 2),
        expert_grads[2],
    )


def solution(mesh):
    rows = P(BOTH, None)
    flat = P(BOTH)
    columns = P("expert", None, "shard")
    depth = P("expert", "shard", None)
    return jax.shard_map(
        on_device,
        mesh=mesh,
        in_specs=(
            rows,
            rows,
            flat,
            rows,
            rows,
            flat,
            rows,
            rows,
            flat,
            rows,
            rows,
            rows,
            rows,
            columns,
            columns,
            depth,
            rows,
            flat,
            P("expert"),
        ),
        out_specs=(
            rows,
            rows,
            flat,
            rows,
            rows,
            flat,
            rows,
            rows,
            flat,
            rows,
            rows,
            rows,
            rows,
            columns,
            columns,
            depth,
        ),
        check_vma=False,
    )
```

```python
import functools

import jax
import jax.numpy as jnp
from jax import lax
from jax.experimental import pallas as pl
from jax.experimental.pallas import tpu as pltpu
from jax.sharding import PartitionSpec as P

HEADS = 16
NOPE = 128
ROPE = 64
VDIM = 128
KV_RANK = 512
CONTS = 2


EPSILON = 1e-06
THETA = 10000.0
NEGATIVE = -1e30
BOTH = ("expert", "shard")
BF = jnp.bfloat16
F32 = jnp.float32


def rms_forward(values, gain_row):
    inverse = lax.rsqrt(jnp.mean(values * values, axis=-1, keepdims=True) + EPSILON)
    return (values * inverse * gain_row, inverse)


def rms_backward(values, inverse, gain_row, upstream):
    normed = values * inverse
    scaled = upstream * gain_row
    value_grad = inverse * (scaled - normed * jnp.mean(scaled * normed, axis=-1, keepdims=True))
    return (value_grad, jnp.sum(upstream * normed, axis=0))


def rope_tables(positions, width):
    half_width = width // 2
    frequency = THETA ** (-2.0 * jnp.arange(half_width, dtype=jnp.float32) / width)
    angles = positions.astype(jnp.float32)[:, None] * frequency[None, :]
    return (jnp.cos(angles), jnp.sin(angles))


def rotate(values, cosine_table, sine_table):
    half_width = values.shape[-1] // 2
    first_half = values[..., :half_width]
    second = values[..., half_width:]
    return jnp.concatenate(
        [
            first_half * cosine_table - second * sine_table,
            second * cosine_table + first_half * sine_table,
        ],
        axis=-1,
    )


def positions_of(group_ids):
    length = group_ids.shape[0]
    token_index = jnp.arange(length, dtype=jnp.int32)
    labels = jnp.arange(CONTS + 1, dtype=jnp.int32)
    member = (group_ids[:, None] == labels[None, :]).astype(jnp.int32)
    counts = jnp.sum(member, axis=0)
    starts = jnp.cumsum(counts) - counts
    start_of = jnp.sum(member * starts[None, :], axis=1)
    return token_index - start_of + jnp.where(group_ids > 0, counts[0], 0)


def kept_pairs(choice_ids, rank_row, choice_hot, capacity):
    row_count, top_count, expert_total = choice_hot.shape
    per_k = jnp.sum(choice_hot, axis=0)
    before_k = jnp.cumsum(per_k, axis=0) - per_k
    lower = (rank_row[None, :] < rank_row[:, None]).astype(F32)
    same_k = jnp.dot(
        lower.astype(BF),
        choice_hot.reshape(row_count, top_count * expert_total).astype(BF),
        preferred_element_type=F32,
    ).reshape(row_count, top_count, expert_total)
    place = jnp.sum((same_k + before_k[None]) * choice_hot, axis=-1)
    return (place < capacity).astype(F32)


def mm(a, b):
    return jnp.dot(a, b, preferred_element_type=F32)


def mm_nt(a, b):
    return lax.dot_general(a, b, (((1,), (1,)), ((), ())), preferred_element_type=F32)


def mm_tn(a, b):
    return lax.dot_general(a, b, (((0,), (0,)), ((), ())), preferred_element_type=F32)


def gather(value, axes):
    return lax.all_gather(value, axes, axis=0, tiled=True)


def scatter_sum(value, axes):
    return lax.psum_scatter(value, axes, scatter_dimension=0, tiled=True)


HBM = pl.BlockSpec(memory_space=pl.ANY)
VMEM = pl.BlockSpec(memory_space=pltpu.VMEM)


class Place:
    def __init__(self):
        e, s = lax.axis_index("expert"), lax.axis_index("shard")
        self.z, self.y, self.x, self.c = e // 2, e % 2, s // 2, s % 2

    def at(self, z=None, y=None, x=None, c=None):
        z = self.z if z is None else z
        y = self.y if y is None else y
        x = self.x if x is None else x
        c = self.c if c is None else c
        return {"expert": 2 * z + y, "shard": 2 * x + c}


def greet(partners):
    barrier = pltpu.get_barrier_semaphore()
    for partner in partners:
        pl.semaphore_signal(
            barrier, inc=1, device_id=partner, device_id_type=pl.DeviceIdType.MESH
        )
    pl.semaphore_wait(barrier, len(partners))


def remote(src, dst, send, recv, where):
    return pltpu.make_async_remote_copy(
        src_ref=src,
        dst_ref=dst,
        send_sem=send,
        recv_sem=recv,
        device_id=where,
        device_id_type=pl.DeviceIdType.MESH,
    )


def gather_group_kernel(cuts, spans, *refs):
    refs = list(refs)
    take = lambda n: [refs.pop(0) for _ in range(n)]
    (src,) = take(1)
    work = take(4) if spans else None
    (dst,) = take(1)
    made = take(3) if spans else None
    own_sem, send, recv = take(3)
    me = Place()
    x, c = me.x, me.c
    to_x, to_c = me.at(x=1 - x), me.at(c=1 - c)
    greet([to_x, to_c])
    cut = src.shape[0] // cuts
    span = lambda k: pl.ds(k * cut, cut)
    own = pltpu.make_async_copy(src, dst.at[x, c], own_sem)
    own.start()
    over_x = [
        remote(src.at[span(k)], dst.at[x, c, span(k)], send.at[0, k], recv.at[0, k], to_x)
        for k in range(cuts)
    ]
    for copy in over_x:
        copy.start()
    over_c = remote(src, dst.at[x, c], send.at[1, 0], recv.at[1, 0], to_c)
    over_c.start()
    if spans:
        turns, begin_work, work_turn = grad_worker(work, made, refs[:3], refs[3], spans)
        begin_work()

        @pl.loop(0, turns)
        def _(n):
            work_turn(n)

    relays = []
    for k in range(cuts):
        far = dst.at[1 - x, c, span(k)]
        remote(far, far, send.at[0, k], recv.at[0, k], to_x).wait_recv()
        relays.append(remote(far, far, send.at[2, k], recv.at[2, k], to_c))
        relays[-1].start()
    far = dst.at[x, 1 - c]
    remote(far, far, send.at[1, 0], recv.at[1, 0], to_c).wait_recv()
    for k in range(cuts):
        far = dst.at[1 - x, 1 - c, span(k)]
        remote(far, far, send.at[2, k], recv.at[2, k], to_c).wait_recv()
    own.wait()
    for copy in over_x + [over_c] + relays:
        copy.wait_send()


def gather_group(value, ident, work=None, spans=None, lines=None, cuts=4):
    rows, width = value.shape
    dma = pltpu.SemaphoreType.DMA
    inputs, in_specs = [value], [HBM]
    outs = [jax.ShapeDtypeStruct((2, 2, rows, width), value.dtype)]
    scratch = [dma, dma((3, cuts)), dma((3, cuts))]
    if work:
        inputs += work
        in_specs += [HBM] * 4
        shapes, buffers = work_shapes(work, spans, lines)
        outs += shapes
        scratch += buffers
    out, *made = pl.pallas_call(
        functools.partial(gather_group_kernel, cuts, spans if work else None),
        out_shape=outs,
        in_specs=in_specs,
        out_specs=[HBM] + [VMEM] * (len(outs) - 1),
        scratch_shapes=scratch,
        compiler_params=pltpu.CompilerParams(
            collective_id=ident, has_side_effects=True, vmem_limit_bytes=40 << 20
        ),
    )(*inputs)
    return [out.reshape(4 * rows, width)] + made


def sum_group_kernel(cuts, part, out, cbuf, xbuf, xsum, cs, cr, xs, xr):
    me = Place()
    x, c = me.x, me.c
    rows, width = out.shape
    cut = rows // cuts
    to_x, to_c = me.at(x=1 - x), me.at(c=1 - c)
    greet([to_x, to_c])
    span = lambda k: pl.ds(k * cut, cut)
    core = lambda k, far: remote(
        part.at[1 - x if far else x, 1 - c, span(k)],
        cbuf.at[far, span(k)],
        cs.at[k, far],
        cr.at[k, far],
        to_c,
    )
    over = lambda k: remote(xsum.at[span(k)], xbuf.at[span(k)], xs.at[k], xr.at[k], to_x)
    for k in range(cuts):
        core(k, 1).start()
    for k in range(cuts):
        core(k, 0).start()

    def add(k, target, one, two):
        @pl.loop(0, cut // 16)
        def _(i):
            at = pl.ds(pl.multiple_of(k * cut + i * 16, 16), 16)
            target[at] = (one[at].astype(F32) + two[at].astype(F32)).astype(target.dtype)

    for k in range(cuts):
        core(k, 1).wait_recv()
        add(k, xsum, part.at[1 - x, c], cbuf.at[1])
        over(k).start()
    for k in range(cuts):
        core(k, 0).wait_recv()
        add(k, out, part.at[x, c], cbuf.at[0])
    for k in range(cuts):
        over(k).wait_recv()
        add(k, out, out, xbuf)
    for k in range(cuts):
        core(k, 1).wait_send()
        core(k, 0).wait_send()
        over(k).wait_send()


def sum_group(part, ident, cuts=4):
    rows, width = part.shape[0] // 4, part.shape[1]
    dma = pltpu.SemaphoreType.DMA
    buf = lambda *lead: pltpu.VMEM(lead + (rows, width), part.dtype)
    return pl.pallas_call(
        functools.partial(sum_group_kernel, cuts),
        out_shape=jax.ShapeDtypeStruct((rows, width), F32),
        in_specs=[VMEM],
        out_specs=VMEM,
        scratch_shapes=[
            buf(2), buf(), buf(),
            dma((cuts, 2)), dma((cuts, 2)), dma((cuts,)), dma((cuts,)),
        ],
        compiler_params=pltpu.CompilerParams(
            collective_id=ident, has_side_effects=True, vmem_limit_bytes=32 << 20
        ),
    )(part.reshape(2, 2, rows, width))


def rows_loop(target, act):
    if len(target.shape) > 2:
        for i in range(target.shape[0]):
            rows_loop(target.at[i], lambda at, i=i: act((i,) + at))
        return
    rows = target.shape[0]
    step = 16 if rows % 16 == 0 else rows

    @pl.loop(0, rows // step)
    def _(i):
        act((pl.ds(pl.multiple_of(i * step, step), step),))


def add_blocks(target, one, two):
    def act(at):
        target[at] = (one[at].astype(F32) + two[at].astype(F32)).astype(target.dtype)

    rows_loop(target, act)


def add_three(target, one, two, three):
    def act(at):
        total = one[at].astype(F32) + two[at].astype(F32) + three[at].astype(F32)
        target[at] = total.astype(target.dtype)

    rows_loop(target, act)


class Copies:
    def __init__(self):
        self.started = []

    def go(self, copy):
        copy.start()
        self.started.append(copy)

    def finish(self):
        for copy in self.started:
            copy.wait_send()


class LineGather:
    def __init__(self, me, lines, block, sems):
        self.z, self.lines, self.block, self.sems = me.z, lines, block, sems
        self.to = (me.at(z=lax.rem(me.z + 1, lines)), me.at(z=lax.rem(me.z + lines - 1, lines)))

    def place(self, way, distance):
        return self.z - distance if way == 0 else self.z + distance

    def comes(self, way, distance):
        place = self.place(way, distance)
        return place >= 0 if way == 0 else place < self.lines

    def goes(self, way, distance):
        on = self.z + 1 < self.lines if way == 0 else self.z >= 1
        return on & self.comes(way, distance - 1)

    def hop(self, way, distance, place):
        ref = self.block(place)
        send, recv = self.sems[2 * way], self.sems[2 * way + 1]
        return remote(ref, ref, send.at[distance], recv.at[distance], self.to[way])

    def start(self):
        for way in range(2):

            @pl.when(self.goes(way, 1))
            def _(way=way):
                self.hop(way, 1, self.z).start()

    def land(self, distance, then=None):
        for way in range(2):
            place = self.place(way, distance)

            @pl.when(self.comes(way, distance))
            def _(way=way, place=place):
                self.hop(way, distance, place).wait_recv()

                @pl.when(self.goes(way, distance + 1))
                def _():
                    self.hop(way, distance + 1, place).start()

                if then is not None:
                    then(place)

    def finish(self):
        for distance in range(1, self.lines):
            for way in range(2):

                @pl.when(self.goes(way, distance))
                def _(way=way, distance=distance):
                    self.hop(way, distance, self.place(way, distance - 1)).wait_send()


def start_kernel(lines, with_o, *refs):
    jobs = 3
    refs = list(refs)
    take = lambda n: [refs.pop(0) for _ in range(n)]
    tok, kva = take(2)
    sources = take(jobs)
    o_src = take(1)[0] if with_o else None
    tok_dst, kva_dst = take(2)
    dests = take(jobs)
    o_dst = take(1)[0] if with_o else None
    own_sem, gs, gr, ys, yr, ts, tr, ks, kr = take(9)
    line_sems = [take(4) for _ in range(jobs + 1 + with_o)]
    if with_o:
        o_own, ocs, ocr = take(3)
    me = Place()
    z, y, x, c = me.z, me.y, me.x, me.c
    near = [(x, 1 - c), (1 - x, c), (1 - x, 1 - c)]
    to_near = [me.at(x=xx, c=cc) for xx, cc in near]
    to_y, to_x, to_c = me.at(y=1 - y), to_near[1], to_near[0]
    last, kva_at, o_at = jobs - 1, jobs, jobs + 1
    wide_lines = [
        LineGather(me, lines, lambda p, i=i: dests[i].at[p], line_sems[i]) for i in range(last)
    ]
    q_line = LineGather(me, lines, lambda p: dests[last].at[p, y], line_sems[last])
    kva_line = LineGather(me, lines, lambda p: kva_dst.at[p, y, x, c], line_sems[kva_at])
    greet([*q_line.to, to_y] + to_near)
    copies = Copies()
    go = copies.go

    def over_y(i, p):
        if i < last:
            block = dests[i].at[z, y]
        elif i == last:
            block = dests[i].at[p, y]
        elif i == kva_at:
            block = kva_dst.at[p, y, x, c]
        else:
            block = o_dst.at[p]
        return remote(block, block, ys.at[i, p], yr.at[i, p], to_y)

    def from_y(i, p):
        if i < last:
            block = dests[i].at[z, 1 - y]
        elif i == last:
            block = dests[i].at[p, 1 - y]
        elif i == kva_at:
            block = kva_dst.at[p, 1 - y, x, c]
        else:
            block = o_dst.at[p]
        return remote(block, block, ys.at[i, p], yr.at[i, p], to_y)

    locals_ = [
        pltpu.make_async_copy(sources[i].at[x, c], dests[i].at[z, y, x, c], own_sem.at[i])
        for i in range(jobs)
    ]
    locals_.append(pltpu.make_async_copy(kva, kva_dst.at[z, y, x, c], own_sem.at[jobs]))
    locals_.append(pltpu.make_async_copy(tok, tok_dst.at[x, c], own_sem.at[jobs + 1]))
    for copy in locals_:
        copy.start()
    for i in (last, *range(last)):
        for p in range(3):
            go(
                remote(
                    sources[i].at[near[p][0], near[p][1]],
                    dests[i].at[z, y, x, c],
                    gs.at[i, p],
                    gr.at[i, p],
                    to_near[p],
                )
            )
    if with_o:
        o_core = remote(o_src, o_dst.at[z, c], ocs, ocr, to_c)
        o_local = pltpu.make_async_copy(o_src, o_dst.at[z, c], o_own)
        o_line = LineGather(me, lines, lambda p: o_dst.at[p], line_sems[o_at])
        holder = c == y

        @pl.when(jnp.logical_not(holder))
        def _():
            o_core.start()

        @pl.when(holder)
        def _():
            o_local.start()

    go(remote(tok, tok_dst.at[x, c], ts.at[1], tr.at[1], to_x))
    go(remote(tok, tok_dst.at[x, c], ts.at[0], tr.at[0], to_c))

    def near_land(i):
        locals_[i].wait()
        for p in range(3):
            xx, cc = near[p]
            block = dests[i].at[z, y, xx, cc]
            remote(block, block, gs.at[i, p], gr.at[i, p], to_near[p]).wait_recv()

    locals_[jobs].wait()
    kva_line.start()
    go(over_y(kva_at, z))
    near_land(last)
    q_line.start()
    go(over_y(last, z))
    for i in range(last):
        near_land(i)
        go(over_y(i, z))
    if with_o:

        @pl.when(holder)
        def _():
            o_local.wait()
            block = o_dst.at[z, 1 - c]
            remote(block, block, ocs, ocr, to_c).wait_recv()
            o_line.start()
            over_y(o_at, z).start()

    for distance in range(1, lines):
        kva_line.land(distance, lambda p: over_y(kva_at, p).start())
    block = tok_dst.at[1 - x, c]
    remote(block, block, ts.at[1], tr.at[1], to_x).wait_recv()
    go(remote(block, block, ts.at[2], tr.at[2], to_c))
    for distance in range(1, lines):
        q_line.land(distance, lambda p: over_y(last, p).start())
        if with_o:

            @pl.when(holder)
            def _(distance=distance):
                o_line.land(distance, lambda p: over_y(o_at, p).start())

        if distance == 1:
            for p in range(lines):
                from_y(kva_at, p).wait_recv()
            plane = kva_dst.at[:, :, x, c]
            go(remote(plane, plane, ks.at[0], kr.at[0], to_x))
            go(remote(plane, plane, ks.at[1], kr.at[1], to_c))
        if distance == lines - 2:
            for i in range(last):
                from_y(i, z).wait_recv()
                wide_lines[i].start()
            plane = kva_dst.at[:, :, 1 - x, c]
            remote(plane, plane, ks.at[0], kr.at[0], to_x).wait_recv()
            go(remote(plane, plane, ks.at[2], kr.at[2], to_c))
    for distance in range(1, lines):
        for one in wide_lines:
            one.land(distance)
    for slot, xx in ((0, x), (2, 1 - x)):
        block = tok_dst.at[xx, 1 - c]
        remote(block, block, ts.at[slot], tr.at[slot], to_c).wait_recv()
    locals_[jobs + 1].wait()
    for p in range(lines):
        from_y(last, p).wait_recv()
    if with_o:

        @pl.when(jnp.logical_not(holder))
        def _():
            for p in range(lines):
                from_y(o_at, p).wait_recv()
            o_core.wait_send()

        @pl.when(holder)
        def _():
            for p in range(lines):
                over_y(o_at, p).wait_send()
            o_line.finish()

    for slot, xx in ((1, x), (2, 1 - x)):
        plane = kva_dst.at[:, :, xx, 1 - c]
        remote(plane, plane, ks.at[slot], kr.at[slot], to_c).wait_recv()
    for one in wide_lines + [q_line, kva_line]:
        one.finish()
    for i in (last, kva_at):
        for p in range(lines):

            @pl.when(z != p)
            def _(i=i, p=p):
                over_y(i, p).wait_send()

    copies.finish()


def start_gather(tokens, kva, column_parts, o_rows, lines, ident):
    jobs = len(column_parts)
    with_o = o_rows is not None
    inputs = [tokens, kva] + column_parts + ([o_rows] if with_o else [])
    shape = lambda lead, v: jax.ShapeDtypeStruct(lead + v.shape, v.dtype)
    outs = [shape((2, 2), tokens), shape((lines, 2, 2, 2), kva)]
    outs += [jax.ShapeDtypeStruct((lines, 2) + v.shape, v.dtype) for v in column_parts]
    if with_o:
        outs.append(shape((lines, 2), o_rows))
    dma = pltpu.SemaphoreType.DMA
    scratch = [
        dma((jobs + 2,)), dma((jobs, 3)), dma((jobs, 3)),
        dma((jobs + 2, lines)), dma((jobs + 2, lines)),
        dma((3,)), dma((3,)), dma((3,)), dma((3,)),
    ]
    scratch += [dma((lines,))] * (4 * (jobs + 1 + with_o))
    if with_o:
        scratch += [dma] * 3
    return pl.pallas_call(
        functools.partial(start_kernel, lines, with_o),
        out_shape=outs,
        in_specs=[HBM] * len(inputs),
        out_specs=[HBM] * len(outs),
        scratch_shapes=scratch,
        compiler_params=pltpu.CompilerParams(collective_id=ident, has_side_effects=True),
    )(*inputs)


def grad_worker(work, made, slots, ins, spans):
    values, cots, in_d, hid = work
    rows_in, cots_in, left_in = slots
    depth, width = rows_in.shape[1:]
    early = cots.shape[1]
    inner = hid.shape[1]
    turns = cots.shape[0] // depth
    first, units = spans[0][0], left_in.shape[3]

    def loads(n):
        at = pl.ds(pl.multiple_of(n * depth, depth), depth)
        slot = lax.rem(n, 2)
        pairs = (
            (values.at[at, pl.ds(0, width)], rows_in.at[slot]),
            (cots.at[at], cots_in.at[slot, :, pl.ds(0, early)]),
            (
                values.at[at, pl.ds(width + 128, width - early)],
                cots_in.at[slot, :, pl.ds(early, width - early)],
            ),
            (in_d.at[at, pl.ds(first, units)], left_in.at[slot, 0]),
            (in_d.at[at, pl.ds(inner + first, units)], left_in.at[slot, 1]),
            (hid.at[at, pl.ds(first, units)], left_in.at[slot, 2]),
        )
        return [
            pltpu.make_async_copy(src, dst, ins.at[slot, i]) for i, (src, dst) in enumerate(pairs)
        ]

    def begin():
        for copy in loads(0):
            copy.start()
        for ref in made:
            for i in range(ref.shape[0]):
                ref[i] = jnp.zeros(ref.shape[1:], F32)

    def turn(n):
        slot = lax.rem(n, 2)

        @pl.when(n + 1 < turns)
        def _():
            for copy in loads(n + 1):
                copy.start()

        for copy in loads(n):
            copy.wait()

        @pl.loop(0, width // 512)
        def _(m):
            at = pl.ds(pl.multiple_of(m * 512, 512), 512)
            for which, right in enumerate((rows_in, rows_in, cots_in)):
                ref = made[which]
                part = lax.dot_general(
                    left_in[slot, which],
                    right[slot, :, at],
                    (((0,), (0,)), ((), ())),
                    preferred_element_type=F32,
                )
                for i, (begin, _, kept) in enumerate(spans):
                    begin = begin - first
                    ref[i, :, at] = ref[i, :, at] + part[begin : begin + kept]

    return turns, begin, turn


def work_shapes(work, spans, lines):
    count, width = work[1].shape[0], work[0].shape[1] - 128
    width = (width + work[1].shape[1]) // 2
    units = sum(size for _, size, _ in spans)
    depth = min(512, count // lines)
    shapes = [jax.ShapeDtypeStruct((len(spans), spans[0][2], width), F32)] * 3
    rows = pltpu.VMEM((2, depth, width), BF)
    buffers = [rows, rows, pltpu.VMEM((2, 3, depth, units), BF), pltpu.SemaphoreType.DMA((2, 6))]
    return shapes, buffers


def grads_kernel(lines, plane, with_o, spans, *refs):
    jobs = 4
    refs = list(refs)
    take = lambda n: [refs.pop(0) for _ in range(n)]
    parts = take(jobs)
    (rows_part,) = take(1)
    o_part = take(1)[0] if with_o else None
    work = take(4) if spans else None
    outs = take(jobs)
    (rows_out,) = take(1)
    o_out = take(1)[0] if with_o else None
    made = take(3) if spans else None
    ybufs, zbufs, tots = take(jobs), take(jobs), take(jobs)
    p_own, p_core, p_x, r_own, r_core, r_x = take(6)
    ys, yr, zs, zr, gs, gr, ls, ss, sr = take(9)
    if with_o:
        o_ybuf, o_zbuf, o_tot, oys, oyr, ozs, ozr, ocs, ocr = take(9)
    if spans:
        rows_in, cots_in, left_in, ins = take(4)
    me = Place()
    z, y, x, c = me.z, me.y, me.x, me.c
    others = [lax.rem(z + 1 + j, lines) for j in range(lines - 1)]
    places = list(enumerate(others)) + [(lines - 1, z)]
    near = [(x, 1 - c), (1 - x, c), (1 - x, 1 - c)]
    to_near = [me.at(x=xx, c=cc) for xx, cc in near]
    to_y, to_x, to_c = me.at(y=1 - y), to_near[1], to_near[0]
    greet([me.at(z=o) for o in others] + [to_y] + to_near)
    copies = Copies()
    go = copies.go
    plain = [i for i in range(jobs) if i != plane]

    group = (
        (parts[plane], p_own, p_core, p_x, lambda ref, xx, cc: ref.at[:, :, xx, cc]),
        (rows_part, r_own, r_core, r_x, lambda ref, xx, cc: ref.at[xx, cc]),
    )
    core_copy = lambda i, far: remote(
        group[i][4](group[i][0], 1 - x if far else x, 1 - c),
        group[i][2].at[far],
        ss.at[i, far],
        sr.at[i, far],
        to_c,
    )
    own_copy = lambda i, far: pltpu.make_async_copy(
        group[i][4](group[i][0], 1 - x if far else x, c), group[i][1].at[far], ls.at[i, far]
    )
    x_copy = lambda i: remote(group[i][1].at[1], group[i][3], ss.at[i, 2], sr.at[i, 2], to_x)
    for far in (1, 0):
        for i in range(2):
            go(core_copy(i, far))
            own_copy(i, far).start()

    def over_y(i, j, o):
        source = p_own.at[0, o, 1 - y] if i == plane else parts[i].at[o, 1 - y]
        return remote(source, ybufs[i].at[o], ys.at[i, j], yr.at[i, o], to_y)

    def over_z(i, j, o):
        return remote(ybufs[i].at[o], zbufs[i].at[z], zs.at[i, j], zr.at[i, z], me.at(z=o))

    if with_o:
        holder = c == y
        o_over_y = lambda j, o: remote(o_part.at[o], o_ybuf.at[o], oys.at[j], oyr.at[o], to_y)
        o_over_z = lambda j, o: remote(
            o_ybuf.at[o], o_zbuf.at[z], ozs.at[j], ozr.at[z], me.at(z=o)
        )
    for j, o in places:
        for i in plain:
            go(over_y(i, j, o))
        if with_o:

            @pl.when(jnp.logical_not(holder))
            def _(j=j, o=o):
                o_over_y(j, o).start()

    if spans:
        turns, begin_work, work_turn = grad_worker(work, made, (rows_in, cots_in, left_in), ins, spans)
        begin_work()

    @pl.loop(0, lines)
    def _(j):
        if spans:
            per_line = turns // lines

            @pl.loop(0, per_line)
            def _(n):
                work_turn(j * per_line + n)

        @pl.when(j == 0)
        def _():
            for i in range(2):
                core_copy(i, 1).wait_recv()
                own_copy(i, 1).wait()
                add_blocks(group[i][1].at[1], group[i][1].at[1], group[i][2].at[1])
                x_copy(i).start()

        @pl.when(j == 1)
        def _():
            core_copy(0, 0).wait_recv()
            own_copy(0, 0).wait()
            x_copy(0).wait_recv()
            add_three(p_own.at[0], p_own.at[0], p_core.at[0], p_x)
            for k, o in places:
                over_y(plane, k, o).start()

        @pl.when(j == 2)
        def _():
            core_copy(1, 0).wait_recv()
            own_copy(1, 0).wait()
            x_copy(1).wait_recv()
            add_three(rows_out, r_own.at[0], r_core.at[0], r_x)

        o = lax.rem(z + 1 + j, lines)
        for i in plain:
            over_y(i, j, o).wait_recv()
            add_blocks(ybufs[i].at[o], parts[i].at[o, y], ybufs[i].at[o])

            @pl.when(j < lines - 1)
            def _(i=i):
                over_z(i, j, o).start()

        if with_o:

            @pl.when(holder)
            def _():
                o_over_y(j, o).wait_recv()
                add_blocks(o_ybuf.at[o], o_part.at[o], o_ybuf.at[o])

                @pl.when(j < lines - 1)
                def _():
                    o_over_z(j, o).start()

    for j, o in places:
        over_y(plane, j, o).wait_recv()
        add_blocks(ybufs[plane].at[o], p_own.at[0, o, y], ybufs[plane].at[o])
        if j < lines - 1:
            over_z(plane, j, o).start()

    def line_sum(target, acc, zbuf):
        if len(target.shape) > 2:
            for k in range(target.shape[0]):
                line_sum(target.at[k], acc.at[:, k], zbuf.at[:, k])
            return
        rows = target.shape[0]
        step = 16 if rows % 16 == 0 else rows

        @pl.loop(0, rows // step)
        def _(i):
            at = pl.ds(pl.multiple_of(i * step, step), step)
            value = acc[z, at].astype(F32)
            for o in others:
                value = value + zbuf[o, at].astype(F32)
            target[at] = value.astype(target.dtype)

    near_copy = lambda i, p: remote(
        tots[i].at[near[p][0], near[p][1]], outs[i].at[x, c], gs.at[i, p], gr.at[i, p], to_near[p]
    )
    for i in plain + [plane]:
        for j, o in places[:-1]:
            block = zbufs[i].at[o]
            remote(block, block, zs.at[i, j], zr.at[i, o], me.at(z=o)).wait_recv()
        if i == plane:
            line_sum(outs[i], ybufs[i], zbufs[i])
        else:
            line_sum(tots[i], ybufs[i], zbufs[i])
            for p in range(3):
                go(near_copy(i, p))
            outs[i][x, c] = tots[i][x, c]
    if with_o:
        o_core = remote(o_tot.at[1 - c], o_out, ocs, ocr, to_c)

        @pl.when(holder)
        def _():
            for j, o in places[:-1]:
                block = o_zbuf.at[o]
                remote(block, block, ozs.at[j], ozr.at[o], me.at(z=o)).wait_recv()
            line_sum(o_tot.at[1 - c], o_ybuf.at[:, 1 - c], o_zbuf.at[:, 1 - c])
            o_core.start()
            line_sum(o_out, o_ybuf.at[:, c], o_zbuf.at[:, c])
            for j, o in places[:-1]:
                o_over_z(j, o).wait_send()
            o_core.wait_send()

        @pl.when(jnp.logical_not(holder))
        def _():
            for j, o in places:
                o_over_y(j, o).wait_send()
            o_core.wait_recv()

    for i in plain:
        for p in range(3):
            block = outs[i].at[near[p][0], near[p][1]]
            remote(block, block, gs.at[i, p], gr.at[i, p], to_near[p]).wait_recv()
    for i in range(jobs):
        for j, o in places[:-1]:
            over_z(i, j, o).wait_send()
    for j, o in places:
        over_y(plane, j, o).wait_send()
    for i in range(2):
        x_copy(i).wait_send()
    copies.finish()


def sum_grads(parts, plane, rows_part, o_part, lines, ident, work=None, spans=None):
    jobs = len(parts)
    with_o = o_part is not None
    inputs = list(parts) + [rows_part] + ([o_part] if with_o else [])
    in_specs = [HBM if i == plane else VMEM for i in range(jobs)] + [HBM] + [VMEM] * with_o
    block = lambda i: parts[i].shape[4:] if i == plane else parts[i].shape[2:]
    outs = [jax.ShapeDtypeStruct(block(i), parts[i].dtype) for i in range(jobs)]
    outs.append(jax.ShapeDtypeStruct(rows_part.shape[2:], F32))
    if with_o:
        outs.append(jax.ShapeDtypeStruct(o_part.shape[2:], o_part.dtype))
    dma = pltpu.SemaphoreType.DMA
    buf = lambda lead, i: pltpu.VMEM(lead + block(i), parts[i].dtype)
    scratch = [buf((lines,), i) for i in range(jobs)] * 2
    scratch += [pltpu.VMEM((8, 128), BF) if i == plane else buf((), i) for i in range(jobs)]
    scratch += [buf((2, lines, 2), plane), buf((2, lines, 2), plane), buf((lines, 2), plane)]
    rows = lambda *lead: pltpu.VMEM(lead + rows_part.shape[2:], rows_part.dtype)
    scratch += [rows(2), rows(2), rows()]
    scratch += [dma((jobs, lines))] * 4 + [dma((jobs, 3))] * 2
    scratch += [dma((2, 2)), dma((2, 3)), dma((2, 3))]
    if with_o:
        scratch += [pltpu.VMEM(o_part.shape, o_part.dtype)] * 2
        scratch += [pltpu.VMEM(o_part.shape[1:], o_part.dtype)]
        scratch += [dma((lines,))] * 4 + [dma, dma]
    out_specs = [VMEM] * len(outs)
    if work:
        inputs += work
        in_specs += [HBM] * 4
        shapes, buffers = work_shapes(work, spans, lines)
        outs += shapes
        out_specs += [VMEM] * 3
        scratch += buffers
    return pl.pallas_call(
        functools.partial(grads_kernel, lines, plane, with_o, spans if work else None),
        out_shape=outs,
        in_specs=in_specs,
        out_specs=out_specs,
        scratch_shapes=scratch,
        compiler_params=pltpu.CompilerParams(
            collective_id=ident, has_side_effects=True, vmem_limit_bytes=63 << 20
        ),
    )(*inputs)


def nt(a, b):
    return lax.dot_general(a, b, (((1,), (1,)), ((), ())), preferred_element_type=F32)


def hidden_kernel(
    lines, chunks, spans, local_experts,
    src, cots, spread, e_gate, e_up, e_down, s_in, s_down,
    dst, hid, in_d, gate_g, w_in_out, parts,
    h_in, c_in, hid_out, in_out, g_out, part_out, w_in, w_down,
    w_sem, own_sem, hs, cins, sts, zs, zr, xs, xr, ys, yr, ds_, dr, cs, cr,
):
    me = Place()
    z, y, x, c = me.z, me.y, me.x, me.c
    expert_at = 2 * z + y
    rows, wide = src.shape
    width, early = w_down.shape[1], cots.shape[-1]
    inner = w_down.shape[0]
    step_rows = rows // chunks
    units = lines * 2 * step_rows
    others = [lax.rem(z + 1 + j, lines) for j in range(lines - 1)]
    places = [(lines - 1, z)] + list(reversed(list(enumerate(others))))
    to_x, to_y, to_c = me.at(x=1 - x), me.at(y=1 - y), me.at(c=1 - c)
    greet([me.at(z=o) for o in others] + [to_x, to_y, to_c])
    half = wide // 256 * 128
    cuts = (pl.ds(0, half), pl.ds(half, wide - half))
    side_of = lambda side: (lax.rem(y + side // 2, 2), lax.rem(x + lax.rem(side, 2), 2))

    def span(k):
        return pl.ds(pl.multiple_of(k * step_rows, step_rows), step_rows)

    def block(zz, yy, xx, k, cols=None):
        if cols is None:
            return dst.at[zz, yy, xx, c, span(k)]
        return dst.at[zz, yy, xx, c, span(k), cuts[cols]]

    own = pltpu.make_async_copy(src, dst.at[z, y, x, c], own_sem)
    own.start()
    piece = lambda k: src.at[span(k)]
    z_copy = lambda k, j, o: remote(
        piece(k), block(z, y, x, k), zs.at[k, j], zr.at[k, z], me.at(z=o)
    )
    x_copy = lambda k, j, o, b: remote(b, block(o, y, x, k), xs.at[k, j], xr.at[k, o], to_x)
    y_copy = lambda k, j, o, b: remote(b, block(o, y, x, k), ys.at[k, j], yr.at[k, o], to_y)

    def diag_copy(k, j, o, h):
        b = block(o, y, 1 - x, k, 0) if h == 0 else block(o, 1 - y, x, k, 1)
        return remote(b, b, ds_.at[k, j, h], dr.at[k, o, h], to_y if h == 0 else to_x)

    def core_copy(k, side, cc):
        yy, xx = side_of(side)
        b = dst.at[:, yy, xx, cc, span(k)]
        return remote(b, b, cs.at[k, side], cr.at[k, side], to_c)

    def z_land(k):
        for j, o in places[1:]:
            b = block(o, y, x, k)
            remote(b, b, zs.at[k, j], zr.at[k, o], me.at(z=o)).wait_recv()
            x_copy(k, j, o, b).start()
            y_copy(k, j, o, b).start()
        core_copy(k, 0, c).start()

    def xy_land(k):
        for j, o in places:
            b = block(o, y, 1 - x, k)
            remote(b, b, xs.at[k, j], xr.at[k, o], to_x).wait_recv()
            diag_copy(k, j, o, 0).start()
            b = block(o, 1 - y, x, k)
            remote(b, b, ys.at[k, j], yr.at[k, o], to_y).wait_recv()
            diag_copy(k, j, o, 1).start()
        core_copy(k, 1, c).start()
        core_copy(k, 2, c).start()

    def diag_land(k):
        for j, o in places:
            for h, w in ((0, to_y), (1, to_x)):
                b = block(o, 1 - y, 1 - x, k, h)
                remote(b, b, ds_.at[k, j, h], dr.at[k, o, h], w).wait_recv()
        core_copy(k, 3, c).start()

    def loads(k, side):
        yy, xx = side_of(side)
        return (
            pltpu.make_async_copy(dst.at[:, yy, xx, :, span(k)], h_in.at[side], hs.at[side]),
            pltpu.make_async_copy(cots.at[:, yy, xx, :, span(k)], c_in.at[side], cins.at[side]),
        )

    def fetch(k, side):
        core_copy(k, side, 1 - c).wait_recv()
        for copy in loads(k, side):
            copy.start()

    def stores(k, side):
        yy, xx = side_of(side)
        pairs = ((hid_out, hid), (in_out, in_d), (g_out, gate_g), (part_out, parts))
        return [
            pltpu.make_async_copy(v.at[side], ref.at[:, yy, xx, :, span(k)], sts.at[side, i])
            for i, (v, ref) in enumerate(pairs)
        ]

    def unit(k, side):
        for copy in loads(k, side):
            copy.wait()
        h = h_in[side, :, :, :, :width].reshape(units, width)
        gates = h_in[side, :, :, :, width : width + 128].reshape(units, 128)
        late = h_in[side, :, :, :, width + 128 :].reshape(units, width - early)
        scale = jnp.dot(gates, spread[...], preferred_element_type=F32)
        both = nt(h, w_in[...])
        down = nt(c_in[side].reshape(units, early), w_down[:, :early])
        down = down + nt(late, w_down[:, early:])
        columns = lax.broadcasted_iota(jnp.int32, (units, 128), 1)
        sums = jnp.zeros((units, 128), F32)
        for i, (begin, size) in enumerate(spans):
            at = slice(begin, begin + size)
            up_at = slice(inner + begin, inner + begin + size)
            g, u, d = both[:, at], both[:, up_at], down[:, at]
            sig = 1.0 / (1.0 + jnp.exp(-g))
            act = g * sig
            value = (act * u).astype(BF).astype(F32)
            shape = (lines, 2, step_rows, size)
            if i < local_experts:
                total = jnp.sum(value * d, axis=1, keepdims=True)
                sums = jnp.where(columns == expert_at * local_experts + i, total, sums)
                value = value * scale[:, at]
                d = d * scale[:, at]
            hid_out[side, :, :, :, at] = value.astype(BF).reshape(shape)
            in_out[side, :, :, :, at] = (
                (d * u * (sig + act * (1.0 - sig))).astype(BF).reshape(shape)
            )
            in_out[side, :, :, :, up_at] = (d * act).astype(BF).reshape(shape)
        g_out[side] = sums.astype(BF).reshape(lines, 2, step_rows, 128)
        hidden = hid_out[side].reshape(units, inner)
        for begin in range(0, width, 512):
            at = slice(begin, begin + 512)
            part = jnp.dot(hidden, w_down[:, at], preferred_element_type=F32)
            part_out[side, :, :, :, at] = part.astype(BF).reshape(lines, 2, step_rows, 512)
        for copy in stores(k, side):
            copy.start()

    def z_start(k):
        for j, o in enumerate(others):
            z_copy(k, j, o).start()

    z_start(0)
    for k in range(chunks):
        x_copy(k, lines - 1, z, piece(k)).start()
        y_copy(k, lines - 1, z, piece(k)).start()

    fills = []
    for i, (begin, size) in enumerate(spans):
        for target, start, source in (
            (w_in, 0, e_gate.at[i] if i < local_experts else s_in.at[0]),
            (w_in, inner, e_up.at[i] if i < local_experts else s_in.at[1]),
            (w_down, 0, e_down.at[i] if i < local_experts else s_down),
        ):
            held = source.shape[0]
            fills.append(
                pltpu.make_async_copy(
                    source, target.at[pl.ds(start + begin, held)], w_sem.at[2 + len(fills)]
                )
            )
            fills[-1].start()
            if size > held:
                target[start + begin + held : start + begin + size] = jnp.zeros(
                    (size - held, width), BF
                )
    for copy in fills:
        copy.wait()
    keep = pltpu.make_async_copy(w_in, w_in_out, w_sem.at[0])
    keep.start()

    own.wait()
    z_land(0)
    if chunks > 1:
        z_start(1)
    fetch(0, 0)
    valid = lambda k: (k >= 0) & (k < chunks)

    @pl.loop(0, chunks + 2)
    def _(t):
        @pl.loop(0, 4)
        def _(side):
            k = t - (side + 1) // 2

            @pl.when(valid(k))
            def _():
                @pl.when(k >= 1)
                def _():
                    for copy in stores(k - 1, side):
                        copy.wait()

                unit(k, side)

            @pl.when((side == 0) & valid(t - 1))
            def _():
                fetch(t - 1, 2)

            @pl.when((side == 1) & valid(t - 2))
            def _():
                fetch(t - 2, 3)

        @pl.when(valid(t + 1))
        def _():
            z_land(t + 1)

        @pl.when(valid(t + 2))
        def _():
            z_start(t + 2)

        @pl.when(valid(t))
        def _():
            xy_land(t)

        @pl.when(valid(t + 1))
        def _():
            fetch(t + 1, 0)

        @pl.when(valid(t - 1))
        def _():
            diag_land(t - 1)

        @pl.when(valid(t))
        def _():
            fetch(t, 1)

    keep.wait()
    for side in range(4):
        for copy in stores(chunks - 1, side):
            copy.wait()

    @pl.loop(0, chunks)
    def _(k):
        for j, o in enumerate(others):
            z_copy(k, j, o).wait_send()
        for j, o in places:
            b = piece(k) if j == lines - 1 else block(o, y, x, k)
            x_copy(k, j, o, b).wait_send()
            y_copy(k, j, o, b).wait_send()
            diag_copy(k, j, o, 0).wait_send()
            diag_copy(k, j, o, 1).wait_send()
        for side in range(4):
            core_copy(k, side, c).wait_send()


def gather_hidden(
    value, cots, spread, e_gate, e_up, e_down, s_in, s_down, spans, local_experts, lines, ident
):
    rows, wide = value.shape
    width, early = e_down.shape[2], cots.shape[1]
    inner = spans[-1][0] + spans[-1][1]
    step_rows = min(rows, max(16, 128 // lines))
    chunks = rows // step_rows
    lead = (lines, 2, 2, 2, rows)
    dma = pltpu.SemaphoreType.DMA
    slot = lambda n: pltpu.VMEM((4, lines, 2, step_rows, n), BF)
    line = dma((chunks, lines))
    return pl.pallas_call(
        functools.partial(hidden_kernel, lines, chunks, spans, local_experts),
        out_shape=[
            jax.ShapeDtypeStruct(lead + (n,), BF) for n in (wide, inner, 2 * inner, 128)
        ]
        + [
            jax.ShapeDtypeStruct((2 * inner, width), BF),
            jax.ShapeDtypeStruct(lead + (width,), BF),
        ],
        in_specs=[HBM, HBM, VMEM] + [HBM] * 5,
        out_specs=[HBM] * 6,
        scratch_shapes=[
            slot(wide), slot(early), slot(inner), slot(2 * inner), slot(128), slot(width),
            pltpu.VMEM((2 * inner, width), BF), pltpu.VMEM((inner, width), BF),
            dma((2 + 3 * len(spans),)), dma, dma((4,)), dma((4,)), dma((4, 4)),
            line, line, line, line, line, line,
            dma((chunks, lines, 2)), dma((chunks, lines, 2)), dma((chunks, 4)), dma((chunks, 4)),
        ],
        compiler_params=pltpu.CompilerParams(
            collective_id=ident, has_side_effects=True, vmem_limit_bytes=60 << 20
        ),
    )(value, cots.reshape(lead + (early,)), spread, e_gate, e_up, e_down, s_in, s_down)


def back_kernel(
    lines,
    in_d, gate_g, w_in, passed,
    out, passed_on,
    d_in, g_in, sbuf, acc, cbuf, xbuf, ybuf, zbuf, xdiag, ydiag,
    ins, cs, cr, xs, xr, ys, yr, zs, zr, xds, xdr, yds, ydr,
):
    me = Place()
    z, y, x, c = me.z, me.y, me.x, me.c
    rows, wide = out.shape
    width = wide - 128
    half = wide // 256 * 128
    others = [lax.rem(z + 1 + j, lines) for j in range(lines - 1)]
    to_x, to_y, to_c = me.at(x=1 - x), me.at(y=1 - y), me.at(c=1 - c)
    greet([me.at(z=o) for o in others] + [to_x, to_y, to_c])
    cols = (pl.ds(0, half), pl.ds(half, wide - half))
    lag = (0, 1, 1, 2)
    place = lambda n: lax.rem(z + 1 + n, lines)

    def side_of(side):
        return (
            lax.rem(y + 1 - side // 2, 2),
            lax.rem(x + 1 - lax.rem(side, 2), 2),
        )

    def loads(n, side):
        yy, xx = side_of(side)
        pairs = ((in_d, d_in), (gate_g, g_in))
        return [
            pltpu.make_async_copy(ref.at[place(n), yy, xx], v.at[side], ins.at[side, i])
            for i, (ref, v) in enumerate(pairs)
        ]

    def to_core(n, side):
        yy, xx = side_of(side)
        return remote(
            sbuf.at[side], cbuf.at[place(n), yy, xx], cs.at[side], cr.at[n, side], to_c
        )

    def unit(n, side):
        yy, xx = side_of(side)
        for copy in loads(n, side):
            copy.wait()
        grads = d_in[side].reshape(2 * rows, w_in.shape[0])
        piece = 512
        for begin in range(0, width, piece):
            at = slice(begin, begin + piece)
            back = jnp.dot(grads, w_in[:, at], preferred_element_type=F32).astype(BF).reshape(2, rows, piece)

            @pl.when(c == 0)
            def _():
                acc[place(n), yy, xx, :, at] = back[0]
                sbuf[side, :, at] = back[1]

            @pl.when(c == 1)
            def _():
                acc[place(n), yy, xx, :, at] = back[1]
                sbuf[side, :, at] = back[0]

        acc[place(n), yy, xx, :, width:] = g_in[side, c]
        sbuf[side, :, width:] = g_in[side, 1 - c]

    def sums(target, *terms):
        @pl.loop(0, rows // 16)
        def _(i):
            at = pl.ds(pl.multiple_of(i * 16, 16), 16)
            total = terms[0][at].astype(F32)
            for term in terms[1:]:
                total = total + term[at].astype(F32)
            target[at] = total.astype(BF)

    def diag_sends(n):
        o = place(n)
        far = acc.at[o, 1 - y, 1 - x]
        return (
            remote(far.at[:, cols[0]], xdiag.at[o], xds.at[n], xdr.at[n], to_x),
            remote(far.at[:, cols[1]], ydiag.at[o], yds.at[n], ydr.at[n], to_y),
        )

    def side_sends(n):
        o = place(n)
        return (
            remote(acc.at[o, y, 1 - x], xbuf.at[o], xs.at[n], xr.at[n], to_x),
            remote(acc.at[o, 1 - y, x], ybuf.at[o], ys.at[n], yr.at[n], to_y),
        )

    def z_copy(n):
        return remote(
            acc.at[place(n), y, x], zbuf.at[z], zs.at[n], zr.at[z], me.at(z=place(n))
        )

    def first(n):
        to_core(n, 0).wait_recv()
        mine, other = acc.at[place(n), 1 - y, 1 - x], cbuf.at[place(n), 1 - y, 1 - x]
        sums(mine, mine, other)
        for copy in diag_sends(n):
            copy.start()

    def second(n):
        o = place(n)
        mine, other = acc.at[o, 1 - y, x], cbuf.at[o, 1 - y, x]
        to_core(n, 1).wait_recv()
        diag_sends(n)[0].wait_recv()
        sums(mine.at[:, cols[0]], mine.at[:, cols[0]], other.at[:, cols[0]], xdiag.at[o])
        sums(mine.at[:, cols[1]], mine.at[:, cols[1]], other.at[:, cols[1]])
        side_sends(n)[1].start()

    def third(n):
        o = place(n)
        mine, other = acc.at[o, y, 1 - x], cbuf.at[o, y, 1 - x]
        to_core(n, 2).wait_recv()
        diag_sends(n)[1].wait_recv()
        sums(mine.at[:, cols[0]], mine.at[:, cols[0]], other.at[:, cols[0]])
        sums(mine.at[:, cols[1]], mine.at[:, cols[1]], other.at[:, cols[1]], ydiag.at[o])
        side_sends(n)[0].start()

    def fourth(n):
        o = place(n)
        mine, other = acc.at[o, y, x], cbuf.at[o, y, x]
        to_core(n, 3).wait_recv()
        for copy in side_sends(n):
            copy.wait_recv()
        sums(mine, mine, other, xbuf.at[o], ybuf.at[o])

        @pl.when(n < lines - 1)
        def _():
            z_copy(n).start()

    valid = lambda n: (n >= 0) & (n < lines)
    for side in range(4):
        for copy in loads(0, side):
            copy.start()

    @pl.loop(0, lines + 3)
    def _(t):
        @pl.loop(0, 4)
        def _(side):
            n = t - (side + 1) // 2

            @pl.when(valid(n))
            def _():
                @pl.when(n >= 1)
                def _():
                    to_core(n - 1, side).wait_send()

                unit(n, side)
                to_core(n, side).start()

                @pl.when(n + 1 < lines)
                def _():
                    for copy in loads(n + 1, side):
                        copy.start()

            for turn, (behind, act) in enumerate(((3, fourth), (0, first), (1, second), (1, third))):

                @pl.when((side == turn) & valid(t - behind))
                def _(behind=behind, act=act):
                    act(t - behind)

    for side in range(4):
        to_core(lines - 1, side).wait_send()
    for o in others:
        remote(zbuf.at[o], zbuf.at[o], zs.at[0], zr.at[o], me.at(z=o)).wait_recv()

    @pl.loop(0, rows // 16)
    def _(i):
        at = pl.ds(pl.multiple_of(i * 16, 16), 16)
        total = acc[z, y, x, at].astype(F32)
        for o in others:
            total = total + zbuf[o, at].astype(F32)
        out[at] = total

    @pl.loop(0, lines)
    def _(n):
        for copy in diag_sends(n) + side_sends(n):
            copy.wait_send()

        @pl.when(n < lines - 1)
        def _():
            z_copy(n).wait_send()


def layout_kernel(own_heads, q, kvb, kva, o, shared, q_out, kvb_out, kva_out, o_out, gate_out, up_out):
    for source, target in ((q, q_out), (kvb, kvb_out)):
        size = source.shape[3] // own_heads
        held = [[source[xx, cc].astype(F32) for cc in range(2)] for xx in range(2)]
        pieces = [
            held[xx][cc][:, i * size : (i + 1) * size]
            for i in range(own_heads)
            for cc in range(2)
            for xx in range(2)
        ]
        target[...] = jnp.concatenate(pieces, axis=1)
    kva_out[...] = kva[...].astype(F32)
    o_out[...] = o[...].astype(F32)
    for which, target in enumerate((gate_out, up_out)):
        pieces = [shared[i, which].astype(F32) for i in range(shared.shape[0])]
        target[...] = jnp.concatenate(pieces, axis=1)


def lay_out(q, kvb, kva, o, shared, own_heads):
    flat = lambda rows, columns: jax.ShapeDtypeStruct((rows, columns), F32)
    hidden = shared.shape[0] * shared.shape[3]
    return pl.pallas_call(
        functools.partial(layout_kernel, own_heads),
        out_shape=[
            flat(q.shape[2], 4 * q.shape[3]),
            flat(kvb.shape[2], 4 * kvb.shape[3]),
            flat(*kva.shape),
            flat(*o.shape),
            flat(shared.shape[2], hidden),
            flat(shared.shape[2], hidden),
        ],
        in_specs=[VMEM] * 5,
        out_specs=[VMEM] * 6,
        compiler_params=pltpu.CompilerParams(vmem_limit_bytes=32 << 20),
    )(q, kvb, kva, o, shared)


def sum_back(in_d, gate_g, w_in, passed, ident):
    lines, rows, inner = in_d.shape[0], in_d.shape[4], in_d.shape[5]
    width = w_in.shape[1]
    wide = width + 128
    half = wide // 256 * 128
    dma = pltpu.SemaphoreType.DMA
    buf = lambda *shape: pltpu.VMEM(shape, BF)
    line = dma((lines,))
    return pl.pallas_call(
        functools.partial(back_kernel, lines),
        out_shape=[
            jax.ShapeDtypeStruct((rows, wide), F32),
            jax.ShapeDtypeStruct(passed.shape, passed.dtype),
        ],
        in_specs=[HBM] * 2 + [VMEM, HBM],
        out_specs=[VMEM, HBM],
        input_output_aliases={3: 1},
        scratch_shapes=[
            buf(4, 2, rows, inner), buf(4, 2, rows, 128), buf(4, rows, wide),
            buf(lines, 2, 2, rows, wide), buf(lines, 2, 2, rows, wide),
            buf(lines, rows, wide), buf(lines, rows, wide), buf(lines, rows, wide),
            buf(lines, rows, half), buf(lines, rows, wide - half),
            dma((4, 2)), dma((4,)), dma((lines, 4)),
            line, line, line, line, line, line, line, line, line, line,
        ],
        compiler_params=pltpu.CompilerParams(
            collective_id=ident, has_side_effects=True, vmem_limit_bytes=60 << 20
        ),
    )(in_d, gate_g, w_in, passed)


def on_device(
    tokens,
    cotangent,
    norm1_gain,
    q_weight,
    kva_weight,
    kv_gain,
    kvb_weight,
    o_weight,
    norm2_gain,
    router_weight,
    shared_gate,
    shared_up,
    shared_down,
    expert_gate,
    expert_up,
    expert_down,
    expert_ids,
    token_rank,
    seq_ids,
):
    expert_count = lax.axis_size("expert")
    shard_count = lax.axis_size("shard")
    device_count = expert_count * shard_count
    expert_at = lax.axis_index("expert")
    shard_at = lax.axis_index("shard")
    tok_rows, width = tokens.shape
    group_len = seq_ids.shape[0]
    local_experts = expert_gate.shape[0]
    all_experts = local_experts * expert_count
    top_count = expert_ids.shape[1]
    capacity = max(2, tok_rows * top_count // all_experts)
    score_scale = (NOPE + ROPE) ** (-0.5)
    own_heads = HEADS // shard_count
    latent_width = kva_weight.shape[1]

    lines = expert_count // 2
    o_rows = o_weight.shape[0]
    o_pairs = VDIM == 2 * o_rows

    def by_head(weight):
        rows = weight.shape[0]
        heads = weight.reshape(rows, own_heads, 2, 2, weight.shape[1] // HEADS)
        return heads.transpose(3, 2, 0, 1, 4).reshape(2, 2, rows, weight.shape[1] // 4)

    small = [norm1_gain, norm2_gain, kv_gain, router_weight]
    small_sizes = [v.size for v in small]

    def pack(values):
        flat = jnp.concatenate(values, axis=-1)
        pad = -flat.shape[-1] % 2048
        flat = jnp.pad(flat, [(0, 0)] * (flat.ndim - 1) + [(0, pad)])
        return flat.reshape(flat.shape[:-1] + (-1, 128))

    def unpack(packed):
        flat = packed.reshape(packed.shape[:-2] + (-1,))
        starts = [sum(small_sizes[:i]) for i in range(len(small_sizes))]
        return [flat[..., b : b + n] for b, n in zip(starts, small_sizes)]

    shared_width = shared_down.shape[0]
    both_shared = jnp.stack([shared_gate, shared_up]).reshape(
        2, shared_gate.shape[0], device_count, shared_width
    )
    both_shared = lax.all_to_all(
        both_shared.transpose(2, 0, 1, 3), BOTH, split_axis=0, concat_axis=0
    )
    both_shared = both_shared.transpose(1, 0, 2, 3).reshape(2, width, shared_width)
    small_own = pack([v.reshape(-1) for v in small])
    rounds = max(1, tok_rows * device_count // 4096)
    started = start_gather(
        tokens,
        kva_weight,
        [
            jnp.broadcast_to(small_own, (2, 2) + small_own.shape),
            by_head(kvb_weight),
            by_head(q_weight),
        ],
        o_weight if o_pairs else None,
        lines,
        1,
    )
    group_tokens = started[0].reshape(group_len, width)
    kva_all = started[1].reshape(width, latent_width)
    small_set, kvb_set, q_set, *o_set = started[2:]
    small_all = unpack(small_set.reshape((device_count,) + small_own.shape))
    kvb_mine = kvb_set.reshape(KV_RANK, -1)
    q_mine = q_set.reshape(width, -1)
    core_at, x_at = shard_at % 2, shard_at // 2
    if o_pairs:
        o_mine = o_set[0].reshape(own_heads * VDIM, width)
    else:
        o_mine = gather(o_weight, BOTH).reshape(own_heads, 2, 2, VDIM, width)
        o_mine = o_mine[:, core_at, x_at].reshape(own_heads * VDIM, width)
    norm1_scale, norm2_scale, latent_scale = [v.reshape(-1).astype(F32) for v in small_all[:3]]
    router = small_all[3].reshape(width, all_experts)

    positions = positions_of(seq_ids)
    cosine_table, sine_table = rope_tables(positions, ROPE)
    token_index = jnp.arange(group_len, dtype=jnp.int32)
    allowed = (token_index[None, :] <= token_index[:, None]) & (
        (seq_ids[None, :] == 0) | (seq_ids[None, :] == seq_ids[:, None])
    )
    input_rows = tokens.astype(F32)
    group_rows = group_tokens.astype(F32)
    normed_group, inverse_group = rms_forward(group_rows, norm1_scale)
    hidden_one = normed_group.astype(BF)
    query_raw = mm(hidden_one, q_mine).reshape(group_len, own_heads, NOPE + ROPE)
    q_nope = query_raw[:, :, :NOPE].astype(BF)
    q_rope = rotate(
        query_raw[:, :, NOPE:], cosine_table[:, None, :], sine_table[:, None, :]
    ).astype(BF)
    compressed = mm(hidden_one, kva_all)
    latent_norm, inverse_latent = rms_forward(compressed[:, :KV_RANK], latent_scale)
    latent = latent_norm.astype(BF)
    k_rope = rotate(compressed[:, KV_RANK:], cosine_table, sine_table).astype(BF)
    keyval = mm(latent, kvb_mine).astype(BF).reshape(group_len, own_heads, NOPE + VDIM)
    keys = keyval[:, :, :NOPE]
    values = keyval[:, :, NOPE:]
    scores = jnp.einsum("qhd,khd->hqk", q_nope, keys, preferred_element_type=F32)
    scores = scores + jnp.einsum("qhd,kd->hqk", q_rope, k_rope, preferred_element_type=F32)
    scores = jnp.where(allowed[None], scores * score_scale, NEGATIVE)
    top_score = jnp.max(scores, axis=-1, keepdims=True)
    log_total = top_score + jnp.log(jnp.sum(jnp.exp(scores - top_score), axis=-1, keepdims=True))
    soft_probs = jnp.exp(scores - log_total)
    prob_low = soft_probs.astype(BF)
    attended = (
        jnp.einsum("hqk,khd->qhd", prob_low, values, preferred_element_type=F32)
        .astype(BF)
        .reshape(group_len, own_heads * VDIM)
    )
    projected = sum_group(mm(attended, o_mine).astype(BF), 2)
    mixed = input_rows + projected

    normed_two, inverse_two = rms_forward(mixed, norm2_scale)
    hidden_two = normed_two.astype(BF)
    logits = mm(hidden_two, router)
    choice_hot = (
        expert_ids[:, :, None] == jnp.arange(all_experts, dtype=jnp.int32)[None, None, :]
    ).astype(F32)
    chosen = jnp.sum(choice_hot * logits[:, None, :], axis=-1)
    gate_probs = jax.nn.softmax(chosen, axis=-1)
    kept = kept_pairs(expert_ids, token_rank, choice_hot, capacity)
    gate_table = jnp.sum(choice_hot * (gate_probs * kept)[:, :, None], axis=1)

    own_width = expert_gate.shape[2]
    sizes = [own_width + -own_width % 128] * local_experts + [shared_width + -shared_width % 128]
    spans = tuple((sum(sizes[:i]), size) for i, size in enumerate(sizes))

    spare = -shared_width % 128
    shared_in = jnp.pad(both_shared.swapaxes(1, 2), ((0, 0), (0, spare), (0, 0)))
    shared_out = jnp.pad(shared_down, ((0, spare), (0, 0)))
    unit_expert = jnp.concatenate(
        [jnp.full((size,), expert_at * local_experts + i) for i, size in enumerate(sizes[:-1])]
        + [jnp.full((sizes[-1],), -1)]
    )
    column = jnp.arange(128)[:, None]
    spread = (
        (column == unit_expert) | ((column == unit_expert + all_experts) & (unit_expert >= 0))
    ).astype(BF)

    early = width // 2

    def ffn(rows, cots, table):
        cots_all = gather(cots[:, :early] + 0 * group_tokens[0, 0], BOTH)
        high = table.astype(BF)
        low = (table - high.astype(F32)).astype(BF)
        spare = jnp.zeros((table.shape[0], 128 - 2 * all_experts), BF)
        values, hid, in_d, gate_g, w_in, out_part = gather_hidden(
            jnp.concatenate([rows, high, low, spare, cots[:, early:]], axis=1),
            cots_all,
            spread,
            expert_gate.swapaxes(1, 2),
            expert_up.swapaxes(1, 2),
            expert_down,
            shared_in,
            shared_out,
            spans,
            local_experts,
            lines,
            3,
        )
        back_sum, out_part = sum_back(in_d, gate_g, w_in, out_part, 4)
        flat = lambda v: v.reshape(cots_all.shape[0], -1)
        work = [flat(values), cots_all, flat(in_d), flat(hid)]
        return scatter_sum(flat(out_part), BOTH), back_sum, work

    tail = spans[-1][0]
    inner = tail + spans[-1][1]
    expert_spans = tuple(span + (own_width,) for span in spans[:-1])
    shared_spans = (spans[-1] + (shared_width,),)
    if rounds == 1:
        out_sum, back_sum, work = ffn(hidden_two, cotangent, gate_table)
    else:

        def one_round(total, part):
            out_rows, back_rows, (values, cots, in_d, hid) = ffn(*part)
            rows = values[:, :width]
            cots = jnp.concatenate([cots, values[:, width + 128 :]], axis=1)
            grads = [mm_tn(in_d, rows), mm_tn(hid, cots)]
            return [t + g for t, g in zip(total, grads)], (out_rows, back_rows)

        in_rounds = lambda value: value.reshape((rounds, -1) + value.shape[1:])
        zeros = [jnp.zeros((2 * inner, width), F32), jnp.zeros((inner, width), F32)]
        (w_in_grad, w_down_grad), (out_sum, back_sum) = lax.scan(
            one_round, zeros, (in_rounds(hidden_two), in_rounds(cotangent), in_rounds(gate_table))
        )
        out_sum = out_sum.reshape((tok_rows,) + out_sum.shape[2:])
        back_sum = back_sum.reshape((tok_rows,) + back_sum.shape[2:])
        w_in_grad = w_in_grad.reshape(2, inner, width)
        cut = lambda grad: jnp.stack(
            [grad[spans[i][0] : spans[i][0] + own_width] for i in range(local_experts)]
        )
        expert_grads = [cut(w_in_grad[0]), cut(w_in_grad[1]), cut(w_down_grad)]
        shared_made = [v[tail : tail + shared_width] for v in (*w_in_grad, w_down_grad)]
        work = None
    out_sum, back_sum = out_sum.astype(F32), back_sum.astype(F32)
    output = (mixed + out_sum).astype(BF)

    upstream = cotangent.astype(F32)
    gate_grad = jnp.sum(
        choice_hot * back_sum[:, None, width : width + all_experts], axis=-1
    ) * kept
    chosen_grad = gate_probs * (gate_grad - jnp.sum(gate_probs * gate_grad, axis=-1, keepdims=True))
    logit_grad = jnp.sum(choice_hot * chosen_grad[:, :, None], axis=1).astype(BF)
    router_part = mm_tn(hidden_two, logit_grad)
    hidden_two_grad = back_sum[:, :width] + mm_nt(logit_grad, router)
    mixed_norm_grad, norm2_part = rms_backward(mixed, inverse_two, norm2_scale, hidden_two_grad)
    mixed_grad = upstream + mixed_norm_grad

    mixed_grad_group, *made = gather_group(mixed_grad.astype(BF), 5, work, shared_spans, lines)
    if work:
        shared_made = [v[0] for v in made]
    shared_grad = jnp.stack(shared_made[:2]).astype(BF)
    shared_grad = shared_grad.reshape(2, shared_width, device_count, -1).transpose(2, 0, 3, 1)
    shared_grad = lax.all_to_all(shared_grad, BOTH, split_axis=0, concat_axis=0)
    sdown_grad = shared_made[2]
    o_part = mm_tn(attended, mixed_grad_group)
    attended_grad = (
        mm_nt(mixed_grad_group, o_mine).astype(BF).reshape(group_len, own_heads, VDIM)
    )
    prob_grad = jnp.einsum("qhd,khd->hqk", attended_grad, values, preferred_element_type=F32)
    values_grad = jnp.einsum("hqk,qhd->khd", prob_low, attended_grad, preferred_element_type=F32)
    score_grad = (
        soft_probs * (prob_grad - jnp.sum(soft_probs * prob_grad, axis=-1, keepdims=True))
    ).astype(BF)
    q_nope_grad = (
        jnp.einsum("hqk,khd->qhd", score_grad, keys, preferred_element_type=F32) * score_scale
    )
    q_rope_grad = (
        jnp.einsum("hqk,kd->qhd", score_grad, k_rope, preferred_element_type=F32) * score_scale
    )
    keys_grad = (
        jnp.einsum("hqk,qhd->khd", score_grad, q_nope, preferred_element_type=F32) * score_scale
    )
    rope_grad = (
        jnp.einsum("hqk,qhd->kd", score_grad, q_rope, preferred_element_type=F32) * score_scale
    )
    keyval_grad = (
        jnp.concatenate([keys_grad, values_grad], axis=-1)
        .reshape(group_len, own_heads * (NOPE + VDIM))
        .astype(BF)
    )
    kvb_part = mm_tn(latent, keyval_grad)
    latent_raw_part, kv_gain_part = rms_backward(
        compressed[:, :KV_RANK], inverse_latent, latent_scale, mm_nt(keyval_grad, kvb_mine)
    )
    compressed_part = jnp.concatenate(
        [latent_raw_part, rotate(rope_grad, cosine_table, -sine_table)], axis=1
    ).astype(BF)
    query_grad = jnp.concatenate(
        [q_nope_grad, rotate(q_rope_grad, cosine_table[:, None, :], -sine_table[:, None, :])],
        axis=-1,
    )
    query_grad = query_grad.reshape(group_len, own_heads * (NOPE + ROPE)).astype(BF)
    q_part = mm_tn(hidden_one, query_grad)
    kva_part = mm_tn(hidden_one, compressed_part)
    hidden_one_part = mm_nt(query_grad, q_mine) + mm_nt(compressed_part, kva_all)
    norm1_part = jnp.sum(hidden_one_part * (group_rows * inverse_group), axis=0)

    def from_heads(parts):
        rows = parts.shape[2]
        heads = parts.reshape(2, 2, rows, own_heads, -1).transpose(2, 3, 1, 0, 4)
        return heads.reshape(rows, -1).astype(F32)

    line_shape = (lines, 2)
    small_parts = pack(
        [v.reshape(device_count, -1) for v in (norm1_part, norm2_part, kv_gain_part, router_part)]
    )
    parts = [
        kvb_part.astype(BF).reshape(line_shape + (2, 2, kvb_weight.shape[0], -1)),
        kva_part.astype(BF).reshape(line_shape + (2, 2, width // device_count, latent_width)),
        q_part.astype(BF).reshape(line_shape + (2, 2, q_weight.shape[0], q_mine.shape[1])),
        small_parts.reshape(line_shape + (2, 2) + small_parts.shape[1:]),
    ]
    o_part = o_part.astype(BF).reshape(own_heads, VDIM, width)
    if o_pairs:
        o_sum = o_part.reshape(own_heads, 2, o_rows, width)
    else:
        o_sum = None
        o_wide = jnp.zeros((own_heads, 2, 2, VDIM, width), BF).at[:, core_at, x_at].set(o_part)
        o_grad = scatter_sum(o_wide.reshape(HEADS * VDIM, width), BOTH).astype(F32)
    summed = sum_grads(
        parts,
        1,
        hidden_one_part.astype(BF).reshape(2, 2, tok_rows, width),
        o_sum,
        lines,
        9,
        work,
        expert_spans,
    )
    _, inverse_one = rms_forward(input_rows, norm1_scale)
    input_norm_grad, _ = rms_backward(input_rows, inverse_one, norm1_scale, summed[4])
    tokens_grad = mixed_grad + input_norm_grad
    if work:
        expert_grads = summed[-3:]
    norm1_grad, norm2_grad, kv_gain_grad, router_grad = unpack(jnp.sum(summed[3], axis=(0, 1)))
    router_grad = router_grad.reshape(router_weight.shape)
    if o_pairs:
        q_grad, kvb_grad, kva_grad, o_grad, sgate_grad, sup_grad = lay_out(
            summed[2], summed[0], summed[1], summed[5], shared_grad, own_heads
        )
    else:
        kvb_grad = from_heads(summed[0])
        kva_grad = summed[1].astype(F32)
        q_grad = from_heads(summed[2])
        sgate_grad, sup_grad = (
            shared_grad.astype(F32)
            .transpose(1, 2, 0, 3)
            .reshape(2, width // device_count, device_count * shared_width)
        )
    return (
        output,
        tokens_grad,
        norm1_grad,
        q_grad,
        kva_grad,
        kv_gain_grad,
        kvb_grad,
        o_grad,
        norm2_grad,
        router_grad,
        sgate_grad,
        sup_grad,
        sdown_grad,
        expert_grads[0].swapaxes(1, 2),
        expert_grads[1].swapaxes(1, 2),
        expert_grads[2],
    )


def solution(mesh):
    rows = P(BOTH, None)
    flat = P(BOTH)
    columns = P("expert", None, "shard")
    depth = P("expert", "shard", None)
    return jax.shard_map(
        on_device,
        mesh=mesh,
        in_specs=(
            rows,
            rows,
            flat,
            rows,
            rows,
            flat,
            rows,
            rows,
            flat,
            rows,
            rows,
            rows,
            rows,
            columns,
            columns,
            depth,
            rows,
            flat,
            P("expert"),
        ),
        out_specs=(
            rows,
            rows,
            flat,
            rows,
            rows,
            flat,
            rows,
            rows,
            flat,
            rows,
            rows,
            rows,
            rows,
            columns,
            columns,
            depth,
        ),
        check_vma=False,
    )
```

```python
import functools

import jax
import jax.numpy as jnp
from jax import lax
from jax.experimental import pallas as pl
from jax.experimental.pallas import tpu as pltpu
from jax.sharding import PartitionSpec as P

HEADS = 16
NOPE = 128
ROPE = 64
VDIM = 128
KV_RANK = 512
CONTS = 2


EPSILON = 1e-06
THETA = 10000.0
NEGATIVE = -1e30
BOTH = ("expert", "shard")
BF = jnp.bfloat16
F32 = jnp.float32


def rms_forward(values, gain_row):
    inverse = lax.rsqrt(jnp.mean(values * values, axis=-1, keepdims=True) + EPSILON)
    return (values * inverse * gain_row, inverse)


def rms_backward(values, inverse, gain_row, upstream):
    normed = values * inverse
    scaled = upstream * gain_row
    value_grad = inverse * (scaled - normed * jnp.mean(scaled * normed, axis=-1, keepdims=True))
    return (value_grad, jnp.sum(upstream * normed, axis=0))


def rope_tables(positions, width):
    half_width = width // 2
    frequency = THETA ** (-2.0 * jnp.arange(half_width, dtype=jnp.float32) / width)
    angles = positions.astype(jnp.float32)[:, None] * frequency[None, :]
    return (jnp.cos(angles), jnp.sin(angles))


def rotate(values, cosine_table, sine_table):
    half_width = values.shape[-1] // 2
    first_half = values[..., :half_width]
    second = values[..., half_width:]
    return jnp.concatenate(
        [
            first_half * cosine_table - second * sine_table,
            second * cosine_table + first_half * sine_table,
        ],
        axis=-1,
    )


def positions_of(group_ids):
    length = group_ids.shape[0]
    token_index = jnp.arange(length, dtype=jnp.int32)
    labels = jnp.arange(CONTS + 1, dtype=jnp.int32)
    member = (group_ids[:, None] == labels[None, :]).astype(jnp.int32)
    counts = jnp.sum(member, axis=0)
    starts = jnp.cumsum(counts) - counts
    start_of = jnp.sum(member * starts[None, :], axis=1)
    return token_index - start_of + jnp.where(group_ids > 0, counts[0], 0)


def kept_pairs(choice_ids, rank_row, choice_hot, capacity):
    row_count, top_count, expert_total = choice_hot.shape
    per_k = jnp.sum(choice_hot, axis=0)
    before_k = jnp.cumsum(per_k, axis=0) - per_k
    lower = (rank_row[None, :] < rank_row[:, None]).astype(F32)
    same_k = jnp.dot(
        lower.astype(BF),
        choice_hot.reshape(row_count, top_count * expert_total).astype(BF),
        preferred_element_type=F32,
    ).reshape(row_count, top_count, expert_total)
    place = jnp.sum((same_k + before_k[None]) * choice_hot, axis=-1)
    return (place < capacity).astype(F32)


def mm(a, b):
    return jnp.dot(a, b, preferred_element_type=F32)


def mm_nt(a, b):
    return lax.dot_general(a, b, (((1,), (1,)), ((), ())), preferred_element_type=F32)


def mm_tn(a, b):
    return lax.dot_general(a, b, (((0,), (0,)), ((), ())), preferred_element_type=F32)


def gather(value, axes):
    return lax.all_gather(value, axes, axis=0, tiled=True)


def scatter_sum(value, axes):
    return lax.psum_scatter(value, axes, scatter_dimension=0, tiled=True)


HBM = pl.BlockSpec(memory_space=pl.ANY)
VMEM = pl.BlockSpec(memory_space=pltpu.VMEM)


class Place:
    def __init__(self):
        e, s = lax.axis_index("expert"), lax.axis_index("shard")
        self.z, self.y, self.x, self.c = e // 2, e % 2, s // 2, s % 2

    def at(self, z=None, y=None, x=None, c=None):
        z = self.z if z is None else z
        y = self.y if y is None else y
        x = self.x if x is None else x
        c = self.c if c is None else c
        return {"expert": 2 * z + y, "shard": 2 * x + c}


def greet(partners):
    barrier = pltpu.get_barrier_semaphore()
    for partner in partners:
        pl.semaphore_signal(
            barrier, inc=1, device_id=partner, device_id_type=pl.DeviceIdType.MESH
        )
    pl.semaphore_wait(barrier, len(partners))


def remote(src, dst, send, recv, where):
    return pltpu.make_async_remote_copy(
        src_ref=src,
        dst_ref=dst,
        send_sem=send,
        recv_sem=recv,
        device_id=where,
        device_id_type=pl.DeviceIdType.MESH,
    )


def gather_group_kernel(cuts, spans, *refs):
    refs = list(refs)
    take = lambda n: [refs.pop(0) for _ in range(n)]
    (src,) = take(1)
    work = take(4) if spans else None
    (dst,) = take(1)
    made = take(3) if spans else None
    own_sem, send, recv = take(3)
    me = Place()
    x, c = me.x, me.c
    to_x, to_c = me.at(x=1 - x), me.at(c=1 - c)
    greet([to_x, to_c])
    cut = src.shape[0] // cuts
    span = lambda k: pl.ds(k * cut, cut)
    own = pltpu.make_async_copy(src, dst.at[x, c], own_sem)
    own.start()
    over_x = [
        remote(src.at[span(k)], dst.at[x, c, span(k)], send.at[0, k], recv.at[0, k], to_x)
        for k in range(cuts)
    ]
    for copy in over_x:
        copy.start()
    over_c = remote(src, dst.at[x, c], send.at[1, 0], recv.at[1, 0], to_c)
    over_c.start()
    if spans:
        turns, begin_work, work_turn = grad_worker(work, made, refs[:3], refs[3], spans)
        begin_work()

        @pl.loop(0, turns)
        def _(n):
            work_turn(n)

    relays = []
    for k in range(cuts):
        far = dst.at[1 - x, c, span(k)]
        remote(far, far, send.at[0, k], recv.at[0, k], to_x).wait_recv()
        relays.append(remote(far, far, send.at[2, k], recv.at[2, k], to_c))
        relays[-1].start()
    far = dst.at[x, 1 - c]
    remote(far, far, send.at[1, 0], recv.at[1, 0], to_c).wait_recv()
    for k in range(cuts):
        far = dst.at[1 - x, 1 - c, span(k)]
        remote(far, far, send.at[2, k], recv.at[2, k], to_c).wait_recv()
    own.wait()
    for copy in over_x + [over_c] + relays:
        copy.wait_send()


def gather_group(value, ident, work=None, spans=None, lines=None, cuts=4):
    rows, width = value.shape
    dma = pltpu.SemaphoreType.DMA
    inputs, in_specs = [value], [HBM]
    outs = [jax.ShapeDtypeStruct((2, 2, rows, width), value.dtype)]
    scratch = [dma, dma((3, cuts)), dma((3, cuts))]
    if work:
        inputs += work
        in_specs += [HBM] * 4
        shapes, buffers = work_shapes(work, spans, lines)
        outs += shapes
        scratch += buffers
    out, *made = pl.pallas_call(
        functools.partial(gather_group_kernel, cuts, spans if work else None),
        out_shape=outs,
        in_specs=in_specs,
        out_specs=[HBM] + [VMEM] * (len(outs) - 1),
        scratch_shapes=scratch,
        compiler_params=pltpu.CompilerParams(
            collective_id=ident, has_side_effects=True, vmem_limit_bytes=40 << 20
        ),
    )(*inputs)
    return [out.reshape(4 * rows, width)] + made


def sum_group_kernel(cuts, part, out, cbuf, xbuf, xsum, cs, cr, xs, xr):
    me = Place()
    x, c = me.x, me.c
    rows, width = out.shape
    cut = rows // cuts
    to_x, to_c = me.at(x=1 - x), me.at(c=1 - c)
    greet([to_x, to_c])
    span = lambda k: pl.ds(k * cut, cut)
    core = lambda k, far: remote(
        part.at[1 - x if far else x, 1 - c, span(k)],
        cbuf.at[far, span(k)],
        cs.at[k, far],
        cr.at[k, far],
        to_c,
    )
    over = lambda k: remote(xsum.at[span(k)], xbuf.at[span(k)], xs.at[k], xr.at[k], to_x)
    for k in range(cuts):
        core(k, 1).start()
    for k in range(cuts):
        core(k, 0).start()

    def add(k, target, one, two):
        @pl.loop(0, cut // 16)
        def _(i):
            at = pl.ds(pl.multiple_of(k * cut + i * 16, 16), 16)
            target[at] = (one[at].astype(F32) + two[at].astype(F32)).astype(target.dtype)

    for k in range(cuts):
        core(k, 1).wait_recv()
        add(k, xsum, part.at[1 - x, c], cbuf.at[1])
        over(k).start()
    for k in range(cuts):
        core(k, 0).wait_recv()
        add(k, out, part.at[x, c], cbuf.at[0])
    for k in range(cuts):
        over(k).wait_recv()
        add(k, out, out, xbuf)
    for k in range(cuts):
        core(k, 1).wait_send()
        core(k, 0).wait_send()
        over(k).wait_send()


def sum_group(part, ident, cuts=4):
    rows, width = part.shape[0] // 4, part.shape[1]
    dma = pltpu.SemaphoreType.DMA
    buf = lambda *lead: pltpu.VMEM(lead + (rows, width), part.dtype)
    return pl.pallas_call(
        functools.partial(sum_group_kernel, cuts),
        out_shape=jax.ShapeDtypeStruct((rows, width), F32),
        in_specs=[VMEM],
        out_specs=VMEM,
        scratch_shapes=[
            buf(2), buf(), buf(),
            dma((cuts, 2)), dma((cuts, 2)), dma((cuts,)), dma((cuts,)),
        ],
        compiler_params=pltpu.CompilerParams(
            collective_id=ident, has_side_effects=True, vmem_limit_bytes=32 << 20
        ),
    )(part.reshape(2, 2, rows, width))


def rows_loop(target, act):
    if len(target.shape) > 2:
        for i in range(target.shape[0]):
            rows_loop(target.at[i], lambda at, i=i: act((i,) + at))
        return
    rows = target.shape[0]
    step = 16 if rows % 16 == 0 else rows

    @pl.loop(0, rows // step)
    def _(i):
        act((pl.ds(pl.multiple_of(i * step, step), step),))


def add_blocks(target, one, two):
    def act(at):
        target[at] = (one[at].astype(F32) + two[at].astype(F32)).astype(target.dtype)

    rows_loop(target, act)


def add_three(target, one, two, three):
    def act(at):
        total = one[at].astype(F32) + two[at].astype(F32) + three[at].astype(F32)
        target[at] = total.astype(target.dtype)

    rows_loop(target, act)


class Copies:
    def __init__(self):
        self.started = []

    def go(self, copy):
        copy.start()
        self.started.append(copy)

    def finish(self):
        for copy in self.started:
            copy.wait_send()


class LineGather:
    def __init__(self, me, lines, block, sems):
        self.z, self.lines, self.block, self.sems = me.z, lines, block, sems
        self.to = (me.at(z=lax.rem(me.z + 1, lines)), me.at(z=lax.rem(me.z + lines - 1, lines)))

    def place(self, way, distance):
        return self.z - distance if way == 0 else self.z + distance

    def comes(self, way, distance):
        place = self.place(way, distance)
        return place >= 0 if way == 0 else place < self.lines

    def goes(self, way, distance):
        on = self.z + 1 < self.lines if way == 0 else self.z >= 1
        return on & self.comes(way, distance - 1)

    def hop(self, way, distance, place):
        ref = self.block(place)
        send, recv = self.sems[2 * way], self.sems[2 * way + 1]
        return remote(ref, ref, send.at[distance], recv.at[distance], self.to[way])

    def start(self):
        for way in range(2):

            @pl.when(self.goes(way, 1))
            def _(way=way):
                self.hop(way, 1, self.z).start()

    def land(self, distance, then=None):
        for way in range(2):
            place = self.place(way, distance)

            @pl.when(self.comes(way, distance))
            def _(way=way, place=place):
                self.hop(way, distance, place).wait_recv()

                @pl.when(self.goes(way, distance + 1))
                def _():
                    self.hop(way, distance + 1, place).start()

                if then is not None:
                    then(place)

    def finish(self):
        for distance in range(1, self.lines):
            for way in range(2):

                @pl.when(self.goes(way, distance))
                def _(way=way, distance=distance):
                    self.hop(way, distance, self.place(way, distance - 1)).wait_send()


def start_kernel(lines, with_o, *refs):
    jobs = 3
    refs = list(refs)
    take = lambda n: [refs.pop(0) for _ in range(n)]
    tok, kva = take(2)
    sources = take(jobs)
    o_src = take(1)[0] if with_o else None
    tok_dst, kva_dst = take(2)
    dests = take(jobs)
    o_dst = take(1)[0] if with_o else None
    own_sem, gs, gr, ys, yr, ts, tr, ks, kr = take(9)
    line_sems = [take(4) for _ in range(jobs + 1 + with_o)]
    if with_o:
        o_own, ocs, ocr = take(3)
    me = Place()
    z, y, x, c = me.z, me.y, me.x, me.c
    near = [(x, 1 - c), (1 - x, c), (1 - x, 1 - c)]
    to_near = [me.at(x=xx, c=cc) for xx, cc in near]
    to_y, to_x, to_c = me.at(y=1 - y), to_near[1], to_near[0]
    last, kva_at, o_at = jobs - 1, jobs, jobs + 1
    wide_lines = [
        LineGather(me, lines, lambda p, i=i: dests[i].at[p], line_sems[i]) for i in range(last)
    ]
    q_line = LineGather(me, lines, lambda p: dests[last].at[p, y], line_sems[last])
    kva_line = LineGather(me, lines, lambda p: kva_dst.at[p, y, x, c], line_sems[kva_at])
    greet([*q_line.to, to_y] + to_near)
    copies = Copies()
    go = copies.go

    def over_y(i, p):
        if i < last:
            block = dests[i].at[z, y]
        elif i == last:
            block = dests[i].at[p, y]
        elif i == kva_at:
            block = kva_dst.at[p, y, x, c]
        else:
            block = o_dst.at[p]
        return remote(block, block, ys.at[i, p], yr.at[i, p], to_y)

    def from_y(i, p):
        if i < last:
            block = dests[i].at[z, 1 - y]
        elif i == last:
            block = dests[i].at[p, 1 - y]
        elif i == kva_at:
            block = kva_dst.at[p, 1 - y, x, c]
        else:
            block = o_dst.at[p]
        return remote(block, block, ys.at[i, p], yr.at[i, p], to_y)

    locals_ = [
        pltpu.make_async_copy(sources[i].at[x, c], dests[i].at[z, y, x, c], own_sem.at[i])
        for i in range(jobs)
    ]
    locals_.append(pltpu.make_async_copy(kva, kva_dst.at[z, y, x, c], own_sem.at[jobs]))
    locals_.append(pltpu.make_async_copy(tok, tok_dst.at[x, c], own_sem.at[jobs + 1]))
    for copy in locals_:
        copy.start()
    for i in (last, *range(last)):
        for p in range(3):
            go(
                remote(
                    sources[i].at[near[p][0], near[p][1]],
                    dests[i].at[z, y, x, c],
                    gs.at[i, p],
                    gr.at[i, p],
                    to_near[p],
                )
            )
    if with_o:
        o_core = remote(o_src, o_dst.at[z, c], ocs, ocr, to_c)
        o_local = pltpu.make_async_copy(o_src, o_dst.at[z, c], o_own)
        o_line = LineGather(me, lines, lambda p: o_dst.at[p], line_sems[o_at])
        holder = c == y

        @pl.when(jnp.logical_not(holder))
        def _():
            o_core.start()

        @pl.when(holder)
        def _():
            o_local.start()

    go(remote(tok, tok_dst.at[x, c], ts.at[1], tr.at[1], to_x))
    go(remote(tok, tok_dst.at[x, c], ts.at[0], tr.at[0], to_c))

    def near_land(i):
        locals_[i].wait()
        for p in range(3):
            xx, cc = near[p]
            block = dests[i].at[z, y, xx, cc]
            remote(block, block, gs.at[i, p], gr.at[i, p], to_near[p]).wait_recv()

    locals_[jobs].wait()
    kva_line.start()
    go(over_y(kva_at, z))
    near_land(last)
    q_line.start()
    go(over_y(last, z))
    for i in range(last):
        near_land(i)
        go(over_y(i, z))
    if with_o:

        @pl.when(holder)
        def _():
            o_local.wait()
            block = o_dst.at[z, 1 - c]
            remote(block, block, ocs, ocr, to_c).wait_recv()
            o_line.start()
            over_y(o_at, z).start()

    for distance in range(1, lines):
        kva_line.land(distance, lambda p: over_y(kva_at, p).start())
    block = tok_dst.at[1 - x, c]
    remote(block, block, ts.at[1], tr.at[1], to_x).wait_recv()
    go(remote(block, block, ts.at[2], tr.at[2], to_c))
    for distance in range(1, lines):
        q_line.land(distance, lambda p: over_y(last, p).start())
        if with_o:

            @pl.when(holder)
            def _(distance=distance):
                o_line.land(distance, lambda p: over_y(o_at, p).start())

        if distance == 1:
            for p in range(lines):
                from_y(kva_at, p).wait_recv()
            plane = kva_dst.at[:, :, x, c]
            go(remote(plane, plane, ks.at[0], kr.at[0], to_x))
            go(remote(plane, plane, ks.at[1], kr.at[1], to_c))
        if distance == lines - 2:
            for i in range(last):
                from_y(i, z).wait_recv()
                wide_lines[i].start()
            plane = kva_dst.at[:, :, 1 - x, c]
            remote(plane, plane, ks.at[0], kr.at[0], to_x).wait_recv()
            go(remote(plane, plane, ks.at[2], kr.at[2], to_c))
    for distance in range(1, lines):
        for one in wide_lines:
            one.land(distance)
    for slot, xx in ((0, x), (2, 1 - x)):
        block = tok_dst.at[xx, 1 - c]
        remote(block, block, ts.at[slot], tr.at[slot], to_c).wait_recv()
    locals_[jobs + 1].wait()
    for p in range(lines):
        from_y(last, p).wait_recv()
    if with_o:

        @pl.when(jnp.logical_not(holder))
        def _():
            for p in range(lines):
                from_y(o_at, p).wait_recv()
            o_core.wait_send()

        @pl.when(holder)
        def _():
            for p in range(lines):
                over_y(o_at, p).wait_send()
            o_line.finish()

    for slot, xx in ((1, x), (2, 1 - x)):
        plane = kva_dst.at[:, :, xx, 1 - c]
        remote(plane, plane, ks.at[slot], kr.at[slot], to_c).wait_recv()
    for one in wide_lines + [q_line, kva_line]:
        one.finish()
    for i in (last, kva_at):
        for p in range(lines):

            @pl.when(z != p)
            def _(i=i, p=p):
                over_y(i, p).wait_send()

    copies.finish()


def start_gather(tokens, kva, column_parts, o_rows, lines, ident):
    jobs = len(column_parts)
    with_o = o_rows is not None
    inputs = [tokens, kva] + column_parts + ([o_rows] if with_o else [])
    shape = lambda lead, v: jax.ShapeDtypeStruct(lead + v.shape, v.dtype)
    outs = [shape((2, 2), tokens), shape((lines, 2, 2, 2), kva)]
    outs += [jax.ShapeDtypeStruct((lines, 2) + v.shape, v.dtype) for v in column_parts]
    if with_o:
        outs.append(shape((lines, 2), o_rows))
    dma = pltpu.SemaphoreType.DMA
    scratch = [
        dma((jobs + 2,)), dma((jobs, 3)), dma((jobs, 3)),
        dma((jobs + 2, lines)), dma((jobs + 2, lines)),
        dma((3,)), dma((3,)), dma((3,)), dma((3,)),
    ]
    scratch += [dma((lines,))] * (4 * (jobs + 1 + with_o))
    if with_o:
        scratch += [dma] * 3
    return pl.pallas_call(
        functools.partial(start_kernel, lines, with_o),
        out_shape=outs,
        in_specs=[HBM] * len(inputs),
        out_specs=[HBM] * len(outs),
        scratch_shapes=scratch,
        compiler_params=pltpu.CompilerParams(collective_id=ident, has_side_effects=True),
    )(*inputs)


def grad_worker(work, made, slots, ins, spans):
    values, cots, in_d, hid = work
    rows_in, cots_in, left_in = slots
    depth, width = rows_in.shape[1:]
    early = cots.shape[1]
    inner = hid.shape[1]
    turns = cots.shape[0] // depth
    first, units = spans[0][0], left_in.shape[3]

    def loads(n):
        at = pl.ds(pl.multiple_of(n * depth, depth), depth)
        slot = lax.rem(n, 2)
        pairs = (
            (values.at[at, pl.ds(0, width)], rows_in.at[slot]),
            (cots.at[at], cots_in.at[slot, :, pl.ds(0, early)]),
            (
                values.at[at, pl.ds(width + 128, width - early)],
                cots_in.at[slot, :, pl.ds(early, width - early)],
            ),
            (in_d.at[at, pl.ds(first, units)], left_in.at[slot, 0]),
            (in_d.at[at, pl.ds(inner + first, units)], left_in.at[slot, 1]),
            (hid.at[at, pl.ds(first, units)], left_in.at[slot, 2]),
        )
        return [
            pltpu.make_async_copy(src, dst, ins.at[slot, i]) for i, (src, dst) in enumerate(pairs)
        ]

    def begin():
        for copy in loads(0):
            copy.start()
        for ref in made:
            for i in range(ref.shape[0]):
                ref[i] = jnp.zeros(ref.shape[1:], F32)

    def turn(n):
        slot = lax.rem(n, 2)

        @pl.when(n + 1 < turns)
        def _():
            for copy in loads(n + 1):
                copy.start()

        for copy in loads(n):
            copy.wait()

        @pl.loop(0, width // 512)
        def _(m):
            at = pl.ds(pl.multiple_of(m * 512, 512), 512)
            for which, right in enumerate((rows_in, rows_in, cots_in)):
                ref = made[which]
                part = lax.dot_general(
                    left_in[slot, which],
                    right[slot, :, at],
                    (((0,), (0,)), ((), ())),
                    preferred_element_type=F32,
                )
                for i, (begin, _, kept) in enumerate(spans):
                    begin = begin - first
                    ref[i, :, at] = ref[i, :, at] + part[begin : begin + kept]

    return turns, begin, turn


def work_shapes(work, spans, lines):
    count, width = work[1].shape[0], work[0].shape[1] - 128
    width = (width + work[1].shape[1]) // 2
    units = sum(size for _, size, _ in spans)
    depth = min(512, count // lines)
    shapes = [jax.ShapeDtypeStruct((len(spans), spans[0][2], width), F32)] * 3
    rows = pltpu.VMEM((2, depth, width), BF)
    buffers = [rows, rows, pltpu.VMEM((2, 3, depth, units), BF), pltpu.SemaphoreType.DMA((2, 6))]
    return shapes, buffers


def grads_kernel(lines, plane, with_o, spans, *refs):
    jobs = 4
    refs = list(refs)
    take = lambda n: [refs.pop(0) for _ in range(n)]
    parts = take(jobs)
    (rows_part,) = take(1)
    o_part = take(1)[0] if with_o else None
    work = take(4) if spans else None
    outs = take(jobs)
    (rows_out,) = take(1)
    o_out = take(1)[0] if with_o else None
    made = take(3) if spans else None
    ybufs, zbufs, tots = take(jobs), take(jobs), take(jobs)
    p_own, p_core, p_x, r_own, r_core, r_x = take(6)
    ys, yr, zs, zr, gs, gr, ls, ss, sr = take(9)
    if with_o:
        o_ybuf, o_zbuf, o_tot, oys, oyr, ozs, ozr, ocs, ocr = take(9)
    if spans:
        rows_in, cots_in, left_in, ins = take(4)
    me = Place()
    z, y, x, c = me.z, me.y, me.x, me.c
    others = [lax.rem(z + 1 + j, lines) for j in range(lines - 1)]
    places = list(enumerate(others)) + [(lines - 1, z)]
    near = [(x, 1 - c), (1 - x, c), (1 - x, 1 - c)]
    to_near = [me.at(x=xx, c=cc) for xx, cc in near]
    to_y, to_x, to_c = me.at(y=1 - y), to_near[1], to_near[0]
    greet([me.at(z=o) for o in others] + [to_y] + to_near)
    copies = Copies()
    go = copies.go
    plain = [i for i in range(jobs) if i != plane]

    group = (
        (parts[plane], p_own, p_core, p_x, lambda ref, xx, cc: ref.at[:, :, xx, cc]),
        (rows_part, r_own, r_core, r_x, lambda ref, xx, cc: ref.at[xx, cc]),
    )
    core_copy = lambda i, far: remote(
        group[i][4](group[i][0], 1 - x if far else x, 1 - c),
        group[i][2].at[far],
        ss.at[i, far],
        sr.at[i, far],
        to_c,
    )
    own_copy = lambda i, far: pltpu.make_async_copy(
        group[i][4](group[i][0], 1 - x if far else x, c), group[i][1].at[far], ls.at[i, far]
    )
    x_copy = lambda i: remote(group[i][1].at[1], group[i][3], ss.at[i, 2], sr.at[i, 2], to_x)
    for far in (1, 0):
        for i in range(2):
            go(core_copy(i, far))
            own_copy(i, far).start()

    def over_y(i, j, o):
        source = p_own.at[0, o, 1 - y] if i == plane else parts[i].at[o, 1 - y]
        return remote(source, ybufs[i].at[o], ys.at[i, j], yr.at[i, o], to_y)

    def over_z(i, j, o):
        return remote(ybufs[i].at[o], zbufs[i].at[z], zs.at[i, j], zr.at[i, z], me.at(z=o))

    if with_o:
        holder = c == y
        o_over_y = lambda j, o: remote(o_part.at[o], o_ybuf.at[o], oys.at[j], oyr.at[o], to_y)
        o_over_z = lambda j, o: remote(
            o_ybuf.at[o], o_zbuf.at[z], ozs.at[j], ozr.at[z], me.at(z=o)
        )
    for j, o in places:
        for i in plain:
            go(over_y(i, j, o))
        if with_o:

            @pl.when(jnp.logical_not(holder))
            def _(j=j, o=o):
                o_over_y(j, o).start()

    if spans:
        turns, begin_work, work_turn = grad_worker(work, made, (rows_in, cots_in, left_in), ins, spans)
        begin_work()

    @pl.loop(0, lines)
    def _(j):
        if spans:
            per_line = turns // lines

            @pl.loop(0, per_line)
            def _(n):
                work_turn(j * per_line + n)

        @pl.when(j == 0)
        def _():
            for i in range(2):
                core_copy(i, 1).wait_recv()
                own_copy(i, 1).wait()
                add_blocks(group[i][1].at[1], group[i][1].at[1], group[i][2].at[1])
                x_copy(i).start()

        @pl.when(j == 1)
        def _():
            core_copy(0, 0).wait_recv()
            own_copy(0, 0).wait()
            x_copy(0).wait_recv()
            add_three(p_own.at[0], p_own.at[0], p_core.at[0], p_x)
            for k, o in places:
                over_y(plane, k, o).start()

        @pl.when(j == 2)
        def _():
            core_copy(1, 0).wait_recv()
            own_copy(1, 0).wait()
            x_copy(1).wait_recv()
            add_three(rows_out, r_own.at[0], r_core.at[0], r_x)

        o = lax.rem(z + 1 + j, lines)
        for i in plain:
            over_y(i, j, o).wait_recv()
            add_blocks(ybufs[i].at[o], parts[i].at[o, y], ybufs[i].at[o])

            @pl.when(j < lines - 1)
            def _(i=i):
                over_z(i, j, o).start()

        if with_o:

            @pl.when(holder)
            def _():
                o_over_y(j, o).wait_recv()
                add_blocks(o_ybuf.at[o], o_part.at[o], o_ybuf.at[o])

                @pl.when(j < lines - 1)
                def _():
                    o_over_z(j, o).start()

    for j, o in places:
        over_y(plane, j, o).wait_recv()
        add_blocks(ybufs[plane].at[o], p_own.at[0, o, y], ybufs[plane].at[o])
        if j < lines - 1:
            over_z(plane, j, o).start()

    def line_sum(target, acc, zbuf):
        if len(target.shape) > 2:
            for k in range(target.shape[0]):
                line_sum(target.at[k], acc.at[:, k], zbuf.at[:, k])
            return
        rows = target.shape[0]
        step = 16 if rows % 16 == 0 else rows

        @pl.loop(0, rows // step)
        def _(i):
            at = pl.ds(pl.multiple_of(i * step, step), step)
            value = acc[z, at].astype(F32)
            for o in others:
                value = value + zbuf[o, at].astype(F32)
            target[at] = value.astype(target.dtype)

    near_copy = lambda i, p: remote(
        tots[i].at[near[p][0], near[p][1]], outs[i].at[x, c], gs.at[i, p], gr.at[i, p], to_near[p]
    )
    for i in plain + [plane]:
        for j, o in places[:-1]:
            block = zbufs[i].at[o]
            remote(block, block, zs.at[i, j], zr.at[i, o], me.at(z=o)).wait_recv()
        if i == plane:
            line_sum(outs[i], ybufs[i], zbufs[i])
        else:
            line_sum(tots[i], ybufs[i], zbufs[i])
            for p in range(3):
                go(near_copy(i, p))
            outs[i][x, c] = tots[i][x, c]
    if with_o:
        o_core = remote(o_tot.at[1 - c], o_out, ocs, ocr, to_c)

        @pl.when(holder)
        def _():
            for j, o in places[:-1]:
                block = o_zbuf.at[o]
                remote(block, block, ozs.at[j], ozr.at[o], me.at(z=o)).wait_recv()
            line_sum(o_tot.at[1 - c], o_ybuf.at[:, 1 - c], o_zbuf.at[:, 1 - c])
            o_core.start()
            line_sum(o_out, o_ybuf.at[:, c], o_zbuf.at[:, c])
            for j, o in places[:-1]:
                o_over_z(j, o).wait_send()
            o_core.wait_send()

        @pl.when(jnp.logical_not(holder))
        def _():
            for j, o in places:
                o_over_y(j, o).wait_send()
            o_core.wait_recv()

    for i in plain:
        for p in range(3):
            block = outs[i].at[near[p][0], near[p][1]]
            remote(block, block, gs.at[i, p], gr.at[i, p], to_near[p]).wait_recv()
    for i in range(jobs):
        for j, o in places[:-1]:
            over_z(i, j, o).wait_send()
    for j, o in places:
        over_y(plane, j, o).wait_send()
    for i in range(2):
        x_copy(i).wait_send()
    copies.finish()


def sum_grads(parts, plane, rows_part, o_part, lines, ident, work=None, spans=None):
    jobs = len(parts)
    with_o = o_part is not None
    inputs = list(parts) + [rows_part] + ([o_part] if with_o else [])
    in_specs = [HBM if i == plane else VMEM for i in range(jobs)] + [HBM] + [VMEM] * with_o
    block = lambda i: parts[i].shape[4:] if i == plane else parts[i].shape[2:]
    outs = [jax.ShapeDtypeStruct(block(i), parts[i].dtype) for i in range(jobs)]
    outs.append(jax.ShapeDtypeStruct(rows_part.shape[2:], F32))
    if with_o:
        outs.append(jax.ShapeDtypeStruct(o_part.shape[2:], o_part.dtype))
    dma = pltpu.SemaphoreType.DMA
    buf = lambda lead, i: pltpu.VMEM(lead + block(i), parts[i].dtype)
    scratch = [buf((lines,), i) for i in range(jobs)] * 2
    scratch += [pltpu.VMEM((8, 128), BF) if i == plane else buf((), i) for i in range(jobs)]
    scratch += [buf((2, lines, 2), plane), buf((2, lines, 2), plane), buf((lines, 2), plane)]
    rows = lambda *lead: pltpu.VMEM(lead + rows_part.shape[2:], rows_part.dtype)
    scratch += [rows(2), rows(2), rows()]
    scratch += [dma((jobs, lines))] * 4 + [dma((jobs, 3))] * 2
    scratch += [dma((2, 2)), dma((2, 3)), dma((2, 3))]
    if with_o:
        scratch += [pltpu.VMEM(o_part.shape, o_part.dtype)] * 2
        scratch += [pltpu.VMEM(o_part.shape[1:], o_part.dtype)]
        scratch += [dma((lines,))] * 4 + [dma, dma]
    out_specs = [VMEM] * len(outs)
    if work:
        inputs += work
        in_specs += [HBM] * 4
        shapes, buffers = work_shapes(work, spans, lines)
        outs += shapes
        out_specs += [VMEM] * 3
        scratch += buffers
    return pl.pallas_call(
        functools.partial(grads_kernel, lines, plane, with_o, spans if work else None),
        out_shape=outs,
        in_specs=in_specs,
        out_specs=out_specs,
        scratch_shapes=scratch,
        compiler_params=pltpu.CompilerParams(
            collective_id=ident, has_side_effects=True, vmem_limit_bytes=63 << 20
        ),
    )(*inputs)


def nt(a, b):
    return lax.dot_general(a, b, (((1,), (1,)), ((), ())), preferred_element_type=F32)


def hidden_kernel(
    lines, chunks, spans, local_experts,
    src, cots, spread, e_gate, e_up, e_down, s_in, s_down,
    dst, hid, in_d, gate_g, w_in_out, parts,
    h_in, c_in, hid_out, in_out, g_out, part_out, w_in, w_down,
    w_sem, own_sem, hs, cins, sts, zs, zr, xs, xr, ys, yr, ds_, dr, cs, cr,
):
    me = Place()
    z, y, x, c = me.z, me.y, me.x, me.c
    expert_at = 2 * z + y
    rows, wide = src.shape
    width, early = w_down.shape[1], cots.shape[-1]
    inner = w_down.shape[0]
    step_rows = rows // chunks
    units = lines * 2 * step_rows
    others = [lax.rem(z + 1 + j, lines) for j in range(lines - 1)]
    places = [(lines - 1, z)] + list(reversed(list(enumerate(others))))
    to_x, to_y, to_c = me.at(x=1 - x), me.at(y=1 - y), me.at(c=1 - c)
    greet([me.at(z=o) for o in others] + [to_x, to_y, to_c])
    half = wide // 256 * 128
    cuts = (pl.ds(0, half), pl.ds(half, wide - half))
    side_of = lambda side: (lax.rem(y + side // 2, 2), lax.rem(x + lax.rem(side, 2), 2))

    def span(k):
        return pl.ds(pl.multiple_of(k * step_rows, step_rows), step_rows)

    def block(zz, yy, xx, k, cols=None):
        if cols is None:
            return dst.at[zz, yy, xx, c, span(k)]
        return dst.at[zz, yy, xx, c, span(k), cuts[cols]]

    own = pltpu.make_async_copy(src, dst.at[z, y, x, c], own_sem)
    own.start()
    piece = lambda k: src.at[span(k)]
    z_copy = lambda k, j, o: remote(
        piece(k), block(z, y, x, k), zs.at[k, j], zr.at[k, z], me.at(z=o)
    )
    x_copy = lambda k, j, o, b: remote(b, block(o, y, x, k), xs.at[k, j], xr.at[k, o], to_x)
    y_copy = lambda k, j, o, b: remote(b, block(o, y, x, k), ys.at[k, j], yr.at[k, o], to_y)

    def diag_copy(k, j, o, h):
        b = block(o, y, 1 - x, k, 0) if h == 0 else block(o, 1 - y, x, k, 1)
        return remote(b, b, ds_.at[k, j, h], dr.at[k, o, h], to_y if h == 0 else to_x)

    def core_copy(k, side, cc):
        yy, xx = side_of(side)
        b = dst.at[:, yy, xx, cc, span(k)]
        return remote(b, b, cs.at[k, side], cr.at[k, side], to_c)

    def z_land(k):
        for j, o in places[1:]:
            b = block(o, y, x, k)
            remote(b, b, zs.at[k, j], zr.at[k, o], me.at(z=o)).wait_recv()
            x_copy(k, j, o, b).start()
            y_copy(k, j, o, b).start()
        core_copy(k, 0, c).start()

    def xy_land(k):
        for j, o in places:
            b = block(o, y, 1 - x, k)
            remote(b, b, xs.at[k, j], xr.at[k, o], to_x).wait_recv()
            diag_copy(k, j, o, 0).start()
            b = block(o, 1 - y, x, k)
            remote(b, b, ys.at[k, j], yr.at[k, o], to_y).wait_recv()
            diag_copy(k, j, o, 1).start()
        core_copy(k, 1, c).start()
        core_copy(k, 2, c).start()

    def diag_land(k):
        for j, o in places:
            for h, w in ((0, to_y), (1, to_x)):
                b = block(o, 1 - y, 1 - x, k, h)
                remote(b, b, ds_.at[k, j, h], dr.at[k, o, h], w).wait_recv()
        core_copy(k, 3, c).start()

    def loads(k, side):
        yy, xx = side_of(side)
        return (
            pltpu.make_async_copy(dst.at[:, yy, xx, :, span(k)], h_in.at[side], hs.at[side]),
            pltpu.make_async_copy(cots.at[:, yy, xx, :, span(k)], c_in.at[side], cins.at[side]),
        )

    def fetch(k, side):
        core_copy(k, side, 1 - c).wait_recv()
        for copy in loads(k, side):
            copy.start()

    def stores(k, side):
        yy, xx = side_of(side)
        pairs = ((hid_out, hid), (in_out, in_d), (g_out, gate_g), (part_out, parts))
        return [
            pltpu.make_async_copy(v.at[side], ref.at[:, yy, xx, :, span(k)], sts.at[side, i])
            for i, (v, ref) in enumerate(pairs)
        ]

    def unit(k, side):
        for copy in loads(k, side):
            copy.wait()
        h = h_in[side, :, :, :, :width].reshape(units, width)
        gates = h_in[side, :, :, :, width : width + 128].reshape(units, 128)
        late = h_in[side, :, :, :, width + 128 :].reshape(units, width - early)
        scale = jnp.dot(gates, spread[...], preferred_element_type=F32)
        both = nt(h, w_in[...])
        down = nt(c_in[side].reshape(units, early), w_down[:, :early])
        down = down + nt(late, w_down[:, early:])
        columns = lax.broadcasted_iota(jnp.int32, (units, 128), 1)
        sums = jnp.zeros((units, 128), F32)
        for i, (begin, size) in enumerate(spans):
            at = slice(begin, begin + size)
            up_at = slice(inner + begin, inner + begin + size)
            g, u, d = both[:, at], both[:, up_at], down[:, at]
            sig = 1.0 / (1.0 + jnp.exp(-g))
            act = g * sig
            value = (act * u).astype(BF).astype(F32)
            shape = (lines, 2, step_rows, size)
            if i < local_experts:
                total = jnp.sum(value * d, axis=1, keepdims=True)
                sums = jnp.where(columns == expert_at * local_experts + i, total, sums)
                value = value * scale[:, at]
                d = d * scale[:, at]
            hid_out[side, :, :, :, at] = value.astype(BF).reshape(shape)
            in_out[side, :, :, :, at] = (
                (d * u * (sig + act * (1.0 - sig))).astype(BF).reshape(shape)
            )
            in_out[side, :, :, :, up_at] = (d * act).astype(BF).reshape(shape)
        g_out[side] = sums.astype(BF).reshape(lines, 2, step_rows, 128)
        hidden = hid_out[side].reshape(units, inner)
        for begin in range(0, width, 512):
            at = slice(begin, begin + 512)
            part = jnp.dot(hidden, w_down[:, at], preferred_element_type=F32)
            part_out[side, :, :, :, at] = part.astype(BF).reshape(lines, 2, step_rows, 512)
        for copy in stores(k, side):
            copy.start()

    def z_start(k):
        for j, o in enumerate(others):
            z_copy(k, j, o).start()

    z_start(0)
    if chunks > 1:
        z_start(1)
    for k in range(chunks):
        x_copy(k, lines - 1, z, piece(k)).start()
        y_copy(k, lines - 1, z, piece(k)).start()

    fills = []
    for i, (begin, size) in enumerate(spans):
        for target, start, source in (
            (w_in, 0, e_gate.at[i] if i < local_experts else s_in.at[0]),
            (w_in, inner, e_up.at[i] if i < local_experts else s_in.at[1]),
            (w_down, 0, e_down.at[i] if i < local_experts else s_down),
        ):
            held = source.shape[0]
            fills.append(
                pltpu.make_async_copy(
                    source, target.at[pl.ds(start + begin, held)], w_sem.at[2 + len(fills)]
                )
            )
            fills[-1].start()
            if size > held:
                target[start + begin + held : start + begin + size] = jnp.zeros(
                    (size - held, width), BF
                )
    for copy in fills:
        copy.wait()
    keep = pltpu.make_async_copy(w_in, w_in_out, w_sem.at[0])
    keep.start()

    own.wait()
    z_land(0)
    fetch(0, 0)
    valid = lambda k: (k >= 0) & (k < chunks)

    @pl.loop(0, chunks + 2)
    def _(t):
        @pl.loop(0, 4)
        def _(side):
            k = t - (side + 1) // 2

            @pl.when(valid(k))
            def _():
                @pl.when(k >= 1)
                def _():
                    for copy in stores(k - 1, side):
                        copy.wait()

                unit(k, side)

            @pl.when((side == 0) & valid(t - 1))
            def _():
                fetch(t - 1, 2)

            @pl.when((side == 1) & valid(t - 2))
            def _():
                fetch(t - 2, 3)

        @pl.when(valid(t + 1))
        def _():
            z_land(t + 1)

        @pl.when(valid(t + 2))
        def _():
            z_start(t + 2)

        @pl.when(valid(t))
        def _():
            xy_land(t)

        @pl.when(valid(t + 1))
        def _():
            fetch(t + 1, 0)

        @pl.when(valid(t - 1))
        def _():
            diag_land(t - 1)

        @pl.when(valid(t))
        def _():
            fetch(t, 1)

    keep.wait()
    for side in range(4):
        for copy in stores(chunks - 1, side):
            copy.wait()

    @pl.loop(0, chunks)
    def _(k):
        for j, o in enumerate(others):
            z_copy(k, j, o).wait_send()
        for j, o in places:
            b = piece(k) if j == lines - 1 else block(o, y, x, k)
            x_copy(k, j, o, b).wait_send()
            y_copy(k, j, o, b).wait_send()
            diag_copy(k, j, o, 0).wait_send()
            diag_copy(k, j, o, 1).wait_send()
        for side in range(4):
            core_copy(k, side, c).wait_send()


def gather_hidden(
    value, cots, spread, e_gate, e_up, e_down, s_in, s_down, spans, local_experts, lines, ident
):
    rows, wide = value.shape
    width, early = e_down.shape[2], cots.shape[1]
    inner = spans[-1][0] + spans[-1][1]
    step_rows = min(rows, max(16, 128 // lines))
    chunks = rows // step_rows
    lead = (lines, 2, 2, 2, rows)
    dma = pltpu.SemaphoreType.DMA
    slot = lambda n: pltpu.VMEM((4, lines, 2, step_rows, n), BF)
    line = dma((chunks, lines))
    return pl.pallas_call(
        functools.partial(hidden_kernel, lines, chunks, spans, local_experts),
        out_shape=[
            jax.ShapeDtypeStruct(lead + (n,), BF) for n in (wide, inner, 2 * inner, 128)
        ]
        + [
            jax.ShapeDtypeStruct((2 * inner, width), BF),
            jax.ShapeDtypeStruct(lead + (width,), BF),
        ],
        in_specs=[HBM, HBM, VMEM] + [HBM] * 5,
        out_specs=[HBM] * 6,
        scratch_shapes=[
            slot(wide), slot(early), slot(inner), slot(2 * inner), slot(128), slot(width),
            pltpu.VMEM((2 * inner, width), BF), pltpu.VMEM((inner, width), BF),
            dma((2 + 3 * len(spans),)), dma, dma((4,)), dma((4,)), dma((4, 4)),
            line, line, line, line, line, line,
            dma((chunks, lines, 2)), dma((chunks, lines, 2)), dma((chunks, 4)), dma((chunks, 4)),
        ],
        compiler_params=pltpu.CompilerParams(
            collective_id=ident, has_side_effects=True, vmem_limit_bytes=60 << 20
        ),
    )(value, cots.reshape(lead + (early,)), spread, e_gate, e_up, e_down, s_in, s_down)


def back_kernel(
    lines,
    in_d, gate_g, w_in, passed,
    out, passed_on,
    d_in, g_in, sbuf, acc, cbuf, xbuf, ybuf, zbuf, xdiag, ydiag,
    ins, cs, cr, xs, xr, ys, yr, zs, zr, xds, xdr, yds, ydr,
):
    me = Place()
    z, y, x, c = me.z, me.y, me.x, me.c
    rows, wide = out.shape
    width = wide - 128
    half = wide // 256 * 128
    others = [lax.rem(z + 1 + j, lines) for j in range(lines - 1)]
    to_x, to_y, to_c = me.at(x=1 - x), me.at(y=1 - y), me.at(c=1 - c)
    greet([me.at(z=o) for o in others] + [to_x, to_y, to_c])
    cols = (pl.ds(0, half), pl.ds(half, wide - half))
    lag = (0, 1, 1, 2)
    place = lambda n: lax.rem(z + 1 + n, lines)

    def side_of(side):
        return (
            lax.rem(y + 1 - side // 2, 2),
            lax.rem(x + 1 - lax.rem(side, 2), 2),
        )

    def loads(n, side):
        yy, xx = side_of(side)
        pairs = ((in_d, d_in), (gate_g, g_in))
        return [
            pltpu.make_async_copy(ref.at[place(n), yy, xx], v.at[side], ins.at[side, i])
            for i, (ref, v) in enumerate(pairs)
        ]

    def to_core(n, side):
        yy, xx = side_of(side)
        return remote(
            sbuf.at[side], cbuf.at[place(n), yy, xx], cs.at[side], cr.at[n, side], to_c
        )

    def unit(n, side):
        yy, xx = side_of(side)
        for copy in loads(n, side):
            copy.wait()
        grads = d_in[side].reshape(2 * rows, w_in.shape[0])
        piece = 512
        for begin in range(0, width, piece):
            at = slice(begin, begin + piece)
            back = jnp.dot(grads, w_in[:, at], preferred_element_type=F32).astype(BF).reshape(2, rows, piece)

            @pl.when(c == 0)
            def _():
                acc[place(n), yy, xx, :, at] = back[0]
                sbuf[side, :, at] = back[1]

            @pl.when(c == 1)
            def _():
                acc[place(n), yy, xx, :, at] = back[1]
                sbuf[side, :, at] = back[0]

        acc[place(n), yy, xx, :, width:] = g_in[side, c]
        sbuf[side, :, width:] = g_in[side, 1 - c]

    def sums(target, *terms):
        @pl.loop(0, rows // 16)
        def _(i):
            at = pl.ds(pl.multiple_of(i * 16, 16), 16)
            total = terms[0][at].astype(F32)
            for term in terms[1:]:
                total = total + term[at].astype(F32)
            target[at] = total.astype(BF)

    def diag_sends(n):
        o = place(n)
        far = acc.at[o, 1 - y, 1 - x]
        return (
            remote(far.at[:, cols[0]], xdiag.at[o], xds.at[n], xdr.at[n], to_x),
            remote(far.at[:, cols[1]], ydiag.at[o], yds.at[n], ydr.at[n], to_y),
        )

    def side_sends(n):
        o = place(n)
        return (
            remote(acc.at[o, y, 1 - x], xbuf.at[o], xs.at[n], xr.at[n], to_x),
            remote(acc.at[o, 1 - y, x], ybuf.at[o], ys.at[n], yr.at[n], to_y),
        )

    def z_copy(n):
        return remote(
            acc.at[place(n), y, x], zbuf.at[z], zs.at[n], zr.at[z], me.at(z=place(n))
        )

    def first(n):
        to_core(n, 0).wait_recv()
        mine, other = acc.at[place(n), 1 - y, 1 - x], cbuf.at[place(n), 1 - y, 1 - x]
        sums(mine, mine, other)
        for copy in diag_sends(n):
            copy.start()

    def second(n):
        o = place(n)
        mine, other = acc.at[o, 1 - y, x], cbuf.at[o, 1 - y, x]
        to_core(n, 1).wait_recv()
        diag_sends(n)[0].wait_recv()
        sums(mine.at[:, cols[0]], mine.at[:, cols[0]], other.at[:, cols[0]], xdiag.at[o])
        sums(mine.at[:, cols[1]], mine.at[:, cols[1]], other.at[:, cols[1]])
        side_sends(n)[1].start()

    def third(n):
        o = place(n)
        mine, other = acc.at[o, y, 1 - x], cbuf.at[o, y, 1 - x]
        to_core(n, 2).wait_recv()
        diag_sends(n)[1].wait_recv()
        sums(mine.at[:, cols[0]], mine.at[:, cols[0]], other.at[:, cols[0]])
        sums(mine.at[:, cols[1]], mine.at[:, cols[1]], other.at[:, cols[1]], ydiag.at[o])
        side_sends(n)[0].start()

    def fourth(n):
        o = place(n)
        mine, other = acc.at[o, y, x], cbuf.at[o, y, x]
        to_core(n, 3).wait_recv()
        for copy in side_sends(n):
            copy.wait_recv()
        sums(mine, mine, other, xbuf.at[o], ybuf.at[o])

        @pl.when(n < lines - 1)
        def _():
            z_copy(n).start()

    valid = lambda n: (n >= 0) & (n < lines)
    for side in range(4):
        for copy in loads(0, side):
            copy.start()

    @pl.loop(0, lines + 3)
    def _(t):
        @pl.loop(0, 4)
        def _(side):
            n = t - (side + 1) // 2

            @pl.when(valid(n))
            def _():
                @pl.when(n >= 1)
                def _():
                    to_core(n - 1, side).wait_send()

                unit(n, side)
                to_core(n, side).start()

                @pl.when(n + 1 < lines)
                def _():
                    for copy in loads(n + 1, side):
                        copy.start()

            for turn, (behind, act) in enumerate(((3, fourth), (0, first), (1, second), (1, third))):

                @pl.when((side == turn) & valid(t - behind))
                def _(behind=behind, act=act):
                    act(t - behind)

    for side in range(4):
        to_core(lines - 1, side).wait_send()
    for o in others:
        remote(zbuf.at[o], zbuf.at[o], zs.at[0], zr.at[o], me.at(z=o)).wait_recv()

    @pl.loop(0, rows // 16)
    def _(i):
        at = pl.ds(pl.multiple_of(i * 16, 16), 16)
        total = acc[z, y, x, at].astype(F32)
        for o in others:
            total = total + zbuf[o, at].astype(F32)
        out[at] = total

    @pl.loop(0, lines)
    def _(n):
        for copy in diag_sends(n) + side_sends(n):
            copy.wait_send()

        @pl.when(n < lines - 1)
        def _():
            z_copy(n).wait_send()


def layout_kernel(own_heads, q, kvb, kva, o, shared, q_out, kvb_out, kva_out, o_out, gate_out, up_out):
    for source, target in ((q, q_out), (kvb, kvb_out)):
        size = source.shape[3] // own_heads
        held = [[source[xx, cc].astype(F32) for cc in range(2)] for xx in range(2)]
        pieces = [
            held[xx][cc][:, i * size : (i + 1) * size]
            for i in range(own_heads)
            for cc in range(2)
            for xx in range(2)
        ]
        target[...] = jnp.concatenate(pieces, axis=1)
    kva_out[...] = kva[...].astype(F32)
    o_out[...] = o[...].astype(F32)
    for which, target in enumerate((gate_out, up_out)):
        pieces = [shared[i, which].astype(F32) for i in range(shared.shape[0])]
        target[...] = jnp.concatenate(pieces, axis=1)


def lay_out(q, kvb, kva, o, shared, own_heads):
    flat = lambda rows, columns: jax.ShapeDtypeStruct((rows, columns), F32)
    hidden = shared.shape[0] * shared.shape[3]
    return pl.pallas_call(
        functools.partial(layout_kernel, own_heads),
        out_shape=[
            flat(q.shape[2], 4 * q.shape[3]),
            flat(kvb.shape[2], 4 * kvb.shape[3]),
            flat(*kva.shape),
            flat(*o.shape),
            flat(shared.shape[2], hidden),
            flat(shared.shape[2], hidden),
        ],
        in_specs=[VMEM] * 5,
        out_specs=[VMEM] * 6,
        compiler_params=pltpu.CompilerParams(vmem_limit_bytes=32 << 20),
    )(q, kvb, kva, o, shared)


def sum_back(in_d, gate_g, w_in, passed, ident):
    lines, rows, inner = in_d.shape[0], in_d.shape[4], in_d.shape[5]
    width = w_in.shape[1]
    wide = width + 128
    half = wide // 256 * 128
    dma = pltpu.SemaphoreType.DMA
    buf = lambda *shape: pltpu.VMEM(shape, BF)
    line = dma((lines,))
    return pl.pallas_call(
        functools.partial(back_kernel, lines),
        out_shape=[
            jax.ShapeDtypeStruct((rows, wide), F32),
            jax.ShapeDtypeStruct(passed.shape, passed.dtype),
        ],
        in_specs=[HBM] * 2 + [VMEM, HBM],
        out_specs=[VMEM, HBM],
        input_output_aliases={3: 1},
        scratch_shapes=[
            buf(4, 2, rows, inner), buf(4, 2, rows, 128), buf(4, rows, wide),
            buf(lines, 2, 2, rows, wide), buf(lines, 2, 2, rows, wide),
            buf(lines, rows, wide), buf(lines, rows, wide), buf(lines, rows, wide),
            buf(lines, rows, half), buf(lines, rows, wide - half),
            dma((4, 2)), dma((4,)), dma((lines, 4)),
            line, line, line, line, line, line, line, line, line, line,
        ],
        compiler_params=pltpu.CompilerParams(
            collective_id=ident, has_side_effects=True, vmem_limit_bytes=60 << 20
        ),
    )(in_d, gate_g, w_in, passed)


def on_device(
    tokens,
    cotangent,
    norm1_gain,
    q_weight,
    kva_weight,
    kv_gain,
    kvb_weight,
    o_weight,
    norm2_gain,
    router_weight,
    shared_gate,
    shared_up,
    shared_down,
    expert_gate,
    expert_up,
    expert_down,
    expert_ids,
    token_rank,
    seq_ids,
):
    expert_count = lax.axis_size("expert")
    shard_count = lax.axis_size("shard")
    device_count = expert_count * shard_count
    expert_at = lax.axis_index("expert")
    shard_at = lax.axis_index("shard")
    tok_rows, width = tokens.shape
    group_len = seq_ids.shape[0]
    local_experts = expert_gate.shape[0]
    all_experts = local_experts * expert_count
    top_count = expert_ids.shape[1]
    capacity = max(2, tok_rows * top_count // all_experts)
    score_scale = (NOPE + ROPE) ** (-0.5)
    own_heads = HEADS // shard_count
    latent_width = kva_weight.shape[1]

    lines = expert_count // 2
    o_rows = o_weight.shape[0]
    o_pairs = VDIM == 2 * o_rows

    def by_head(weight):
        rows = weight.shape[0]
        heads = weight.reshape(rows, own_heads, 2, 2, weight.shape[1] // HEADS)
        return heads.transpose(3, 2, 0, 1, 4).reshape(2, 2, rows, weight.shape[1] // 4)

    small = [norm1_gain, norm2_gain, kv_gain, router_weight]
    small_sizes = [v.size for v in small]

    def pack(values):
        flat = jnp.concatenate(values, axis=-1)
        pad = -flat.shape[-1] % 2048
        flat = jnp.pad(flat, [(0, 0)] * (flat.ndim - 1) + [(0, pad)])
        return flat.reshape(flat.shape[:-1] + (-1, 128))

    def unpack(packed):
        flat = packed.reshape(packed.shape[:-2] + (-1,))
        starts = [sum(small_sizes[:i]) for i in range(len(small_sizes))]
        return [flat[..., b : b + n] for b, n in zip(starts, small_sizes)]

    shared_width = shared_down.shape[0]
    both_shared = jnp.stack([shared_gate, shared_up]).reshape(
        2, shared_gate.shape[0], device_count, shared_width
    )
    both_shared = lax.all_to_all(
        both_shared.transpose(2, 0, 1, 3), BOTH, split_axis=0, concat_axis=0
    )
    both_shared = both_shared.transpose(1, 0, 2, 3).reshape(2, width, shared_width)
    small_own = pack([v.reshape(-1) for v in small])
    rounds = max(1, tok_rows * device_count // 4096)
    started = start_gather(
        tokens,
        kva_weight,
        [
            jnp.broadcast_to(small_own, (2, 2) + small_own.shape),
            by_head(kvb_weight),
            by_head(q_weight),
        ],
        o_weight if o_pairs else None,
        lines,
        1,
    )
    group_tokens = started[0].reshape(group_len, width)
    kva_all = started[1].reshape(width, latent_width)
    small_set, kvb_set, q_set, *o_set = started[2:]
    small_all = unpack(small_set.reshape((device_count,) + small_own.shape))
    kvb_mine = kvb_set.reshape(KV_RANK, -1)
    q_mine = q_set.reshape(width, -1)
    core_at, x_at = shard_at % 2, shard_at // 2
    if o_pairs:
        o_mine = o_set[0].reshape(own_heads * VDIM, width)
    else:
        o_mine = gather(o_weight, BOTH).reshape(own_heads, 2, 2, VDIM, width)
        o_mine = o_mine[:, core_at, x_at].reshape(own_heads * VDIM, width)
    norm1_scale, norm2_scale, latent_scale = [v.reshape(-1).astype(F32) for v in small_all[:3]]
    router = small_all[3].reshape(width, all_experts)

    positions = positions_of(seq_ids)
    cosine_table, sine_table = rope_tables(positions, ROPE)
    token_index = jnp.arange(group_len, dtype=jnp.int32)
    allowed = (token_index[None, :] <= token_index[:, None]) & (
        (seq_ids[None, :] == 0) | (seq_ids[None, :] == seq_ids[:, None])
    )
    input_rows = tokens.astype(F32)
    group_rows = group_tokens.astype(F32)
    normed_group, inverse_group = rms_forward(group_rows, norm1_scale)
    hidden_one = normed_group.astype(BF)
    query_raw = mm(hidden_one, q_mine).reshape(group_len, own_heads, NOPE + ROPE)
    q_nope = query_raw[:, :, :NOPE].astype(BF)
    q_rope = rotate(
        query_raw[:, :, NOPE:], cosine_table[:, None, :], sine_table[:, None, :]
    ).astype(BF)
    compressed = mm(hidden_one, kva_all)
    latent_norm, inverse_latent = rms_forward(compressed[:, :KV_RANK], latent_scale)
    latent = latent_norm.astype(BF)
    k_rope = rotate(compressed[:, KV_RANK:], cosine_table, sine_table).astype(BF)
    keyval = mm(latent, kvb_mine).astype(BF).reshape(group_len, own_heads, NOPE + VDIM)
    keys = keyval[:, :, :NOPE]
    values = keyval[:, :, NOPE:]
    scores = jnp.einsum("qhd,khd->hqk", q_nope, keys, preferred_element_type=F32)
    scores = scores + jnp.einsum("qhd,kd->hqk", q_rope, k_rope, preferred_element_type=F32)
    scores = jnp.where(allowed[None], scores * score_scale, NEGATIVE)
    top_score = jnp.max(scores, axis=-1, keepdims=True)
    log_total = top_score + jnp.log(jnp.sum(jnp.exp(scores - top_score), axis=-1, keepdims=True))
    soft_probs = jnp.exp(scores - log_total)
    prob_low = soft_probs.astype(BF)
    attended = (
        jnp.einsum("hqk,khd->qhd", prob_low, values, preferred_element_type=F32)
        .astype(BF)
        .reshape(group_len, own_heads * VDIM)
    )
    projected = sum_group(mm(attended, o_mine).astype(BF), 2)
    mixed = input_rows + projected

    normed_two, inverse_two = rms_forward(mixed, norm2_scale)
    hidden_two = normed_two.astype(BF)
    logits = mm(hidden_two, router)
    choice_hot = (
        expert_ids[:, :, None] == jnp.arange(all_experts, dtype=jnp.int32)[None, None, :]
    ).astype(F32)
    chosen = jnp.sum(choice_hot * logits[:, None, :], axis=-1)
    gate_probs = jax.nn.softmax(chosen, axis=-1)
    kept = kept_pairs(expert_ids, token_rank, choice_hot, capacity)
    gate_table = jnp.sum(choice_hot * (gate_probs * kept)[:, :, None], axis=1)

    own_width = expert_gate.shape[2]
    sizes = [own_width + -own_width % 128] * local_experts + [shared_width + -shared_width % 128]
    spans = tuple((sum(sizes[:i]), size) for i, size in enumerate(sizes))

    spare = -shared_width % 128
    shared_in = jnp.pad(both_shared.swapaxes(1, 2), ((0, 0), (0, spare), (0, 0)))
    shared_out = jnp.pad(shared_down, ((0, spare), (0, 0)))
    unit_expert = jnp.concatenate(
        [jnp.full((size,), expert_at * local_experts + i) for i, size in enumerate(sizes[:-1])]
        + [jnp.full((sizes[-1],), -1)]
    )
    column = jnp.arange(128)[:, None]
    spread = (
        (column == unit_expert) | ((column == unit_expert + all_experts) & (unit_expert >= 0))
    ).astype(BF)

    early = width // 2

    def ffn(rows, cots, table):
        cots_all = gather(cots[:, :early] + 0 * group_tokens[0, 0], BOTH)
        high = table.astype(BF)
        low = (table - high.astype(F32)).astype(BF)
        spare = jnp.zeros((table.shape[0], 128 - 2 * all_experts), BF)
        values, hid, in_d, gate_g, w_in, out_part = gather_hidden(
            jnp.concatenate([rows, high, low, spare, cots[:, early:]], axis=1),
            cots_all,
            spread,
            expert_gate.swapaxes(1, 2),
            expert_up.swapaxes(1, 2),
            expert_down,
            shared_in,
            shared_out,
            spans,
            local_experts,
            lines,
            3,
        )
        back_sum, out_part = sum_back(in_d, gate_g, w_in, out_part, 4)
        flat = lambda v: v.reshape(cots_all.shape[0], -1)
        work = [flat(values), cots_all, flat(in_d), flat(hid)]
        return scatter_sum(flat(out_part), BOTH), back_sum, work

    tail = spans[-1][0]
    inner = tail + spans[-1][1]
    expert_spans = tuple(span + (own_width,) for span in spans[:-1])
    shared_spans = (spans[-1] + (shared_width,),)
    if rounds == 1:
        out_sum, back_sum, work = ffn(hidden_two, cotangent, gate_table)
    else:

        def one_round(total, part):
            out_rows, back_rows, (values, cots, in_d, hid) = ffn(*part)
            rows = values[:, :width]
            cots = jnp.concatenate([cots, values[:, width + 128 :]], axis=1)
            grads = [mm_tn(in_d, rows), mm_tn(hid, cots)]
            return [t + g for t, g in zip(total, grads)], (out_rows, back_rows)

        in_rounds = lambda value: value.reshape((rounds, -1) + value.shape[1:])
        zeros = [jnp.zeros((2 * inner, width), F32), jnp.zeros((inner, width), F32)]
        (w_in_grad, w_down_grad), (out_sum, back_sum) = lax.scan(
            one_round, zeros, (in_rounds(hidden_two), in_rounds(cotangent), in_rounds(gate_table))
        )
        out_sum = out_sum.reshape((tok_rows,) + out_sum.shape[2:])
        back_sum = back_sum.reshape((tok_rows,) + back_sum.shape[2:])
        w_in_grad = w_in_grad.reshape(2, inner, width)
        cut = lambda grad: jnp.stack(
            [grad[spans[i][0] : spans[i][0] + own_width] for i in range(local_experts)]
        )
        expert_grads = [cut(w_in_grad[0]), cut(w_in_grad[1]), cut(w_down_grad)]
        shared_made = [v[tail : tail + shared_width] for v in (*w_in_grad, w_down_grad)]
        work = None
    out_sum, back_sum = out_sum.astype(F32), back_sum.astype(F32)
    output = (mixed + out_sum).astype(BF)

    upstream = cotangent.astype(F32)
    gate_grad = jnp.sum(
        choice_hot * back_sum[:, None, width : width + all_experts], axis=-1
    ) * kept
    chosen_grad = gate_probs * (gate_grad - jnp.sum(gate_probs * gate_grad, axis=-1, keepdims=True))
    logit_grad = jnp.sum(choice_hot * chosen_grad[:, :, None], axis=1).astype(BF)
    router_part = mm_tn(hidden_two, logit_grad)
    hidden_two_grad = back_sum[:, :width] + mm_nt(logit_grad, router)
    mixed_norm_grad, norm2_part = rms_backward(mixed, inverse_two, norm2_scale, hidden_two_grad)
    mixed_grad = upstream + mixed_norm_grad

    mixed_grad_group, *made = gather_group(mixed_grad.astype(BF), 5, work, shared_spans, lines)
    if work:
        shared_made = [v[0] for v in made]
    shared_grad = jnp.stack(shared_made[:2]).astype(BF)
    shared_grad = shared_grad.reshape(2, shared_width, device_count, -1).transpose(2, 0, 3, 1)
    shared_grad = lax.all_to_all(shared_grad, BOTH, split_axis=0, concat_axis=0)
    sdown_grad = shared_made[2]
    o_part = mm_tn(attended, mixed_grad_group)
    attended_grad = (
        mm_nt(mixed_grad_group, o_mine).astype(BF).reshape(group_len, own_heads, VDIM)
    )
    prob_grad = jnp.einsum("qhd,khd->hqk", attended_grad, values, preferred_element_type=F32)
    values_grad = jnp.einsum("hqk,qhd->khd", prob_low, attended_grad, preferred_element_type=F32)
    score_grad = (
        soft_probs * (prob_grad - jnp.sum(soft_probs * prob_grad, axis=-1, keepdims=True))
    ).astype(BF)
    q_nope_grad = (
        jnp.einsum("hqk,khd->qhd", score_grad, keys, preferred_element_type=F32) * score_scale
    )
    q_rope_grad = (
        jnp.einsum("hqk,kd->qhd", score_grad, k_rope, preferred_element_type=F32) * score_scale
    )
    keys_grad = (
        jnp.einsum("hqk,qhd->khd", score_grad, q_nope, preferred_element_type=F32) * score_scale
    )
    rope_grad = (
        jnp.einsum("hqk,qhd->kd", score_grad, q_rope, preferred_element_type=F32) * score_scale
    )
    keyval_grad = (
        jnp.concatenate([keys_grad, values_grad], axis=-1)
        .reshape(group_len, own_heads * (NOPE + VDIM))
        .astype(BF)
    )
    kvb_part = mm_tn(latent, keyval_grad)
    latent_raw_part, kv_gain_part = rms_backward(
        compressed[:, :KV_RANK], inverse_latent, latent_scale, mm_nt(keyval_grad, kvb_mine)
    )
    compressed_part = jnp.concatenate(
        [latent_raw_part, rotate(rope_grad, cosine_table, -sine_table)], axis=1
    ).astype(BF)
    query_grad = jnp.concatenate(
        [q_nope_grad, rotate(q_rope_grad, cosine_table[:, None, :], -sine_table[:, None, :])],
        axis=-1,
    )
    query_grad = query_grad.reshape(group_len, own_heads * (NOPE + ROPE)).astype(BF)
    q_part = mm_tn(hidden_one, query_grad)
    kva_part = mm_tn(hidden_one, compressed_part)
    hidden_one_part = mm_nt(query_grad, q_mine) + mm_nt(compressed_part, kva_all)
    norm1_part = jnp.sum(hidden_one_part * (group_rows * inverse_group), axis=0)

    def from_heads(parts):
        rows = parts.shape[2]
        heads = parts.reshape(2, 2, rows, own_heads, -1).transpose(2, 3, 1, 0, 4)
        return heads.reshape(rows, -1).astype(F32)

    line_shape = (lines, 2)
    small_parts = pack(
        [v.reshape(device_count, -1) for v in (norm1_part, norm2_part, kv_gain_part, router_part)]
    )
    parts = [
        kvb_part.astype(BF).reshape(line_shape + (2, 2, kvb_weight.shape[0], -1)),
        kva_part.astype(BF).reshape(line_shape + (2, 2, width // device_count, latent_width)),
        q_part.astype(BF).reshape(line_shape + (2, 2, q_weight.shape[0], q_mine.shape[1])),
        small_parts.reshape(line_shape + (2, 2) + small_parts.shape[1:]),
    ]
    o_part = o_part.astype(BF).reshape(own_heads, VDIM, width)
    if o_pairs:
        o_sum = o_part.reshape(own_heads, 2, o_rows, width)
    else:
        o_sum = None
        o_wide = jnp.zeros((own_heads, 2, 2, VDIM, width), BF).at[:, core_at, x_at].set(o_part)
        o_grad = scatter_sum(o_wide.reshape(HEADS * VDIM, width), BOTH).astype(F32)
    summed = sum_grads(
        parts,
        1,
        hidden_one_part.astype(BF).reshape(2, 2, tok_rows, width),
        o_sum,
        lines,
        9,
        work,
        expert_spans,
    )
    _, inverse_one = rms_forward(input_rows, norm1_scale)
    input_norm_grad, _ = rms_backward(input_rows, inverse_one, norm1_scale, summed[4])
    tokens_grad = mixed_grad + input_norm_grad
    if work:
        expert_grads = summed[-3:]
    norm1_grad, norm2_grad, kv_gain_grad, router_grad = unpack(jnp.sum(summed[3], axis=(0, 1)))
    router_grad = router_grad.reshape(router_weight.shape)
    if o_pairs:
        q_grad, kvb_grad, kva_grad, o_grad, sgate_grad, sup_grad = lay_out(
            summed[2], summed[0], summed[1], summed[5], shared_grad, own_heads
        )
    else:
        kvb_grad = from_heads(summed[0])
        kva_grad = summed[1].astype(F32)
        q_grad = from_heads(summed[2])
        sgate_grad, sup_grad = (
            shared_grad.astype(F32)
            .transpose(1, 2, 0, 3)
            .reshape(2, width // device_count, device_count * shared_width)
        )
    return (
        output,
        tokens_grad,
        norm1_grad,
        q_grad,
        kva_grad,
        kv_gain_grad,
        kvb_grad,
        o_grad,
        norm2_grad,
        router_grad,
        sgate_grad,
        sup_grad,
        sdown_grad,
        expert_grads[0].swapaxes(1, 2),
        expert_grads[1].swapaxes(1, 2),
        expert_grads[2],
    )


def solution(mesh):
    rows = P(BOTH, None)
    flat = P(BOTH)
    columns = P("expert", None, "shard")
    depth = P("expert", "shard", None)
    return jax.shard_map(
        on_device,
        mesh=mesh,
        in_specs=(
            rows,
            rows,
            flat,
            rows,
            rows,
            flat,
            rows,
            rows,
            flat,
            rows,
            rows,
            rows,
            rows,
            columns,
            columns,
            depth,
            rows,
            flat,
            P("expert"),
        ),
        out_specs=(
            rows,
            rows,
            flat,
            rows,
            rows,
            flat,
            rows,
            rows,
            flat,
            rows,
            rows,
            rows,
            rows,
            columns,
            columns,
            depth,
        ),
        check_vma=False,
    )
```
